256 devices in a mesh: beam: 8 (over y, core), chan: 32 (over z, x).
Axes of the slice: x: 4, y: 4, z: 8, core: 2. Of those that a mesh axis runs over, the one named last changes fastest.
Arguments:
- observed: float32 [2, 1024, 4096], P(None, 'chan', 'beam'), parts along dimension 2, may hold values from -40 to 40
- window: float32 [4, 1024], replicated, may hold values from -1.5 to 1.5
- decays: float32 [1024, 4096], P('chan', 'beam'), parts along dimension 1, may hold values from 0.3 to 1
Outputs:
- solution: float32 [2, 4096, 1024], P(None, ('beam', 'chan')), parts along dimension 1
- residual: float32 [2, 4096, 1024], P(None, ('beam', 'chan')), parts along dimension 1
The draws below stay inside these ranges and needn't reach their ends.
There are 8 independent parts, one for each index of `beam`. The reference program is written for one: setup_inputs(seed, part) draws one part's arguments, and reference() takes and returns one part's arrays. A program takes and returns all parts, laid end to end along the dimension named above; an argument that names none is the same for every part. Nothing has to cross between parts.
All inputs are finite; a program needn't handle non-finite values.
Results may differ from the reference program's by a relative error of at most 0.0003.
Values sent between devices are 32-bit elements; how exact they have to be, the bound alone decides.
A program may use at most 64 MiB of HBM per device.

```python
import math
import jax
import jax.numpy as jnp
from jax import lax

CHANNELS = 1024
TAPS = 4
ITERS = 2
FRAMES = 512


def draw_observed(key, part):
    key = jax.random.fold_in(key, 5)
    first, second = jax.random.split(key)
    place = jnp.arange(FRAMES, dtype=jnp.float32) / FRAMES
    base = jax.random.truncated_normal(first, -4.0, 4.0, (2, CHANNELS, FRAMES), jnp.float32)
    spread = jnp.exp(jax.random.uniform(second, (CHANNELS,), jnp.float32, math.log(0.3), math.log(3.0)))
    ramp = jnp.exp(place * math.log(3.0))
    return base * spread[None, :, None] * ramp[None, None, :]


def draw_window(key, part):
    key = jax.random.fold_in(key, 11)
    length = TAPS * CHANNELS
    steps = jnp.arange(length, dtype=jnp.float32) + 0.5
    centre = (steps - length / 2.0) / CHANNELS
    proto = jnp.sinc(centre) * (0.54 - 0.46 * jnp.cos(2.0 * math.pi * steps / length))
    rough = jax.random.uniform(key, (length,), jnp.float32, 0.7, 1.3)
    return (proto * rough).reshape(TAPS, CHANNELS)


def draw_decays(key, part):
    key = jax.random.fold_in(key, 7)
    keys = jax.random.split(key, 5)
    share = 0.5
    quick = jax.random.uniform(keys[0], (CHANNELS,), jnp.float32) < share
    quick_rate = jnp.exp(-1.0 / jax.random.uniform(keys[1], (CHANNELS,), jnp.float32, 30.0, 50.0))
    slow_rate = jnp.exp(-jax.random.uniform(keys[2], (CHANNELS,), jnp.float32, 0.5, 2.0) / FRAMES)
    rate = jnp.where(quick, quick_rate, slow_rate)
    spots = jax.random.randint(keys[3], (4,), 0, FRAMES)
    struck = jnp.any(jnp.arange(FRAMES)[None, :] == spots[:, None], axis=0)
    loss = jax.random.uniform(keys[4], (CHANNELS,), jnp.float32, 0.5, 0.8)
    return jnp.where(struck[None, :], (rate * loss)[:, None], rate[:, None] * jnp.ones((1, FRAMES), jnp.float32))


def setup_inputs(seed: int = 0, part: int = 0) -> dict:
    streams_of = jax.random.split(jax.random.key(seed), 4)
    own_keys = jax.random.split(jax.random.fold_in(streams_of[3], part), 4)
    observed = draw_observed(jax.random.fold_in(jax.random.fold_in(streams_of[3], part), 71), part)
    window = draw_window(jax.random.fold_in(streams_of[3], 71), part)
    decays = draw_decays(jax.random.fold_in(jax.random.fold_in(streams_of[3], part), 71), part)
    return dict(observed=observed, window=window, decays=decays)


def running(decay, data):

    def combine(left, right):
        return (left[0] * right[0], right[0] * left[1] + right[1])
    return lax.associative_scan(combine, (decay, data), axis=2)

def whiten(data, decay):
    after = jnp.concatenate([decay[:, :, 1:], jnp.zeros_like(decay[:, :, :1])], axis=2)
    gain = 1.0 - decay
    smooth = running(decay, gain * data)[1]
    first = data + 2.0 * smooth
    back = jnp.flip(running(jnp.flip(after, 2), jnp.flip(first, 2))[1], 2)
    return first + 2.0 * gain * back

def analysis(field, window):
    lag = TAPS - 1
    wave = field[0] + 1j * field[1]
    padded = jnp.pad(wave, ((lag, 0), (0, 0)))
    mixed = window[0][None, :] * wave
    for tap in range(1, TAPS):
        mixed = mixed + window[tap][None, :] * padded[lag - tap:lag - tap + FRAMES]
    spec = jnp.fft.fft(mixed, axis=1) / jnp.sqrt(float(CHANNELS))
    return jnp.stack([jnp.real(spec).T, jnp.imag(spec).T])

def synthesis(spec, window):
    lag = TAPS - 1
    wave = (spec[0] + 1j * spec[1]).T
    unmixed = jnp.fft.ifft(wave, axis=1) * jnp.sqrt(float(CHANNELS))
    padded = jnp.pad(unmixed, ((0, lag), (0, 0)))
    result = window[0][None, :] * unmixed
    for tap in range(1, TAPS):
        result = result + window[tap][None, :] * padded[tap:tap + FRAMES]
    return jnp.stack([jnp.real(result), jnp.imag(result)]).astype(spec.dtype)

def reference(observed, window, decays):
    decay = decays[None]
    rhs = synthesis(whiten(observed, decay), window)
    solution = jnp.zeros_like(rhs)
    residual, direction = (rhs, rhs)
    norm_now = jnp.sum(residual * residual)
    for step in range(ITERS):
        image = synthesis(whiten(analysis(direction, window), decay), window) + 0.5 * direction
        alpha = norm_now / jnp.sum(direction * image)
        solution = solution + alpha * direction
        residual = residual - alpha * image
        norm_next = jnp.sum(residual * residual)
        direction = residual + norm_next / norm_now * direction
        norm_now = norm_next
    return (solution, residual)
```

```python
import functools
import math

import jax
import jax.numpy as jnp
import ml_dtypes
import numpy as np
from jax import lax
from jax.experimental import pallas as pl
from jax.experimental.pallas import tpu as pltpu
from jax.sharding import PartitionSpec as P

MESH = pl.DeviceIdType.MESH
F32 = jnp.float32
BF16 = jnp.bfloat16
GROUP = 32
NX = 4
NZ = 8
RIDGE = 0.5
FLIP = (0, 4, 2, 6, 1, 5, 3, 7)


def tables():
    lane = np.arange(128)
    k2 = 4 * (lane % 32) + lane // 32
    n2 = np.arange(128)
    angle = 2.0 * np.pi * ((k2[:, None] * n2[None, :]) % 128) / 128.0
    cos, sin = np.cos(angle) / 32.0, np.sin(angle) / 32.0
    inverse = np.block([[cos, sin], [-sin, cos]])

    def split(matrix):
        high = matrix.astype(ml_dtypes.bfloat16)
        low = (matrix - high.astype(np.float64)).astype(ml_dtypes.bfloat16)
        return np.concatenate([high, high, low], axis=0)

    mats = np.stack([split(inverse), split(inverse.T)])
    turn = 2.0 * np.pi * np.array(FLIP)[:, None] * n2[None, :] / 1024.0
    eighth = 2.0 * np.pi * np.maximum(np.arange(8) - 4, 0) / 8.0
    eighth = np.broadcast_to(eighth[:, None], (8, 128))
    tabs = np.stack([np.cos(turn), np.sin(turn), np.cos(eighth), np.sin(eighth)])
    return mats, tabs.astype(np.float32)


def kernel(
    obs_hbm, win_hbm, dec_hbm, mats_hbm, tabs_hbm, sol_ref, res_ref,
    obs_v, win_v, dec_v, mats_v, tabs_v, stage, got,
    spec, dec, e0_s, carry_x, carry_z, xb, zb, cx, cz, sb,
    in_sem, own_sem, a_send, a_recv, xc_send, xc_recv, zc_send, zc_recv,
    x_send, x_recv, z_send, z_recv, s_send, s_recv,
):
    me = lax.axis_index("chan")
    mz = me // NX
    mx = lax.rem(me, NX)
    inputs = []
    for t, (src, dst) in enumerate(
        ((obs_hbm, obs_v), (dec_hbm, dec_v), (win_hbm, win_v), (mats_hbm, mats_v), (tabs_hbm, tabs_v))
    ):
        copy = pltpu.make_async_copy(src, dst, in_sem.at[t])
        copy.start()
        inputs.append(copy)
    barrier = pltpu.get_barrier_semaphore()
    for t in range(1, GROUP):
        pl.semaphore_signal(
            barrier, inc=1, device_id={"chan": lax.rem(me + t, GROUP)}, device_id_type=MESH
        )
    inputs[0].wait()
    inputs[1].wait()

    frames = 512
    lane = lax.broadcasted_iota(jnp.int32, (32, frames), 1)
    row = lax.rem(lax.broadcasted_iota(jnp.int32, (32, frames), 0), 8)

    def shift(value, steps):
        return pltpu.roll(value, steps % frames, axis=value.ndim - 1)

    a = dec_v[...]
    gain = 1.0 - a
    data = [obs_v[0], obs_v[1]]
    prod = jnp.where(lane == 0, 0.0, a)
    run = [gain * d for d in data]
    step = 1
    while step < frames:
        run = [r + prod * shift(r, step) for r in run]
        prod = prod * shift(prod, step)
        step *= 2
    first = [d + 2.0 * r for d, r in zip(data, run)]
    prod = jnp.where(lane == frames - 1, 0.0, shift(a, -1))
    run = first
    step = 1
    while step < frames:
        run = [r + prod * shift(r, -step) for r in run]
        prod = prod * shift(prod, -step)
        step *= 2
    white = [f + 2.0 * gain * r for f, r in zip(first, run)]

    up = (row == 1) | (row == 3)
    down = (row == 4) | (row == 6)

    def flipped(value):
        return jnp.where(
            up,
            pltpu.roll(value, 29, axis=0),
            jnp.where(down, pltpu.roll(value, 3, axis=0), value),
        )

    def moved(value, offset):
        moved_value = shift(value, -offset)
        inside = (lane + offset >= 0) & (lane + offset < frames)
        return jnp.where(inside, moved_value, 0.0)

    white = [flipped(w) for w in white]
    af = flipped(a)
    packed = jnp.concatenate(
        [moved(white[0], -6), moved(white[1], -6), moved(white[0], 10), moved(white[1], 10)], axis=0
    )
    stage[:, 0:16, :] = packed.T.reshape(GROUP, 16, 128)
    packed = jnp.concatenate([moved(af, 8 * t - 6) for t in range(4)], axis=0)
    stage[:, 16:24, :] = packed.T.reshape(GROUP, 16, 128)[:, :8]

    pl.semaphore_wait(barrier, GROUP - 1)

    spreads = []
    for t in range(1, GROUP):
        to = lax.rem(me + t, GROUP)
        copy = pltpu.make_async_remote_copy(
            src_ref=stage.at[to], dst_ref=got.at[:, me, :], send_sem=a_send.at[t], recv_sem=a_recv.at[t],
            device_id={"chan": to}, device_id_type=MESH,
        )
        copy.start()
        spreads.append(copy)
    own = pltpu.make_async_copy(stage.at[me], got.at[:, me, :], own_sem)
    own.start()
    for copy in inputs[2:]:
        copy.wait()

    win = [
        jnp.concatenate([win_v[p : p + 1, n * 128 : (n + 1) * 128] for n in range(8)], axis=0)
        for p in range(4)
    ]

    def butterfly(value, distance):
        index = lax.broadcasted_iota(jnp.int32, value.shape, 1)
        high = (index & distance) != 0
        if distance == 4:
            other = pltpu.roll(value, 4, axis=1)
        else:
            other = jnp.where(
                high, pltpu.roll(value, distance, axis=1), pltpu.roll(value, 8 - distance, axis=1)
            )
        return jnp.where(high, other - value, other + value)

    def quarter(re, im, sign):
        index = lax.broadcasted_iota(jnp.int32, re.shape, 1)
        turned = (index & 3) == 3
        return jnp.where(turned, -sign * im, re), jnp.where(turned, sign * re, im)

    def times(re, im, c, s):
        return re * c - im * s, re * s + im * c

    def product(re, im, which):
        count = re.shape[0]
        x = jnp.concatenate([re.reshape(count * 8, 128), im.reshape(count * 8, 128)], axis=1)
        high = x.astype(BF16)
        low = (x - high.astype(F32)).astype(BF16)
        y = jnp.dot(
            jnp.concatenate([high, low, high], axis=1), mats_v[which], preferred_element_type=F32
        )
        return y[:, :128].reshape(count, 8, 128), y[:, 128:].reshape(count, 8, 128)

    def to_wave(re, im):
        re, im = product(re, im, 0)
        re, im = times(re, im, tabs_v[0], tabs_v[1])
        re, im = butterfly(re, 1), butterfly(im, 1)
        re, im = quarter(re, im, 1.0)
        re, im = butterfly(re, 2), butterfly(im, 2)
        re, im = times(re, im, tabs_v[2], tabs_v[3])
        return butterfly(re, 4), butterfly(im, 4)

    def to_spec(re, im):
        re, im = butterfly(re, 4), butterfly(im, 4)
        re, im = times(re, im, tabs_v[2], -tabs_v[3])
        re, im = butterfly(re, 2), butterfly(im, 2)
        re, im = quarter(re, im, -1.0)
        re, im = butterfly(re, 1), butterfly(im, 1)
        re, im = times(re, im, tabs_v[0], -tabs_v[1])
        return product(re, im, 1)

    def gather_taps(u, count):
        out = win[0] * u[0:count]
        for p in range(1, 4):
            out = out + win[p] * u[p : p + count]
        return out

    def spread_taps(v, count):
        out = win[0] * v[3 : 3 + count]
        for p in range(1, 4):
            out = out + win[p] * v[3 - p : 3 - p + count]
        return out

    def keep(value, start, before, after):
        index = lax.broadcasted_iota(jnp.int32, value.shape, 0) + start
        out = value
        if before:
            out = jnp.where((index < 6) & (me == 0), 0.0, out)
        if after:
            out = jnp.where((index >= 22) & (me == GROUP - 1), 0.0, out)
        return out

    own.wait()
    for copy in spreads:
        copy.wait_recv()

    lane8 = lax.broadcasted_iota(jnp.int32, (8, 128), 1)
    low64 = lane8 < 64
    low32 = (lane8 & 32) == 0

    def exchange(v):
        y = [None] * 4
        for i in range(2):
            y[i] = jnp.where(low64, v[i], pltpu.roll(v[i + 2], 64, axis=1))
            y[i + 2] = jnp.where(low64, pltpu.roll(v[i], 64, axis=1), v[i + 2])
        z = [None] * 4
        for i in (0, 2):
            z[i] = jnp.where(low32, y[i], pltpu.roll(y[i + 1], 32, axis=1))
            z[i + 1] = jnp.where(low32, pltpu.roll(y[i], 96, axis=1), y[i + 1])
        return z

    for q in range(2):
        turned = got[16 + 4 * q : 20 + 4 * q].reshape(128, 128).T
        for part in range(4):
            base = part * 32
            out = exchange([turned[base + 8 * i : base + 8 * i + 8] for i in range(4)])
            for r in range(4):
                dec[8 * part + 4 * q + r] = out[r]

    def coefficients(start, count):
        stop = start + count
        p = dec[start]
        ps = [p]
        for g in range(start + 1, stop):
            p = dec[g] * p
            ps.append(p)
        b = dec[stop]
        h = ps[-1]
        bs, hs = [b], [h]
        for g in range(stop - 2, start - 1, -1):
            b = dec[g + 1] * b
            h = ps[g - start] + dec[g + 1] * h
            bs.append(b)
            hs.append(h)
        bs.reverse()
        hs.reverse()
        two_p = jnp.stack([2.0 * v for v in ps])
        gains = [2.0 * (1.0 - dec[g]) for g in range(start, stop)]
        left = jnp.stack([2.0 * x + 2.0 * y * z for x, y, z in zip(ps, gains, hs)])
        right = jnp.stack([y * z for y, z in zip(gains, bs)])
        return two_p, left, right, ps[15], bs[count - 16], 2.0 * hs[count - 16]

    two_p0, left0, right0, a0, b0, k0 = coefficients(3, 25)
    two_p1, left1, right1, a1, b1, k1 = coefficients(6, 19)
    for n, value in enumerate((a0, b0, k0, a1, b1, k1)):
        cx[mx, 8 * n : 8 * n + 8] = value

    def x_copies(src, dst, send, recv):
        out = []
        for t in range(1, NX):
            to = mz * NX + lax.rem(mx + t, NX)
            out.append(pltpu.make_async_remote_copy(
                src_ref=src, dst_ref=dst, send_sem=send.at[t], recv_sem=recv.at[t],
                device_id={"chan": to}, device_id_type=MESH,
            ))
        for copy in out:
            copy.start()
        return out

    def z_copies(src, dst, send, recv):
        out = []
        for t in range(1, NZ):
            to = lax.rem(mz + t, NZ) * NX + mx
            out.append(pltpu.make_async_remote_copy(
                src_ref=src, dst_ref=dst, send_sem=send.at[t], recv_sem=recv.at[t],
                device_id={"chan": to}, device_id_type=MESH,
            ))
        for copy in out:
            copy.start()
        return out

    sent = list(spreads)
    x_coefs = x_copies(cx.at[mx], cx.at[mx], xc_send, xc_recv)
    sent += x_coefs

    for q in range(4):
        turned = got[4 * q : 4 * q + 4].reshape(128, 128).T
        for half in range(2):
            for c in range(2):
                base = half * 64 + c * 32
                out = exchange([turned[base + 8 * i : base + 8 * i + 8] for i in range(4)])
                for r in range(4):
                    spec[c, 16 * half + 4 * q + r] = out[r]

    def local_whiten(re, im, start, count):
        stop = start + count
        x = [jnp.stack([re[g], im[g]]) for g in range(count)]
        s = (1.0 - dec[start]) * x[0]
        e = [x[0] + 2.0 * s]
        leaving_right = None
        for g in range(1, count):
            a = dec[start + g]
            s = a * s + (1.0 - a) * x[g]
            e.append(x[g] + 2.0 * s)
            if g == 15:
                leaving_right = s
        back = e[-1]
        w = [None] * count
        leaving_left = None
        w[-1] = e[-1] + 2.0 * (1.0 - dec[stop - 1]) * back
        for g in range(count - 2, -1, -1):
            back = e[g] + dec[start + g + 1] * back
            w[g] = e[g] + 2.0 * (1.0 - dec[start + g]) * back
            if g == count - 16:
                leaving_left = back
        return e, w, leaving_right, leaving_left

    def chain(carry, back, left, right, a, b, k):
        count = len(left)
        cs = [carry]
        for n in range(count):
            cs.append(a[n] * cs[n] + left[n])
        ds = [None] * count
        d = back
        for n in range(count - 1, -1, -1):
            ds[n] = d
            d = b[n] * d + (right[n] + k[n] * cs[n])
        return cs, ds, d

    def pair(ref, base):
        return jnp.stack([ref[base : base + 8], ref[base + 8 : base + 16]])

    zero = jnp.zeros((2, 8, 128), F32)

    def x_side(turn):
        c = [[cx[n, 24 * turn + 8 * m : 24 * turn + 8 * m + 8] for n in range(NX)] for m in range(3)]
        return c

    def group_coefficients(turn):
        a, b, k = x_side(turn)
        ga, gb, gk = a[0], b[0], k[0]
        for n in range(1, NX):
            gk = gb * k[n] * ga + gk
            gb = gb * b[n]
            ga = a[n] * ga
        cz[turn, mz, 0:8] = ga
        cz[turn, mz, 8:16] = gb
        cz[turn, mz, 16:24] = gk

    def carries(turn, right_going, left_going, rows):
        nrow = 32 + len(rows)
        xv = xb.at[turn, mx]
        xv[0:8] = right_going[0]
        xv[8:16] = right_going[1]
        xv[16:24] = left_going[0]
        xv[24:32] = left_going[1]
        for n, value in enumerate(rows):
            xv[32 + n : 33 + n] = value
        part = xb.at[turn, mx, pl.ds(0, nrow)]
        copies = x_copies(part, part, x_send.at[turn], x_recv.at[turn])
        sent.extend(copies)
        if turn == 0:
            for copy in x_coefs:
                copy.wait_recv()
            for which in range(2):
                group_coefficients(which)
            sent.extend(z_coefs_start(0))
        for copy in copies:
            copy.wait_recv()
        a, b, k = x_side(turn)
        left = [pair(xb.at[turn, n], 0) for n in range(NX)]
        right = [pair(xb.at[turn, n], 16) for n in range(NX)]
        cs, ds, out = chain(zero, zero, left, right, a, b, k)
        zv = zb.at[turn, mz]
        zv[0:8] = cs[NX][0]
        zv[8:16] = cs[NX][1]
        zv[16:24] = out[0]
        zv[24:32] = out[1]
        for n in range(len(rows)):
            total = xb[turn, 0, 32 + n : 33 + n]
            for m in range(1, NX):
                total = total + xb[turn, m, 32 + n : 33 + n]
            zv[32 + n : 33 + n] = total
        part = zb.at[turn, mz, pl.ds(0, nrow)]
        copies = z_copies(part, part, z_send.at[turn], z_recv.at[turn])
        sent.extend(copies)
        if turn == 0:
            sent.extend(z_coefs_start(1))
        for copy in z_coefs[turn]:
            copy.wait_recv()
        for copy in copies:
            copy.wait_recv()
        za, zbk, zk = [[cz[turn, n, 8 * m : 8 * m + 8] for n in range(NZ)] for m in range(3)]
        zleft = [pair(zb.at[turn, n], 0) for n in range(NZ)]
        zright = [pair(zb.at[turn, n], 16) for n in range(NZ)]
        zcs, zds, _ = chain(zero, zero, zleft, zright, za, zbk, zk)
        for n in range(NZ):
            carry_z[0, n] = zcs[n]
            carry_z[1, n] = zds[n]
        cs, ds, _ = chain(carry_z[0, mz], carry_z[1, mz], left, right, a, b, k)
        for n in range(NX):
            carry_x[0, n] = cs[n]
            carry_x[1, n] = ds[n]
        sums = []
        for n in range(len(rows)):
            total = zb[turn, 0, 32 + n : 33 + n]
            for m in range(1, NZ):
                total = total + zb[turn, m, 32 + n : 33 + n]
            sums.append(jnp.sum(total, axis=1, keepdims=True))
        return carry_x[0, mx], carry_x[1, mx], sums

    z_coefs = [None, None]

    def z_coefs_start(turn):
        z_coefs[turn] = z_copies(
            cz.at[turn, mz], cz.at[turn, mz], zc_send.at[turn], zc_recv.at[turn]
        )
        return z_coefs[turn]

    def corrected(w, left, right, c, d):
        re = jnp.stack([v[0] for v in w]) + left * c[0] + right * d[0]
        im = jnp.stack([v[1] for v in w]) + left * c[1] + right * d[1]
        return re, im

    def padded(re, im):
        fill = jnp.zeros((1, 8, 128), F32)
        return jnp.concatenate([re, fill]), jnp.concatenate([im, fill])

    def folded(value):
        return jnp.sum(jnp.sum(value, axis=0), axis=0, keepdims=True)

    u = to_wave(spec[0], spec[1])
    r0 = [keep(gather_taps(v, 29), 0, True, False) for v in u]
    x = to_spec(*[spread_taps(v, 26) for v in r0])
    x = [keep(v, 3, False, True) for v in x]
    e0, w0, going_right, going_left = local_whiten(x[0], x[1], 3, 25)
    c, d, _ = carries(0, going_right, going_left, [])
    for n in range(2):
        e0_s[n] = jnp.stack([v[n] for v in e0[3:19]]) + two_p0[3:19] * c[n]
    w = corrected(w0, left0, right0, c, d)

    u = to_wave(*padded(*w))
    q1 = [
        keep(gather_taps(v, 22) + RIDGE * r[3:25], 3, True, False) for v, r in zip(u, r0)
    ]
    mine_r0 = [v[6:22] for v in r0]
    mine_q1 = [v[3:19] for v in q1]
    rr_part = folded(mine_r0[0] * mine_r0[0] + mine_r0[1] * mine_r0[1])
    rq_part = folded(mine_r0[0] * mine_q1[0] + mine_r0[1] * mine_q1[1])
    x = to_spec(*padded(*[spread_taps(v, 19) for v in q1]))
    x = [keep(v, 6, False, True) for v in x]
    e1, w1, going_right, going_left = local_whiten(x[0], x[1], 6, 19)
    c, d, (rr, rq) = carries(1, going_right, going_left, [rr_part, rq_part])
    alpha = rr / rq

    r1 = [r - alpha * q for r, q in zip(mine_r0, mine_q1)]
    energy = []
    for n in range(2):
        e = e0_s[n] - alpha * (jnp.stack([v[n] for v in e1[:16]]) + two_p1[:16] * c[n])
        energy.append(e * e)
    new_part = folded(r1[0] * r1[0] + r1[1] * r1[1])
    energy_part = folded(energy[0] + energy[1])
    new_part = new_part + pltpu.roll(new_part, 64, axis=1)
    energy_part = energy_part + pltpu.roll(energy_part, 64, axis=1)
    low = lax.broadcasted_iota(jnp.int32, (1, 128), 1) < 64
    sb[me] = jnp.where(low, new_part, energy_part)
    lasts = []
    for t in range(1, GROUP):
        to = lax.rem(me + t, GROUP)
        copy = pltpu.make_async_remote_copy(
            src_ref=sb.at[me], dst_ref=sb.at[me], send_sem=s_send.at[t], recv_sem=s_recv.at[t],
            device_id={"chan": to}, device_id_type=MESH,
        )
        copy.start()
        lasts.append(copy)
    sent += lasts

    w = corrected(w1, left1, right1, c, d)
    u = to_wave(*padded(*w))
    q2 = [gather_taps(v, 16) + RIDGE * q for v, q in zip(u, mine_q1)]
    n1 = [q - alpha * p for q, p in zip(mine_q1, q2)]

    for copy in lasts:
        copy.wait_recv()
    total = sb[0]
    for n in range(1, GROUP):
        total = total + sb[n]
    new = jnp.sum(jnp.where(low, total, 0.0), axis=1, keepdims=True)
    energy = jnp.sum(jnp.where(low, 0.0, total), axis=1, keepdims=True)
    beta = new / rr
    alpha_next = new / (energy + RIDGE * new - beta * new / alpha)
    for n in range(2):
        direction = r1[n] + beta * mine_r0[n]
        image = n1[n] + beta * mine_q1[n]
        sol = alpha * mine_r0[n] + alpha_next * direction
        res = r1[n] - alpha_next * image
        sol_ref[n] = sol.reshape(16, 1024)
        res_ref[n] = res.reshape(16, 1024)
    for copy in sent:
        copy.wait_send()


def body(observed, window, decays):
    mats, tabs = tables()
    any_space = pl.BlockSpec(memory_space=pl.ANY)
    vmem = pl.BlockSpec(memory_space=pltpu.VMEM)
    dma = pltpu.SemaphoreType.DMA
    out = jax.ShapeDtypeStruct((2, 16, 1024), F32)
    return pl.pallas_call(
        kernel,
        out_shape=(out, out),
        in_specs=[any_space] * 5,
        out_specs=(vmem, vmem),
        scratch_shapes=[
            pltpu.VMEM((2, 32, 512), F32),
            pltpu.VMEM((4, 1024), F32),
            pltpu.VMEM((32, 512), F32),
            pltpu.VMEM((2, 768, 256), BF16),
            pltpu.VMEM((4, 8, 128), F32),
            pltpu.VMEM((GROUP, 24, 128), F32),
            pltpu.VMEM((24, GROUP, 128), F32),
            pltpu.VMEM((2, 32, 8, 128), F32),
            pltpu.VMEM((32, 8, 128), F32),
            pltpu.VMEM((2, 16, 8, 128), F32),
            pltpu.VMEM((2, NX, 2, 8, 128), F32),
            pltpu.VMEM((2, NZ, 2, 8, 128), F32),
            pltpu.VMEM((2, NX, 40, 128), F32),
            pltpu.VMEM((2, NZ, 40, 128), F32),
            pltpu.VMEM((NX, 48, 128), F32),
            pltpu.VMEM((2, NZ, 24, 128), F32),
            pltpu.VMEM((GROUP, 1, 128), F32),
            dma((5,)),
            dma,
            dma((GROUP,)), dma((GROUP,)),
            dma((NX,)), dma((NX,)),
            dma((2, NZ)), dma((2, NZ)),
            dma((2, NX)), dma((2, NX)),
            dma((2, NZ)), dma((2, NZ)),
            dma((GROUP,)), dma((GROUP,)),
        ],
        name="invert",
        compiler_params=pltpu.CompilerParams(
            collective_id=0, has_side_effects=True, vmem_limit_bytes=48 * 1024 * 1024
        ),
    )(observed, window, decays, jnp.asarray(mats), jnp.asarray(tabs))


def solution(mesh):
    return jax.shard_map(
        body,
        mesh=mesh,
        in_specs=(P(None, "chan", "beam"), P(), P("chan", "beam")),
        out_specs=(P(None, ("beam", "chan"), None), P(None, ("beam", "chan"), None)),
        check_vma=False,
    )
```

```python
import functools
import math

import jax
import jax.numpy as jnp
import numpy as np
from jax import lax
from jax.experimental import pallas as pl
from jax.experimental.pallas import tpu as pltpu
from jax.sharding import PartitionSpec as P

MESH = pl.DeviceIdType.MESH
F32 = jnp.float32
BF16 = jnp.bfloat16
GROUP = 32
NX = 4
NZ = 8
RIDGE = 0.5
FLIP = (0, 4, 2, 6, 1, 5, 3, 7)


def tables():
    lane = np.arange(128)
    k2 = 4 * (lane % 32) + lane // 32
    n2 = np.arange(128)
    angle = 2.0 * np.pi * ((k2[:, None] * n2[None, :]) % 128) / 128.0
    cos, sin = np.cos(angle) / 32.0, np.sin(angle) / 32.0
    inverse = np.block([[cos, sin], [-sin, cos]])

    mats = np.stack([inverse, inverse.T]).astype(np.float32)
    turn = 2.0 * np.pi * np.array(FLIP)[:, None] * n2[None, :] / 1024.0
    eighth = 2.0 * np.pi * np.maximum(np.arange(8) - 4, 0) / 8.0
    eighth = np.broadcast_to(eighth[:, None], (8, 128))
    tabs = np.stack([np.cos(turn), np.sin(turn), np.cos(eighth), np.sin(eighth)])
    return mats, tabs.astype(np.float32)


def kernel(
    obs_hbm, win_hbm, dec_hbm, mats_hbm, tabs_hbm, sol_ref, res_ref,
    obs_v, win_v, dec_v, full_v, tabs_v, mats_v, stage_o, stage_d, got_o, got_d,
    spec, dec, carry_x, carry_z, xb, zb, cx, cz,
    in_sem, own_sem, o_send, o_recv, d_send, d_recv, xc_send, xc_recv,
    zc_send, zc_recv, x_send, x_recv, z_send, z_recv,
):
    me = lax.axis_index("chan")
    mz = me // NX
    mx = lax.rem(me, NX)
    barrier = pltpu.get_barrier_semaphore()
    for t in range(1, GROUP):
        pl.semaphore_signal(
            barrier, inc=1, device_id={"chan": lax.rem(me + t, GROUP)}, device_id_type=MESH
        )
    inputs = []
    for t, (src, dst) in enumerate(
        ((obs_hbm, obs_v), (dec_hbm, dec_v), (win_hbm, win_v), (mats_hbm, full_v), (tabs_hbm, tabs_v))
    ):
        copy = pltpu.make_async_copy(src, dst, in_sem.at[t])
        copy.start()
        inputs.append(copy)
    inputs[0].wait()
    inputs[1].wait()

    frames = 512
    lane = lax.broadcasted_iota(jnp.int32, (32, frames), 1)
    row = lax.rem(lax.broadcasted_iota(jnp.int32, (32, frames), 0), 8)

    def shift(value, steps):
        return pltpu.roll(value, steps % frames, axis=value.ndim - 1)

    a = dec_v[...]
    gain = 1.0 - a
    data = [obs_v[0], obs_v[1]]
    prod = jnp.where(lane == 0, 0.0, a)
    run = [gain * d for d in data]
    step = 1
    while step < frames:
        run = [r + prod * shift(r, step) for r in run]
        prod = prod * shift(prod, step)
        step *= 2
    first = [d + 2.0 * r for d, r in zip(data, run)]
    prod = jnp.where(lane == frames - 1, 0.0, shift(a, -1))
    run = first
    step = 1
    while step < frames:
        run = [r + prod * shift(r, -step) for r in run]
        prod = prod * shift(prod, -step)
        step *= 2
    white = [f + 2.0 * gain * r for f, r in zip(first, run)]

    up = (row == 1) | (row == 3)
    down = (row == 4) | (row == 6)

    def flipped(value):
        return jnp.where(
            up,
            pltpu.roll(value, 29, axis=0),
            jnp.where(down, pltpu.roll(value, 3, axis=0), value),
        )

    def moved(value, offset):
        moved_value = shift(value, -offset)
        inside = (lane + offset >= 0) & (lane + offset < frames)
        return jnp.where(inside, moved_value, 0.0)

    white = [flipped(w) for w in white]
    af = flipped(a)
    packed = jnp.concatenate(
        [moved(white[0], -6), moved(white[1], -6), moved(white[0], 10), moved(white[1], 10)], axis=0
    )
    stage_o[...] = packed.T.reshape(GROUP, 16, 128)
    packed = jnp.concatenate([moved(af, 8 * t - 6) for t in range(4)], axis=0)
    stage_d[...] = packed.T.reshape(GROUP, 16, 128)[:, :8]

    pl.semaphore_wait(barrier, GROUP - 1)

    others = sorted(
        ((dz, dx) for dz in range(NZ) for dx in range(NX) if dz or dx),
        key=lambda o: -min(o[0], NZ - o[0]) - min(o[1], NX - o[1]),
    )
    spreads = []
    for stage, got, send, recv in ((stage_d, got_d, d_send, d_recv), (stage_o, got_o, o_send, o_recv)):
        copies = []
        for t, (dz, dx) in enumerate(others):
            to = lax.rem(mz + dz, NZ) * NX + lax.rem(mx + dx, NX)
            copy = pltpu.make_async_remote_copy(
                src_ref=stage.at[to], dst_ref=got.at[:, me, :], send_sem=send.at[t], recv_sem=recv.at[t],
                device_id={"chan": to}, device_id_type=MESH,
            )
            copy.start()
            copies.append(copy)
        spreads.append(copies)
    own = [
        pltpu.make_async_copy(stage_d.at[me], got_d.at[:, me, :], own_sem.at[0]),
        pltpu.make_async_copy(stage_o.at[me], got_o.at[:, me, :], own_sem.at[1]),
    ]
    for copy in own:
        copy.start()
    for copy in inputs[2:]:
        copy.wait()

    for which in range(2):
        full = full_v[which]
        high = full.astype(BF16)
        mats_v[which, 0:256] = high
        mats_v[which, 256:512] = high
        mats_v[which, 512:768] = (full - high.astype(F32)).astype(BF16)

    win = [
        jnp.concatenate([win_v[p : p + 1, n * 128 : (n + 1) * 128] for n in range(8)], axis=0)
        for p in range(4)
    ]

    def butterfly(value, distance):
        index = lax.broadcasted_iota(jnp.int32, value.shape, 1)
        high = (index & distance) != 0
        if distance == 4:
            other = pltpu.roll(value, 4, axis=1)
        else:
            other = jnp.where(
                high, pltpu.roll(value, distance, axis=1), pltpu.roll(value, 8 - distance, axis=1)
            )
        return jnp.where(high, other - value, other + value)

    def quarter(re, im, sign):
        index = lax.broadcasted_iota(jnp.int32, re.shape, 1)
        turned = (index & 3) == 3
        return jnp.where(turned, -sign * im, re), jnp.where(turned, sign * re, im)

    def times(re, im, c, s):
        return re * c - im * s, re * s + im * c

    def product(re, im, which):
        count = re.shape[0]
        x = jnp.concatenate([re.reshape(count * 8, 128), im.reshape(count * 8, 128)], axis=1)
        high = x.astype(BF16)
        low = (x - high.astype(F32)).astype(BF16)
        y = jnp.dot(
            jnp.concatenate([high, low, high], axis=1), mats_v[which], preferred_element_type=F32
        )
        return y[:, :128].reshape(count, 8, 128), y[:, 128:].reshape(count, 8, 128)

    def to_wave(re, im):
        re, im = product(re, im, 0)
        re, im = times(re, im, tabs_v[0], tabs_v[1])
        re, im = butterfly(re, 1), butterfly(im, 1)
        re, im = quarter(re, im, 1.0)
        re, im = butterfly(re, 2), butterfly(im, 2)
        re, im = times(re, im, tabs_v[2], tabs_v[3])
        return butterfly(re, 4), butterfly(im, 4)

    def to_spec(re, im):
        re, im = butterfly(re, 4), butterfly(im, 4)
        re, im = times(re, im, tabs_v[2], -tabs_v[3])
        re, im = butterfly(re, 2), butterfly(im, 2)
        re, im = quarter(re, im, -1.0)
        re, im = butterfly(re, 1), butterfly(im, 1)
        re, im = times(re, im, tabs_v[0], -tabs_v[1])
        return product(re, im, 1)

    def gather_taps(u, count):
        out = win[0] * u[0:count]
        for p in range(1, 4):
            out = out + win[p] * u[p : p + count]
        return out

    def spread_taps(v, count):
        out = win[0] * v[3 : 3 + count]
        for p in range(1, 4):
            out = out + win[p] * v[3 - p : 3 - p + count]
        return out

    def keep(value, start, before, after):
        index = lax.broadcasted_iota(jnp.int32, value.shape, 0) + start
        out = value
        if before:
            out = jnp.where((index < 6) & (me == 0), 0.0, out)
        if after:
            out = jnp.where((index >= 22) & (me == GROUP - 1), 0.0, out)
        return out

    own[0].wait()
    for copy in spreads[0]:
        copy.wait_recv()

    lane8 = lax.broadcasted_iota(jnp.int32, (8, 128), 1)
    low64 = lane8 < 64
    low32 = (lane8 & 32) == 0

    def exchange(v):
        y = [None] * 4
        for i in range(2):
            y[i] = jnp.where(low64, v[i], pltpu.roll(v[i + 2], 64, axis=1))
            y[i + 2] = jnp.where(low64, pltpu.roll(v[i], 64, axis=1), v[i + 2])
        z = [None] * 4
        for i in (0, 2):
            z[i] = jnp.where(low32, y[i], pltpu.roll(y[i + 1], 32, axis=1))
            z[i + 1] = jnp.where(low32, pltpu.roll(y[i], 96, axis=1), y[i + 1])
        return z

    for q in range(2):
        turned = got_d[4 * q : 4 * q + 4].reshape(128, 128).T
        for part in range(4):
            base = part * 32
            out = exchange([turned[base + 8 * i : base + 8 * i + 8] for i in range(4)])
            for r in range(4):
                dec[8 * part + 4 * q + r] = out[r]

    def coefficients(start, count):
        stop = start + count
        p = dec[start]
        ps = [p]
        for g in range(start + 1, stop):
            p = dec[g] * p
            ps.append(p)
        b = dec[stop]
        h = ps[-1]
        bs, hs = [b], [h]
        for g in range(stop - 2, start - 1, -1):
            b = dec[g + 1] * b
            h = ps[g - start] + dec[g + 1] * h
            bs.append(b)
            hs.append(h)
        bs.reverse()
        hs.reverse()
        two_p = jnp.stack([2.0 * v for v in ps])
        gains = [2.0 * (1.0 - dec[g]) for g in range(start, stop)]
        left = jnp.stack([2.0 * x + 2.0 * y * z for x, y, z in zip(ps, gains, hs)])
        right = jnp.stack([y * z for y, z in zip(gains, bs)])
        square = sum(4.0 * ps[g - start] * ps[g - start] for g in range(6, 22))
        return two_p, left, right, (ps[15], square, bs[count - 16], 2.0 * hs[count - 16])

    two_p0, left0, right0, coefs0 = coefficients(3, 25)
    two_p1, left1, right1, coefs1 = coefficients(6, 19)
    for turn, coefs in enumerate((coefs0, coefs1)):
        for n, value in enumerate(coefs):
            cx[turn, mx, 8 * n : 8 * n + 8] = value

    sent = spreads[0] + spreads[1]
    sent_left = []

    def x_copies(part, send, recv):
        out = []
        for t in range(1, NX):
            to = mz * NX + lax.rem(mx + t, NX)
            out.append(pltpu.make_async_remote_copy(
                src_ref=part, dst_ref=part, send_sem=send.at[t], recv_sem=recv.at[t],
                device_id={"chan": to}, device_id_type=MESH,
            ))
        for copy in out:
            copy.start()
        sent.extend(out)
        return out

    def z_copies(part, send, recv, left_only=False):
        out = []
        for t in (4, 3, 5, 2, 6, 1, 7):
            to = lax.rem(mz + t, NZ) * NX + mx
            copy = pltpu.make_async_remote_copy(
                src_ref=part, dst_ref=part, send_sem=send.at[t], recv_sem=recv.at[t],
                device_id={"chan": to}, device_id_type=MESH,
            )
            if left_only:
                pl.when(mz + t >= NZ)(copy.start)
                sent_left.append((t, copy))
            else:
                copy.start()
                sent.append(copy)
            out.append((t, copy))
        return out

    def wait_left(copies):
        for t, copy in copies:
            pl.when(mz < t)(copy.wait_recv)

    def wait_all(copies):
        for _, copy in copies:
            copy.wait_recv()

    x_coefs = [x_copies(cx.at[0, mx], xc_send.at[0], xc_recv.at[0]), None]

    own[1].wait()
    for copy in spreads[1]:
        copy.wait_recv()

    for q in range(4):
        turned = got_o[4 * q : 4 * q + 4].reshape(128, 128).T
        for half in range(2):
            for c in range(2):
                base = half * 64 + c * 32
                out = exchange([turned[base + 8 * i : base + 8 * i + 8] for i in range(4)])
                for r in range(4):
                    spec[c, 16 * half + 4 * q + r] = out[r]

    def local_whiten(re, im, start, count):
        stop = start + count
        x = [jnp.stack([re[g], im[g]]) for g in range(count)]
        s = (1.0 - dec[start]) * x[0]
        e = [x[0] + 2.0 * s]
        leaving_right = None
        for g in range(1, count):
            a = dec[start + g]
            s = a * s + (1.0 - a) * x[g]
            e.append(x[g] + 2.0 * s)
            if g == 15:
                leaving_right = s
        back = e[-1]
        w = [None] * count
        leaving_left = None
        w[-1] = e[-1] + 2.0 * (1.0 - dec[stop - 1]) * back
        for g in range(count - 2, -1, -1):
            back = e[g] + dec[start + g + 1] * back
            w[g] = e[g] + 2.0 * (1.0 - dec[start + g]) * back
            if g == count - 16:
                leaving_left = back
        return e, w, leaving_right, leaving_left

    def chain(carry, back, left, right, a, b, k):
        count = len(left)
        cs = [carry]
        for n in range(count):
            cs.append(a[n] * cs[n] + left[n])
        ds = [None] * count
        d = back
        for n in range(count - 1, -1, -1):
            ds[n] = d
            d = b[n] * d + (right[n] + k[n] * cs[n])
        return cs, ds, d

    def pair(ref, base):
        return jnp.stack([ref[base : base + 8], ref[base + 8 : base + 16]])

    zero = jnp.zeros((2, 8, 128), F32)

    z_coefs = [None, None]

    def group_coefficients(turn):
        for copy in x_coefs[turn]:
            copy.wait_recv()
        a, q, b, k = [[cx[turn, n, 8 * m : 8 * m + 8] for n in range(NX)] for m in range(4)]
        ga, gq, gb, gk = a[0], q[0], b[0], k[0]
        for n in range(1, NX):
            gq = gq + q[n] * (ga * ga)
            gk = gb * k[n] * ga + gk
            gb = gb * b[n]
            ga = a[n] * ga
        for m, value in enumerate((ga, gq, gb, gk)):
            cz[turn, mz, 8 * m : 8 * m + 8] = value
        z_coefs[turn] = (
            z_copies(cz.at[turn, mz, pl.ds(0, 16)], zc_send.at[turn, 0], zc_recv.at[turn, 0]),
            z_copies(cz.at[turn, mz, pl.ds(16, 16)], zc_send.at[turn, 1], zc_recv.at[turn, 1], True),
        )

    def row_sum(value):
        return jnp.sum(value, axis=0, keepdims=True)

    def write_pair(ref, base, value):
        ref[base : base + 8] = value[0]
        ref[base + 8 : base + 16] = value[1]

    def carries(turn, e, two_p, right_going, left_going, row):
        xv = xb.at[turn, mx]
        write_pair(xv, 0, right_going)
        write_pair(xv, 16, left_going)
        x_lh = x_copies(xb.at[turn, mx, pl.ds(0, 32)], x_send.at[turn, 0], x_recv.at[turn, 0])
        linear = sum((2.0 * e[g]) * two_p[g] for g in range(16))
        square = sum(e[g] * e[g] for g in range(16))
        write_pair(xv, 32, linear)
        xv[48:49] = row_sum(square[0] + square[1])
        xv[49:50] = row
        x_rest = x_copies(xb.at[turn, mx, pl.ds(32, 18)], x_send.at[turn, 1], x_recv.at[turn, 1])
        if turn == 0:
            x_coefs[1] = x_copies(cx.at[1, mx], xc_send.at[1], xc_recv.at[1])
            group_coefficients(0)
        a, q, b, k = [[cx[turn, n, 8 * m : 8 * m + 8] for n in range(NX)] for m in range(4)]
        for copy in x_lh:
            copy.wait_recv()
        left = [pair(xb.at[turn, n], 0) for n in range(NX)]
        right = [pair(xb.at[turn, n], 16) for n in range(NX)]
        cs, _, out = chain(zero, zero, left, right, a, b, k)
        zv = zb.at[turn, mz]
        write_pair(zv, 0, cs[NX])
        z_l = z_copies(zb.at[turn, mz, pl.ds(0, 16)], z_send.at[turn, 0], z_recv.at[turn, 0])
        write_pair(zv, 16, out)
        z_h = z_copies(zb.at[turn, mz, pl.ds(16, 16)], z_send.at[turn, 1], z_recv.at[turn, 1], True)
        for copy in x_rest:
            copy.wait_recv()
        linear = [pair(xb.at[turn, n], 32) for n in range(NX)]
        total = linear[0]
        partial = jnp.zeros((8, 128), F32)
        ga = a[0]
        for n in range(1, NX):
            full = linear[n] + q[n] * cs[n]
            partial = partial + full[0] * cs[n][0] + full[1] * cs[n][1]
            total = total + ga * (full + q[n] * cs[n])
            ga = a[n] * ga
        write_pair(zv, 32, total)
        zv[48:49] = row_sum(partial) + sum(xb[turn, n, 48:49] for n in range(NX))
        zv[49:50] = sum(xb[turn, n, 49:50] for n in range(NX))
        z_rest = z_copies(zb.at[turn, mz, pl.ds(32, 18)], z_send.at[turn, 2], z_recv.at[turn, 2])
        if turn == 0:
            group_coefficients(1)
        wait_all(z_coefs[turn][0])
        wait_left(z_coefs[turn][1])
        wait_all(z_l)
        za, zq, zbk, zk = [[cz[turn, n, 8 * m : 8 * m + 8] for n in range(NZ)] for m in range(4)]
        zleft = [pair(zb.at[turn, n], 0) for n in range(NZ)]
        wait_left(z_h)
        zright = [pair(zb.at[turn, n], 16) for n in range(NZ)]
        zcs, zds, _ = chain(zero, zero, zleft, zright, za, zbk, zk)
        for n in range(NZ):
            carry_z[0, n] = zcs[n]
            carry_z[1, n] = zds[n]
        cs, ds, _ = chain(carry_z[0, mz], carry_z[1, mz], left, right, a, b, k)
        for n in range(NX):
            carry_x[0, n] = cs[n]
            carry_x[1, n] = ds[n]

        def sums():
            wait_all(z_rest)
            partial = jnp.zeros((8, 128), F32)
            for n in range(NZ):
                full = (pair(zb.at[turn, n], 32) + zq[n] * zcs[n]) * zcs[n]
                partial = partial + full[0] + full[1]
            squares = row_sum(partial) + sum(zb[turn, n, 48:49] for n in range(NZ))
            rows = sum(zb[turn, n, 49:50] for n in range(NZ))
            return jnp.sum(squares, axis=1, keepdims=True), jnp.sum(rows, axis=1, keepdims=True)

        return carry_x[0, mx], carry_x[1, mx], sums

    def corrected(w, left, right, c, d):
        re = jnp.stack([v[0] for v in w]) + left * c[0] + right * d[0]
        im = jnp.stack([v[1] for v in w]) + left * c[1] + right * d[1]
        return re, im

    def padded(re, im):
        fill = jnp.zeros((1, 8, 128), F32)
        return jnp.concatenate([re, fill]), jnp.concatenate([im, fill])

    def squares(value):
        return row_sum(jnp.sum(value[0] * value[0] + value[1] * value[1], axis=0))

    u = to_wave(spec[0], spec[1])
    r0 = [keep(gather_taps(v, 29), 0, True, False) for v in u]
    x = to_spec(*[spread_taps(v, 26) for v in r0])
    x0 = [keep(v, 3, False, True) for v in x]
    mine_r0 = [v[6:22] for v in r0]
    e, w, going_right, going_left = local_whiten(x0[0], x0[1], 3, 25)
    c, d, sums = carries(0, e[3:19], two_p0[3:19], going_right, going_left, squares(mine_r0))
    w = corrected(w, left0, right0, c, d)

    u = to_wave(*padded(*w))
    q1 = [
        keep(gather_taps(v, 22) + RIDGE * r[3:25], 3, True, False) for v, r in zip(u, r0)
    ]
    x = to_spec(*padded(*[spread_taps(v, 19) for v in q1]))
    energy, rr = sums()
    alpha = rr / (energy + RIDGE * rr)
    x1 = [b[3:22] - alpha * keep(v[:19], 6, False, True) for b, v in zip(x0, x)]
    mine_q1 = [v[3:19] for v in q1]
    r1 = [r - alpha * q for r, q in zip(mine_r0, mine_q1)]
    e, w, going_right, going_left = local_whiten(x1[0], x1[1], 6, 19)
    c, d, sums = carries(1, e[:16], two_p1[:16], going_right, going_left, squares(r1))
    w = corrected(w, left1, right1, c, d)

    u = to_wave(*padded(*w))
    n1 = [gather_taps(v, 16) + RIDGE * r for v, r in zip(u, r1)]
    energy, new = sums()
    beta = new / rr
    alpha_next = new / (energy + RIDGE * new - beta * new / alpha)
    for n in range(2):
        direction = r1[n] + beta * mine_r0[n]
        image = n1[n] + beta * mine_q1[n]
        sol = alpha * mine_r0[n] + alpha_next * direction
        res = r1[n] - alpha_next * image
        sol_ref[n] = sol.reshape(16, 1024)
        res_ref[n] = res.reshape(16, 1024)
    for copy in sent:
        copy.wait_send()
    for t, copy in sent_left:
        pl.when(mz + t >= NZ)(copy.wait_send)


def body(observed, window, decays):
    mats, tabs = tables()
    any_space = pl.BlockSpec(memory_space=pltpu.HBM)
    vmem = pl.BlockSpec(memory_space=pltpu.VMEM)
    dma = pltpu.SemaphoreType.DMA
    out = jax.ShapeDtypeStruct((2, 16, 1024), F32)
    return pl.pallas_call(
        kernel,
        out_shape=(out, out),
        in_specs=[any_space] * 5,
        out_specs=(vmem, vmem),
        scratch_shapes=[
            pltpu.VMEM((2, 32, 512), F32),
            pltpu.VMEM((4, 1024), F32),
            pltpu.VMEM((32, 512), F32),
            pltpu.VMEM((2, 256, 256), F32),
            pltpu.VMEM((4, 8, 128), F32),
            pltpu.VMEM((2, 768, 256), BF16),
            pltpu.VMEM((GROUP, 16, 128), F32),
            pltpu.VMEM((GROUP, 8, 128), F32),
            pltpu.VMEM((16, GROUP, 128), F32),
            pltpu.VMEM((8, GROUP, 128), F32),
            pltpu.VMEM((2, 32, 8, 128), F32),
            pltpu.VMEM((32, 8, 128), F32),
            pltpu.VMEM((2, NX, 2, 8, 128), F32),
            pltpu.VMEM((2, NZ, 2, 8, 128), F32),
            pltpu.VMEM((2, NX, 56, 128), F32),
            pltpu.VMEM((2, NZ, 56, 128), F32),
            pltpu.VMEM((2, NX, 32, 128), F32),
            pltpu.VMEM((2, NZ, 32, 128), F32),
            dma((5,)),
            dma((2,)),
            dma((GROUP,)), dma((GROUP,)),
            dma((GROUP,)), dma((GROUP,)),
            dma((2, NX)), dma((2, NX)),
            dma((2, 2, NZ)), dma((2, 2, NZ)),
            dma((2, 2, NX)), dma((2, 2, NX)),
            dma((2, 3, NZ)), dma((2, 3, NZ)),
        ],
        name="invert",
        compiler_params=pltpu.CompilerParams(
            collective_id=0, has_side_effects=True, vmem_limit_bytes=48 * 1024 * 1024
        ),
    )(*[pltpu.with_memory_space_constraint(v, pltpu.HBM) for v in (observed, window, decays, jnp.asarray(mats), jnp.asarray(tabs))])


def solution(mesh):
    return jax.shard_map(
        body,
        mesh=mesh,
        in_specs=(P(None, "chan", "beam"), P(), P("chan", "beam")),
        out_specs=(P(None, ("beam", "chan"), None), P(None, ("beam", "chan"), None)),
        check_vma=False,
    )
```

```python
import functools
import math

import jax
import jax.numpy as jnp
import numpy as np
from jax import lax
from jax.experimental import pallas as pl
from jax.experimental.pallas import tpu as pltpu
from jax.sharding import PartitionSpec as P

MESH = pl.DeviceIdType.MESH
F32 = jnp.float32
BF16 = jnp.bfloat16
GROUP = 32
NX = 4
NZ = 8
RIDGE = 0.5
FLIP = (0, 4, 2, 6, 1, 5, 3, 7)


def tables():
    lane = np.arange(128)
    k2 = 4 * (lane % 32) + lane // 32
    n2 = np.arange(128)
    angle = 2.0 * np.pi * ((k2[:, None] * n2[None, :]) % 128) / 128.0
    cos, sin = np.cos(angle) / 32.0, np.sin(angle) / 32.0
    inverse = np.block([[cos, sin], [-sin, cos]])

    mats = np.stack([inverse, inverse.T]).astype(np.float32)
    turn = 2.0 * np.pi * np.array(FLIP)[:, None] * n2[None, :] / 1024.0
    eighth = 2.0 * np.pi * np.maximum(np.arange(8) - 4, 0) / 8.0
    eighth = np.broadcast_to(eighth[:, None], (8, 128))
    tabs = np.stack([np.cos(turn), np.sin(turn), np.cos(eighth), np.sin(eighth)])
    return mats, tabs.astype(np.float32)


def kernel(
    obs_hbm, win_hbm, dec_hbm, mats_hbm, tabs_hbm, sol_ref, res_ref,
    obs_v, win_v, dec_v, full_v, tabs_v, mats_v, stage_o, stage_d, got_o, got_d,
    spec, dec, carry_x, carry_z, xb, zb, cx, cz,
    in_sem, own_sem, o_send, o_recv, d_send, d_recv, xc_send, xc_recv,
    zc_send, zc_recv, x_send, x_recv, z_send, z_recv,
):
    me = lax.axis_index("chan")
    mz = me // NX
    mx = lax.rem(me, NX)
    barrier = pltpu.get_barrier_semaphore()
    for t in range(1, GROUP):
        pl.semaphore_signal(
            barrier, inc=1, device_id={"chan": lax.rem(me + t, GROUP)}, device_id_type=MESH
        )
    inputs = []
    for t, (src, dst) in enumerate(
        ((obs_hbm, obs_v), (dec_hbm, dec_v), (win_hbm, win_v), (mats_hbm, full_v), (tabs_hbm, tabs_v))
    ):
        copy = pltpu.make_async_copy(src, dst, in_sem.at[t])
        copy.start()
        inputs.append(copy)
    inputs[0].wait()
    inputs[1].wait()

    frames = 512
    lane = lax.broadcasted_iota(jnp.int32, (32, frames), 1)
    row = lax.rem(lax.broadcasted_iota(jnp.int32, (32, frames), 0), 8)

    def shift(value, steps):
        return pltpu.roll(value, steps % frames, axis=value.ndim - 1)

    a = dec_v[...]
    gain = 1.0 - a
    data = [obs_v[0], obs_v[1]]
    prod = jnp.where(lane == 0, 0.0, a)
    run = [gain * d for d in data]
    step = 1
    while step < frames:
        run = [r + prod * shift(r, step) for r in run]
        prod = prod * shift(prod, step)
        step *= 2
    first = [d + 2.0 * r for d, r in zip(data, run)]
    prod = jnp.where(lane == frames - 1, 0.0, shift(a, -1))
    run = first
    step = 1
    while step < frames:
        run = [r + prod * shift(r, -step) for r in run]
        prod = prod * shift(prod, -step)
        step *= 2
    white = [f + 2.0 * gain * r for f, r in zip(first, run)]

    up = (row == 1) | (row == 3)
    down = (row == 4) | (row == 6)

    def flipped(value):
        return jnp.where(
            up,
            pltpu.roll(value, 29, axis=0),
            jnp.where(down, pltpu.roll(value, 3, axis=0), value),
        )

    def moved(value, offset):
        moved_value = shift(value, -offset)
        inside = (lane + offset >= 0) & (lane + offset < frames)
        return jnp.where(inside, moved_value, 0.0)

    white = [flipped(w) for w in white]
    af = flipped(a)
    packed = jnp.concatenate(
        [moved(white[0], -6), moved(white[1], -6), moved(white[0], 10), moved(white[1], 10)], axis=0
    )
    stage_o[...] = packed.T.reshape(GROUP, 16, 128)
    packed = jnp.concatenate([moved(af, 8 * t - 6) for t in range(4)], axis=0)
    stage_d[...] = packed.T.reshape(GROUP, 16, 128)[:, :8]

    pl.semaphore_wait(barrier, GROUP - 1)

    others = sorted(
        ((dz, dx) for dz in range(NZ) for dx in range(NX) if dz or dx),
        key=lambda o: -min(o[0], NZ - o[0]) - min(o[1], NX - o[1]),
    )
    spreads = []
    for stage, got, send, recv in ((stage_d, got_d, d_send, d_recv), (stage_o, got_o, o_send, o_recv)):
        copies = []
        for t, (dz, dx) in enumerate(others):
            to = lax.rem(mz + dz, NZ) * NX + lax.rem(mx + dx, NX)
            copy = pltpu.make_async_remote_copy(
                src_ref=stage.at[to], dst_ref=got.at[:, me, :], send_sem=send.at[t], recv_sem=recv.at[t],
                device_id={"chan": to}, device_id_type=MESH,
            )
            copy.start()
            copies.append(copy)
        spreads.append(copies)
    own = [
        pltpu.make_async_copy(stage_d.at[me], got_d.at[:, me, :], own_sem.at[0]),
        pltpu.make_async_copy(stage_o.at[me], got_o.at[:, me, :], own_sem.at[1]),
    ]
    for copy in own:
        copy.start()
    for copy in inputs[2:]:
        copy.wait()

    for which in range(2):
        full = full_v[which]
        high = full.astype(BF16)
        mats_v[which, 0:256] = high
        mats_v[which, 256:512] = high
        mats_v[which, 512:768] = (full - high.astype(F32)).astype(BF16)

    win = [
        jnp.concatenate([win_v[p : p + 1, n * 128 : (n + 1) * 128] for n in range(8)], axis=0)
        for p in range(4)
    ]

    def butterfly(value, distance):
        index = lax.broadcasted_iota(jnp.int32, value.shape, 1)
        high = (index & distance) != 0
        if distance == 4:
            other = pltpu.roll(value, 4, axis=1)
        else:
            other = jnp.where(
                high, pltpu.roll(value, distance, axis=1), pltpu.roll(value, 8 - distance, axis=1)
            )
        return jnp.where(high, other - value, other + value)

    def quarter(re, im, sign):
        index = lax.broadcasted_iota(jnp.int32, re.shape, 1)
        turned = (index & 3) == 3
        return jnp.where(turned, -sign * im, re), jnp.where(turned, sign * re, im)

    def times(re, im, c, s):
        return re * c - im * s, re * s + im * c

    def product(re, im, which):
        count = re.shape[0]
        x = jnp.concatenate([re.reshape(count * 8, 128), im.reshape(count * 8, 128)], axis=1)
        high = x.astype(BF16)
        low = (x - high.astype(F32)).astype(BF16)
        y = jnp.dot(
            jnp.concatenate([high, low, high], axis=1), mats_v[which], preferred_element_type=F32
        )
        return y[:, :128].reshape(count, 8, 128), y[:, 128:].reshape(count, 8, 128)

    def to_wave(re, im):
        re, im = product(re, im, 0)
        re, im = times(re, im, tabs_v[0], tabs_v[1])
        re, im = butterfly(re, 1), butterfly(im, 1)
        re, im = quarter(re, im, 1.0)
        re, im = butterfly(re, 2), butterfly(im, 2)
        re, im = times(re, im, tabs_v[2], tabs_v[3])
        return butterfly(re, 4), butterfly(im, 4)

    def to_spec(re, im):
        re, im = butterfly(re, 4), butterfly(im, 4)
        re, im = times(re, im, tabs_v[2], -tabs_v[3])
        re, im = butterfly(re, 2), butterfly(im, 2)
        re, im = quarter(re, im, -1.0)
        re, im = butterfly(re, 1), butterfly(im, 1)
        re, im = times(re, im, tabs_v[0], -tabs_v[1])
        return product(re, im, 1)

    def gather_taps(u, count):
        out = win[0] * u[0:count]
        for p in range(1, 4):
            out = out + win[p] * u[p : p + count]
        return out

    def spread_taps(v, count):
        out = win[0] * v[3 : 3 + count]
        for p in range(1, 4):
            out = out + win[p] * v[3 - p : 3 - p + count]
        return out

    def keep(value, start, before, after):
        index = lax.broadcasted_iota(jnp.int32, value.shape, 0) + start
        out = value
        if before:
            out = jnp.where((index < 6) & (me == 0), 0.0, out)
        if after:
            out = jnp.where((index >= 22) & (me == GROUP - 1), 0.0, out)
        return out

    own[0].wait()
    for copy in spreads[0]:
        copy.wait_recv()

    lane8 = lax.broadcasted_iota(jnp.int32, (8, 128), 1)
    low64 = lane8 < 64
    low32 = (lane8 & 32) == 0

    def exchange(v):
        y = [None] * 4
        for i in range(2):
            y[i] = jnp.where(low64, v[i], pltpu.roll(v[i + 2], 64, axis=1))
            y[i + 2] = jnp.where(low64, pltpu.roll(v[i], 64, axis=1), v[i + 2])
        z = [None] * 4
        for i in (0, 2):
            z[i] = jnp.where(low32, y[i], pltpu.roll(y[i + 1], 32, axis=1))
            z[i + 1] = jnp.where(low32, pltpu.roll(y[i], 96, axis=1), y[i + 1])
        return z

    for q in range(2):
        turned = got_d[4 * q : 4 * q + 4].reshape(128, 128).T
        for part in range(4):
            base = part * 32
            out = exchange([turned[base + 8 * i : base + 8 * i + 8] for i in range(4)])
            for r in range(4):
                dec[8 * part + 4 * q + r] = out[r]

    def inverse(a):
        return jnp.where(a > 0.0, 1.0 / jnp.where(a > 0.0, a, 1.0), 0.0)

    def backward(e, start, stop):
        g = {21: e[21]}
        for f in range(20, start - 1, -1):
            g[f] = e[f] + dec[f + 1] * g[f + 1]
        if stop > 22:
            g[22] = jnp.zeros_like(e[21])
        for f in range(23, stop):
            g[f] = (g[f - 1] - e[f - 1]) * inv[f]
        return g

    inv = {f: inverse(dec[f]) for f in (4, 5, 22, 23, 24, 25, 26, 27)}
    twice = {f: 2.0 * (1.0 - dec[f]) for f in range(3, 28)}
    prods = {5: jnp.ones((8, 128), F32)}
    for f in range(6, 28):
        prods[f] = dec[f] * prods[f - 1]
    prods[4] = inv[5]
    prods[3] = inv[4] * inv[5]
    from_c = {f: 2.0 * prods[f] for f in range(3, 28)}
    back_c = backward(from_c, 3, 28)
    back_d = {21: jnp.ones((8, 128), F32), 22: inv[22]}
    for f in range(20, 2, -1):
        back_d[f] = dec[f + 1] * back_d[f + 1]
    for f in range(23, 28):
        back_d[f] = back_d[f - 1] * inv[f]
    left_all = jnp.stack([from_c[f] + twice[f] * back_c[f] for f in range(3, 28)])
    right_all = jnp.stack([twice[f] * back_d[f] for f in range(3, 28)])
    cx[mx, 0:8] = prods[21]
    cx[mx, 8:16] = dec[6] * back_c[6]

    sent = spreads[0] + spreads[1]

    def x_copies(part, send, recv):
        out = []
        for t in range(1, NX):
            to = mz * NX + lax.rem(mx + t, NX)
            out.append(pltpu.make_async_remote_copy(
                src_ref=part, dst_ref=part, send_sem=send.at[t], recv_sem=recv.at[t],
                device_id={"chan": to}, device_id_type=MESH,
            ))
        for copy in out:
            copy.start()
        sent.extend(out)
        return out

    def z_copies(part, send, recv):
        out = []
        for t in (4, 3, 5, 2, 6, 1, 7):
            to = lax.rem(mz + t, NZ) * NX + mx
            out.append(pltpu.make_async_remote_copy(
                src_ref=part, dst_ref=part, send_sem=send.at[t], recv_sem=recv.at[t],
                device_id={"chan": to}, device_id_type=MESH,
            ))
        for copy in out:
            copy.start()
        sent.extend(out)
        return out

    def wait_all(copies):
        for copy in copies:
            copy.wait_recv()

    x_coefs = x_copies(cx.at[mx], xc_send, xc_recv)

    own[1].wait()
    for copy in spreads[1]:
        copy.wait_recv()

    for q in range(4):
        turned = got_o[4 * q : 4 * q + 4].reshape(128, 128).T
        for half in range(2):
            for c in range(2):
                base = half * 64 + c * 32
                out = exchange([turned[base + 8 * i : base + 8 * i + 8] for i in range(4)])
                for r in range(4):
                    spec[c, 16 * half + 4 * q + r] = out[r]

    def local_whiten(re, im, start, stop):
        x = {f: jnp.stack([re[f - start], im[f - start]]) for f in range(start, stop)}
        s = {5: jnp.zeros((2, 8, 128), F32)}
        for f in range(6, stop):
            s[f] = dec[f] * s[f - 1] + (1.0 - dec[f]) * x[f]
        for f in range(4, start - 1, -1):
            s[f] = (s[f + 1] - (1.0 - dec[f + 1]) * x[f + 1]) * inv[f + 1]
        e = {f: x[f] + 2.0 * s[f] for f in range(start, stop)}
        g = backward(e, start, stop)
        w = [e[f] + twice[f] * g[f] for f in range(start, stop)]
        return e, w, s[21], dec[6] * g[6]

    def chain(carry, back, left, right, a, k):
        count = len(left)
        cs = [carry]
        for n in range(count):
            cs.append(a[n] * cs[n] + left[n])
        ds = [None] * count
        d = back
        for n in range(count - 1, -1, -1):
            ds[n] = d
            d = a[n] * d + (right[n] + k[n] * cs[n])
        return cs, ds, d

    def pair(ref, base):
        return jnp.stack([ref[base : base + 8], ref[base + 8 : base + 16]])

    zero = jnp.zeros((2, 8, 128), F32)

    def row_sum(value):
        return jnp.sum(value, axis=0, keepdims=True)

    def write_pair(ref, base, value):
        ref[base : base + 8] = value[0]
        ref[base + 8 : base + 16] = value[1]

    def crossed(cs, right, k):
        total = jnp.zeros((8, 128), F32)
        for c, h, q in zip(cs, right, k):
            full = (4.0 * h + (2.0 * q) * c) * c
            total = total + full[0] + full[1]
        return row_sum(total)

    z_coefs = []

    def group_coefficients():
        for copy in x_coefs:
            copy.wait_recv()
        a, k = [[cx[n, 8 * m : 8 * m + 8] for n in range(NX)] for m in range(2)]
        ga, gk = a[0], k[0]
        for n in range(1, NX):
            gk = gk + k[n] * (ga * ga)
            ga = a[n] * ga
        cz[mz, 0:8] = ga
        cz[mz, 8:16] = gk
        z_coefs.extend(z_copies(cz.at[mz], zc_send, zc_recv))

    def carries(turn, e, right_going, left_going, row):
        xv = xb.at[turn, mx]
        write_pair(xv, 0, right_going)
        write_pair(xv, 16, left_going)
        square = sum(e[f] * e[f] for f in range(6, 22))
        xv[32:33] = row_sum(square[0] + square[1])
        xv[33:34] = row
        x_all = x_copies(xb.at[turn, mx, pl.ds(0, 34)], x_send.at[turn], x_recv.at[turn])
        if turn == 0:
            group_coefficients()
        a, k = [[cx[n, 8 * m : 8 * m + 8] for n in range(NX)] for m in range(2)]
        for copy in x_all:
            copy.wait_recv()
        left = [pair(xb.at[turn, n], 0) for n in range(NX)]
        right = [pair(xb.at[turn, n], 16) for n in range(NX)]
        cs, _, out = chain(zero, zero, left, right, a, k)
        zv = zb.at[turn, mz]
        write_pair(zv, 0, cs[NX])
        write_pair(zv, 16, out)
        zv[32:33] = crossed(cs[:NX], right, k) + sum(xb[turn, n, 32:33] for n in range(NX))
        zv[33:34] = sum(xb[turn, n, 33:34] for n in range(NX))
        z_all = z_copies(zb.at[turn, mz, pl.ds(0, 34)], z_send.at[turn], z_recv.at[turn])
        if turn == 0:
            wait_all(z_coefs)
        za, zk = [[cz[n, 8 * m : 8 * m + 8] for n in range(NZ)] for m in range(2)]
        wait_all(z_all)
        zleft = [pair(zb.at[turn, n], 0) for n in range(NZ)]
        zright = [pair(zb.at[turn, n], 16) for n in range(NZ)]
        zcs, zds, _ = chain(zero, zero, zleft, zright, za, zk)
        for n in range(NZ):
            carry_z[0, n] = zcs[n]
            carry_z[1, n] = zds[n]
        cs, ds, _ = chain(carry_z[0, mz], carry_z[1, mz], left, right, a, k)
        for n in range(NX):
            carry_x[0, n] = cs[n]
            carry_x[1, n] = ds[n]

        def sums():
            squares = crossed(zcs[:NZ], zright, zk) + sum(zb[turn, n, 32:33] for n in range(NZ))
            rows = sum(zb[turn, n, 33:34] for n in range(NZ))
            return jnp.sum(squares, axis=1, keepdims=True), jnp.sum(rows, axis=1, keepdims=True)

        return carry_x[0, mx], carry_x[1, mx], sums

    def corrected(w, left, right, c, d):
        re = jnp.stack([v[0] for v in w]) + left * c[0] + right * d[0]
        im = jnp.stack([v[1] for v in w]) + left * c[1] + right * d[1]
        return re, im

    def padded(re, im):
        fill = jnp.zeros((1, 8, 128), F32)
        return jnp.concatenate([re, fill]), jnp.concatenate([im, fill])

    def squares(value):
        return row_sum(jnp.sum(value[0] * value[0] + value[1] * value[1], axis=0))

    u = to_wave(spec[0], spec[1])
    r0 = [keep(gather_taps(v, 29), 0, True, False) for v in u]
    x = to_spec(*[spread_taps(v, 26) for v in r0])
    x0 = [keep(v, 3, False, True) for v in x]
    mine_r0 = [v[6:22] for v in r0]
    e, w, going_right, going_left = local_whiten(x0[0], x0[1], 3, 28)
    c, d, sums = carries(0, e, going_right, going_left, squares(mine_r0))
    w = corrected(w, left_all, right_all, c, d)

    u = to_wave(*padded(*w))
    q1 = [
        keep(gather_taps(v, 22) + RIDGE * r[3:25], 3, True, False) for v, r in zip(u, r0)
    ]
    x = to_spec(*padded(*[spread_taps(v, 19) for v in q1]))
    energy, rr = sums()
    alpha = rr / (energy + RIDGE * rr)
    x1 = [b[3:22] - alpha * keep(v[:19], 6, False, True) for b, v in zip(x0, x)]
    mine_q1 = [v[3:19] for v in q1]
    r1 = [r - alpha * q for r, q in zip(mine_r0, mine_q1)]
    e, w, going_right, going_left = local_whiten(x1[0], x1[1], 6, 25)
    c, d, sums = carries(1, e, going_right, going_left, squares(r1))
    w = corrected(w, left_all[3:22], right_all[3:22], c, d)

    u = to_wave(*padded(*w))
    n1 = [gather_taps(v, 16) + RIDGE * r for v, r in zip(u, r1)]
    energy, new = sums()
    beta = new / rr
    alpha_next = new / (energy + RIDGE * new - beta * new / alpha)
    for n in range(2):
        direction = r1[n] + beta * mine_r0[n]
        image = n1[n] + beta * mine_q1[n]
        sol = alpha * mine_r0[n] + alpha_next * direction
        res = r1[n] - alpha_next * image
        sol_ref[n] = sol.reshape(16, 1024)
        res_ref[n] = res.reshape(16, 1024)
    for copy in sent:
        copy.wait_send()


def body(observed, window, decays):
    mats, tabs = tables()
    any_space = pl.BlockSpec(memory_space=pltpu.HBM)
    vmem = pl.BlockSpec(memory_space=pltpu.VMEM)
    dma = pltpu.SemaphoreType.DMA
    out = jax.ShapeDtypeStruct((2, 16, 1024), F32)
    return pl.pallas_call(
        kernel,
        out_shape=(out, out),
        in_specs=[any_space] * 5,
        out_specs=(vmem, vmem),
        scratch_shapes=[
            pltpu.VMEM((2, 32, 512), F32),
            pltpu.VMEM((4, 1024), F32),
            pltpu.VMEM((32, 512), F32),
            pltpu.VMEM((2, 256, 256), F32),
            pltpu.VMEM((4, 8, 128), F32),
            pltpu.VMEM((2, 768, 256), BF16),
            pltpu.VMEM((GROUP, 16, 128), F32),
            pltpu.VMEM((GROUP, 8, 128), F32),
            pltpu.VMEM((16, GROUP, 128), F32),
            pltpu.VMEM((8, GROUP, 128), F32),
            pltpu.VMEM((2, 32, 8, 128), F32),
            pltpu.VMEM((32, 8, 128), F32),
            pltpu.VMEM((2, NX, 2, 8, 128), F32),
            pltpu.VMEM((2, NZ, 2, 8, 128), F32),
            pltpu.VMEM((2, NX, 40, 128), F32),
            pltpu.VMEM((2, NZ, 40, 128), F32),
            pltpu.VMEM((NX, 16, 128), F32),
            pltpu.VMEM((NZ, 16, 128), F32),
            dma((5,)),
            dma((2,)),
            dma((GROUP,)), dma((GROUP,)),
            dma((GROUP,)), dma((GROUP,)),
            dma((NX,)), dma((NX,)),
            dma((NZ,)), dma((NZ,)),
            dma((2, NX)), dma((2, NX)),
            dma((2, NZ)), dma((2, NZ)),
        ],
        name="invert",
        compiler_params=pltpu.CompilerParams(
            collective_id=0, has_side_effects=True, vmem_limit_bytes=48 * 1024 * 1024
        ),
    )(*[pltpu.with_memory_space_constraint(v, pltpu.HBM) for v in (observed, window, decays, jnp.asarray(mats), jnp.asarray(tabs))])


def solution(mesh):
    return jax.shard_map(
        body,
        mesh=mesh,
        in_specs=(P(None, "chan", "beam"), P(), P("chan", "beam")),
        out_specs=(P(None, ("beam", "chan"), None), P(None, ("beam", "chan"), None)),
        check_vma=False,
    )
```

```python
import functools
import math

import jax
import jax.numpy as jnp
import numpy as np
from jax import lax
from jax.experimental import pallas as pl
from jax.experimental.pallas import tpu as pltpu
from jax.sharding import PartitionSpec as P

MESH = pl.DeviceIdType.MESH
F32 = jnp.float32
BF16 = jnp.bfloat16
GROUP = 32
NX = 4
NZ = 8
RIDGE = 0.5
FLIP = (0, 4, 2, 6, 1, 5, 3, 7)


def tables():
    lane = np.arange(128)
    k2 = 4 * (lane % 32) + lane // 32
    n2 = np.arange(128)
    angle = 2.0 * np.pi * ((k2[:, None] * n2[None, :]) % 128) / 128.0
    cos, sin = np.cos(angle) / 32.0, np.sin(angle) / 32.0
    inverse = np.block([[cos, sin], [-sin, cos]])

    mats = np.stack([inverse, inverse.T]).astype(np.float32)
    turn = 2.0 * np.pi * np.array(FLIP)[:, None] * n2[None, :] / 1024.0
    eighth = 2.0 * np.pi * np.maximum(np.arange(8) - 4, 0) / 8.0
    eighth = np.broadcast_to(eighth[:, None], (8, 128))
    tabs = np.stack([np.cos(turn), np.sin(turn), np.cos(eighth), np.sin(eighth)])
    return mats, tabs.astype(np.float32)


def kernel(
    obs_hbm, win_hbm, dec_hbm, mats_hbm, tabs_hbm, base_ref, mid_ref, drop_ref, share_ref,
    obs_v, win_v, dec_v, full_v, tabs_v, mats_v, stage_o, stage_d, got_o, got_d,
    spec, dec, carry_x, carry_z, xb, zb, cx, cz,
    in_sem, own_sem, o_send, o_recv, d_send, d_recv, xc_send, xc_recv,
    zc_send, zc_recv, x_send, x_recv, z_send, z_recv,
):
    me = lax.axis_index("chan")
    mz = me // NX
    mx = lax.rem(me, NX)
    barrier = pltpu.get_barrier_semaphore()
    for t in range(1, GROUP):
        pl.semaphore_signal(
            barrier, inc=1, device_id={"chan": lax.rem(me + t, GROUP)}, device_id_type=MESH
        )
    inputs = []
    for t, (src, dst) in enumerate(
        ((obs_hbm, obs_v), (dec_hbm, dec_v), (win_hbm, win_v), (mats_hbm, full_v), (tabs_hbm, tabs_v))
    ):
        copy = pltpu.make_async_copy(src, dst, in_sem.at[t])
        copy.start()
        inputs.append(copy)
    inputs[0].wait()
    inputs[1].wait()

    frames = 512
    lane = lax.broadcasted_iota(jnp.int32, (32, frames), 1)
    row = lax.rem(lax.broadcasted_iota(jnp.int32, (32, frames), 0), 8)

    def shift(value, steps):
        return pltpu.roll(value, steps % frames, axis=value.ndim - 1)

    a = dec_v[...]
    gain = 1.0 - a
    data = [obs_v[0], obs_v[1]]
    prod = jnp.where(lane == 0, 0.0, a)
    run = [gain * d for d in data]
    step = 1
    while step < frames:
        run = [r + prod * shift(r, step) for r in run]
        prod = prod * shift(prod, step)
        step *= 2
    first = [d + 2.0 * r for d, r in zip(data, run)]
    prod = jnp.where(lane == frames - 1, 0.0, shift(a, -1))
    run = first
    step = 1
    while step < frames:
        run = [r + prod * shift(r, -step) for r in run]
        prod = prod * shift(prod, -step)
        step *= 2
    white = [f + 2.0 * gain * r for f, r in zip(first, run)]

    up = (row == 1) | (row == 3)
    down = (row == 4) | (row == 6)

    def flipped(value):
        return jnp.where(
            up,
            pltpu.roll(value, 29, axis=0),
            jnp.where(down, pltpu.roll(value, 3, axis=0), value),
        )

    def moved(value, offset):
        moved_value = shift(value, -offset)
        inside = (lane + offset >= 0) & (lane + offset < frames)
        return jnp.where(inside, moved_value, 0.0)

    white = [flipped(w) for w in white]
    af = flipped(a)
    packed = jnp.concatenate(
        [moved(white[0], -6), moved(white[1], -6), moved(white[0], 10), moved(white[1], 10)], axis=0
    )
    stage_o[...] = packed.T.reshape(GROUP, 16, 128)
    packed = jnp.concatenate([moved(af, 8 * t - 6) for t in range(4)], axis=0)
    stage_d[...] = packed.T.reshape(GROUP, 16, 128)[:, :8]

    pl.semaphore_wait(barrier, GROUP - 1)

    others = sorted(
        ((dz, dx) for dz in range(NZ) for dx in range(NX) if dz or dx),
        key=lambda o: -min(o[0], NZ - o[0]) - min(o[1], NX - o[1]),
    )
    for stage, got, send, recv in ((stage_d, got_d, d_send, d_recv), (stage_o, got_o, o_send, o_recv)):
        for dz, dx in others:
            to = lax.rem(mz + dz, NZ) * NX + lax.rem(mx + dx, NX)
            copy = pltpu.make_async_remote_copy(
                src_ref=stage.at[to], dst_ref=got.at[:, me, :], send_sem=send, recv_sem=recv,
                device_id={"chan": to}, device_id_type=MESH,
            )
            copy.start()
    own = [
        pltpu.make_async_copy(stage_d.at[me], got_d.at[:, me, :], own_sem.at[0]),
        pltpu.make_async_copy(stage_o.at[me], got_o.at[:, me, :], own_sem.at[1]),
    ]
    for copy in own:
        copy.start()
    for copy in inputs[2:]:
        copy.wait()

    for which in range(2):
        full = full_v[which]
        high = full.astype(BF16)
        mats_v[which, 0:256] = high
        mats_v[which, 256:512] = high
        mats_v[which, 512:768] = (full - high.astype(F32)).astype(BF16)

    win = [
        jnp.concatenate([win_v[p : p + 1, n * 128 : (n + 1) * 128] for n in range(8)], axis=0)
        for p in range(4)
    ]

    def butterfly(value, distance):
        index = lax.broadcasted_iota(jnp.int32, value.shape, 1)
        high = (index & distance) != 0
        if distance == 4:
            other = pltpu.roll(value, 4, axis=1)
        else:
            other = jnp.where(
                high, pltpu.roll(value, distance, axis=1), pltpu.roll(value, 8 - distance, axis=1)
            )
        return jnp.where(high, other - value, other + value)

    def quarter(re, im, sign):
        index = lax.broadcasted_iota(jnp.int32, re.shape, 1)
        turned = (index & 3) == 3
        return jnp.where(turned, -sign * im, re), jnp.where(turned, sign * re, im)

    def times(re, im, c, s):
        return re * c - im * s, re * s + im * c

    def product(re, im, which):
        count = re.shape[0]
        x = jnp.concatenate([re.reshape(count * 8, 128), im.reshape(count * 8, 128)], axis=1)
        high = x.astype(BF16)
        low = (x - high.astype(F32)).astype(BF16)
        y = jnp.dot(
            jnp.concatenate([high, low, high], axis=1), mats_v[which], preferred_element_type=F32
        )
        return y[:, :128].reshape(count, 8, 128), y[:, 128:].reshape(count, 8, 128)

    def to_wave(re, im):
        re, im = product(re, im, 0)
        re, im = times(re, im, tabs_v[0], tabs_v[1])
        re, im = butterfly(re, 1), butterfly(im, 1)
        re, im = quarter(re, im, 1.0)
        re, im = butterfly(re, 2), butterfly(im, 2)
        re, im = times(re, im, tabs_v[2], tabs_v[3])
        return butterfly(re, 4), butterfly(im, 4)

    def to_spec(re, im):
        re, im = butterfly(re, 4), butterfly(im, 4)
        re, im = times(re, im, tabs_v[2], -tabs_v[3])
        re, im = butterfly(re, 2), butterfly(im, 2)
        re, im = quarter(re, im, -1.0)
        re, im = butterfly(re, 1), butterfly(im, 1)
        re, im = times(re, im, tabs_v[0], -tabs_v[1])
        return product(re, im, 1)

    def gather_taps(u, count):
        out = win[0] * u[0:count]
        for p in range(1, 4):
            out = out + win[p] * u[p : p + count]
        return out

    def spread_taps(v, count):
        out = win[0] * v[3 : 3 + count]
        for p in range(1, 4):
            out = out + win[p] * v[3 - p : 3 - p + count]
        return out

    def keep(value, start, before, after):
        index = lax.broadcasted_iota(jnp.int32, value.shape, 0) + start
        out = value
        if before:
            out = jnp.where((index < 6) & (me == 0), 0.0, out)
        if after:
            out = jnp.where((index >= 22) & (me == GROUP - 1), 0.0, out)
        return out

    def wait_for(ref, sem):
        pltpu.make_async_copy(ref, ref, sem).wait()

    own[0].wait()
    wait_for(got_d.at[:, pl.ds(0, GROUP - 1)], d_recv)

    lane8 = lax.broadcasted_iota(jnp.int32, (8, 128), 1)
    low64 = lane8 < 64
    low32 = (lane8 & 32) == 0

    def exchange(v):
        y = [None] * 4
        for i in range(2):
            y[i] = jnp.where(low64, v[i], pltpu.roll(v[i + 2], 64, axis=1))
            y[i + 2] = jnp.where(low64, pltpu.roll(v[i], 64, axis=1), v[i + 2])
        z = [None] * 4
        for i in (0, 2):
            z[i] = jnp.where(low32, y[i], pltpu.roll(y[i + 1], 32, axis=1))
            z[i + 1] = jnp.where(low32, pltpu.roll(y[i], 96, axis=1), y[i + 1])
        return z

    for q in range(2):
        turned = got_d[4 * q : 4 * q + 4].reshape(128, 128).T
        for part in range(4):
            base = part * 32
            out = exchange([turned[base + 8 * i : base + 8 * i + 8] for i in range(4)])
            for r in range(4):
                dec[8 * part + 4 * q + r] = out[r]

    def inverse(a):
        return jnp.where(a > 0.0, 1.0 / jnp.where(a > 0.0, a, 1.0), 0.0)

    def backward(e, start, stop):
        g = {21: e[21]}
        for f in range(20, start - 1, -1):
            g[f] = e[f] + dec[f + 1] * g[f + 1]
        if stop > 22:
            g[22] = jnp.zeros_like(e[21])
        for f in range(23, stop):
            g[f] = (g[f - 1] - e[f - 1]) * inv[f]
        return g

    inv = {f: inverse(dec[f]) for f in (4, 5, 22, 23, 24, 25, 26, 27)}
    twice = {f: 2.0 * (1.0 - dec[f]) for f in range(3, 28)}
    prods = {5: jnp.ones((8, 128), F32)}
    for f in range(6, 28):
        prods[f] = dec[f] * prods[f - 1]
    prods[4] = inv[5]
    prods[3] = inv[4] * inv[5]
    from_c = {f: 2.0 * prods[f] for f in range(3, 28)}
    back_c = backward(from_c, 3, 28)
    back_d = {21: jnp.ones((8, 128), F32), 22: inv[22]}
    for f in range(20, 2, -1):
        back_d[f] = dec[f + 1] * back_d[f + 1]
    for f in range(23, 28):
        back_d[f] = back_d[f - 1] * inv[f]
    left_all = jnp.stack([from_c[f] + twice[f] * back_c[f] for f in range(3, 28)])
    right_all = jnp.stack([twice[f] * back_d[f] for f in range(3, 28)])
    cx[mx, 0:8] = prods[21]
    cx[mx, 8:16] = dec[6] * back_c[6]


    def x_copies(part, send, recv):
        out = []
        for t in range(1, NX):
            to = mz * NX + lax.rem(mx + t, NX)
            out.append(pltpu.make_async_remote_copy(
                src_ref=part, dst_ref=part, send_sem=send, recv_sem=recv,
                device_id={"chan": to}, device_id_type=MESH,
            ))
        for copy in out:
            copy.start()

    def z_copies(part, send, recv):
        out = []
        for t in (4, 3, 5, 2, 6, 1, 7):
            to = lax.rem(mz + t, NZ) * NX + mx
            out.append(pltpu.make_async_remote_copy(
                src_ref=part, dst_ref=part, send_sem=send, recv_sem=recv,
                device_id={"chan": to}, device_id_type=MESH,
            ))
        for copy in out:
            copy.start()

    x_copies(cx.at[mx], xc_send, xc_recv)

    own[1].wait()
    wait_for(got_o.at[:, pl.ds(0, GROUP - 1)], o_recv)

    for q in range(4):
        turned = got_o[4 * q : 4 * q + 4].reshape(128, 128).T
        for half in range(2):
            for c in range(2):
                base = half * 64 + c * 32
                out = exchange([turned[base + 8 * i : base + 8 * i + 8] for i in range(4)])
                for r in range(4):
                    spec[c, 16 * half + 4 * q + r] = out[r]

    def local_whiten(re, im, start, stop):
        x = {f: jnp.stack([re[f - start], im[f - start]]) for f in range(start, stop)}
        s = {5: jnp.zeros((2, 8, 128), F32)}
        for f in range(6, stop):
            s[f] = dec[f] * s[f - 1] + (1.0 - dec[f]) * x[f]
        for f in range(4, start - 1, -1):
            s[f] = (s[f + 1] - (1.0 - dec[f + 1]) * x[f + 1]) * inv[f + 1]
        e = {f: x[f] + 2.0 * s[f] for f in range(start, stop)}
        g = backward(e, start, stop)
        w = [e[f] + twice[f] * g[f] for f in range(start, stop)]
        return e, w, s[21], dec[6] * g[6]

    def chain(carry, back, left, right, a, k):
        count = len(left)
        cs = [carry]
        for n in range(count):
            cs.append(a[n] * cs[n] + left[n])
        ds = [None] * count
        d = back
        for n in range(count - 1, -1, -1):
            ds[n] = d
            d = a[n] * d + (right[n] + k[n] * cs[n])
        return cs, ds, d

    def pair(ref, base):
        return jnp.stack([ref[base : base + 8], ref[base + 8 : base + 16]])

    zero = jnp.zeros((2, 8, 128), F32)

    def row_sum(value):
        return jnp.sum(value, axis=0, keepdims=True)

    def write_pair(ref, base, value):
        ref[base : base + 8] = value[0]
        ref[base + 8 : base + 16] = value[1]

    def crossed(cs, right, k):
        total = jnp.zeros((8, 128), F32)
        for c, h, q in zip(cs, right, k):
            full = (4.0 * h + (2.0 * q) * c) * c
            total = total + full[0] + full[1]
        return row_sum(total)

    def group_coefficients():
        wait_for(cx.at[pl.ds(0, NX - 1)], xc_recv)
        a, k = [[cx[n, 8 * m : 8 * m + 8] for n in range(NX)] for m in range(2)]
        ga, gk = a[0], k[0]
        for n in range(1, NX):
            gk = gk + k[n] * (ga * ga)
            ga = a[n] * ga
        cz[mz, 0:8] = ga
        cz[mz, 8:16] = gk
        z_copies(cz.at[mz], zc_send, zc_recv)

    def carries(turn, e, right_going, left_going, row):
        xv = xb.at[turn, mx]
        write_pair(xv, 0, right_going)
        write_pair(xv, 16, left_going)
        square = sum(e[f] * e[f] for f in range(6, 22))
        xv[32:33] = row_sum(square[0] + square[1])
        xv[33:34] = row
        x_copies(xb.at[turn, mx, pl.ds(0, 34)], x_send.at[turn], x_recv.at[turn])
        if turn == 0:
            group_coefficients()
        a, k = [[cx[n, 8 * m : 8 * m + 8] for n in range(NX)] for m in range(2)]
        if turn == 0:
            wait_for(stage_d.at[pl.ds(0, GROUP - 1)], d_send)
            wait_for(stage_o.at[pl.ds(0, GROUP - 1)], o_send)
            wait_for(cx.at[pl.ds(0, NX - 1)], xc_send)
        else:
            wait_for(cz.at[pl.ds(0, NZ - 1)], zc_send)
            wait_for(zb.at[0, pl.ds(0, NZ - 1), pl.ds(0, 34)], z_send.at[0])
        wait_for(xb.at[turn, pl.ds(0, NX - 1), pl.ds(0, 34)], x_recv.at[turn])
        left = [pair(xb.at[turn, n], 0) for n in range(NX)]
        right = [pair(xb.at[turn, n], 16) for n in range(NX)]
        cs, _, out = chain(zero, zero, left, right, a, k)
        zv = zb.at[turn, mz]
        write_pair(zv, 0, cs[NX])
        write_pair(zv, 16, out)
        zv[32:33] = crossed(cs[:NX], right, k) + sum(xb[turn, n, 32:33] for n in range(NX))
        zv[33:34] = sum(xb[turn, n, 33:34] for n in range(NX))
        z_copies(zb.at[turn, mz, pl.ds(0, 34)], z_send.at[turn], z_recv.at[turn])
        if turn == 0:
            wait_for(cz.at[pl.ds(0, NZ - 1)], zc_recv)
        za, zk = [[cz[n, 8 * m : 8 * m + 8] for n in range(NZ)] for m in range(2)]
        wait_for(xb.at[turn, pl.ds(0, NX - 1), pl.ds(0, 34)], x_send.at[turn])
        wait_for(zb.at[turn, pl.ds(0, NZ - 1), pl.ds(0, 34)], z_recv.at[turn])
        zleft = [pair(zb.at[turn, n], 0) for n in range(NZ)]
        zright = [pair(zb.at[turn, n], 16) for n in range(NZ)]
        zcs, zds, _ = chain(zero, zero, zleft, zright, za, zk)
        for n in range(NZ):
            carry_z[0, n] = zcs[n]
            carry_z[1, n] = zds[n]
        cs, ds, _ = chain(carry_z[0, mz], carry_z[1, mz], left, right, a, k)
        for n in range(NX):
            carry_x[0, n] = cs[n]
            carry_x[1, n] = ds[n]

        def sums():
            squares = crossed(zcs[:NZ], zright, zk) + sum(zb[turn, n, 32:33] for n in range(NZ))
            rows = sum(zb[turn, n, 33:34] for n in range(NZ))
            return jnp.sum(squares, axis=1, keepdims=True), jnp.sum(rows, axis=1, keepdims=True)

        return carry_x[0, mx], carry_x[1, mx], sums

    def corrected(w, left, right, c, d):
        re = jnp.stack([v[0] for v in w]) + left * c[0] + right * d[0]
        im = jnp.stack([v[1] for v in w]) + left * c[1] + right * d[1]
        return re, im

    def padded(re, im):
        fill = jnp.zeros((1, 8, 128), F32)
        return jnp.concatenate([re, fill]), jnp.concatenate([im, fill])

    def squares(value):
        return row_sum(jnp.sum(value[0] * value[0] + value[1] * value[1], axis=0))

    u = to_wave(spec[0], spec[1])
    r0 = [keep(gather_taps(v, 29), 0, True, False) for v in u]
    x = to_spec(*[spread_taps(v, 26) for v in r0])
    x0 = [keep(v, 3, False, True) for v in x]
    mine_r0 = [v[6:22] for v in r0]
    e, w, going_right, going_left = local_whiten(x0[0], x0[1], 3, 28)
    c, d, sums = carries(0, e, going_right, going_left, squares(mine_r0))
    w = corrected(w, left_all, right_all, c, d)

    u = to_wave(*padded(*w))
    q1 = [
        keep(gather_taps(v, 22) + RIDGE * r[3:25], 3, True, False) for v, r in zip(u, r0)
    ]
    x = to_spec(*padded(*[spread_taps(v, 19) for v in q1]))
    energy, rr = sums()
    alpha = rr / (energy + RIDGE * rr)
    x1 = [b[3:22] - alpha * keep(v[:19], 6, False, True) for b, v in zip(x0, x)]
    mine_q1 = [v[3:19] for v in q1]
    r1 = [r - alpha * q for r, q in zip(mine_r0, mine_q1)]
    e, w, going_right, going_left = local_whiten(x1[0], x1[1], 6, 25)
    c, d, sums = carries(1, e, going_right, going_left, squares(r1))
    w = corrected(w, left_all[3:22], right_all[3:22], c, d)

    u = to_wave(*padded(*w))
    n1 = [gather_taps(v, 16) + RIDGE * r for v, r in zip(u, r1)]
    energy, new = sums()
    beta = new / rr
    alpha_next = new / (energy + RIDGE * new - beta * new / alpha)
    share_ref[...] = jnp.broadcast_to(alpha_next, (8, 1024))
    for n in range(2):
        image = n1[n] + beta * mine_q1[n]
        base_ref[n] = ((alpha + alpha_next * beta) * mine_r0[n]).reshape(16, 1024)
        mid_ref[n] = r1[n].reshape(16, 1024)
        drop_ref[n] = (alpha_next * image).reshape(16, 1024)
    wait_for(zb.at[1, pl.ds(0, NZ - 1), pl.ds(0, 34)], z_send.at[1])


def body(observed, window, decays):
    mats, tabs = tables()
    any_space = pl.BlockSpec(memory_space=pltpu.HBM)
    vmem = pl.BlockSpec(memory_space=pltpu.VMEM)
    dma = pltpu.SemaphoreType.DMA
    out = jax.ShapeDtypeStruct((2, 16, 1024), F32)
    base, mid, drop, share = pl.pallas_call(
        kernel,
        out_shape=(out, out, out, jax.ShapeDtypeStruct((8, 1024), F32)),
        in_specs=[any_space] * 5,
        out_specs=(vmem,) * 4,
        scratch_shapes=[
            pltpu.VMEM((2, 32, 512), F32),
            pltpu.VMEM((4, 1024), F32),
            pltpu.VMEM((32, 512), F32),
            pltpu.VMEM((2, 256, 256), F32),
            pltpu.VMEM((4, 8, 128), F32),
            pltpu.VMEM((2, 768, 256), BF16),
            pltpu.VMEM((GROUP, 16, 128), F32),
            pltpu.VMEM((GROUP, 8, 128), F32),
            pltpu.VMEM((16, GROUP, 128), F32),
            pltpu.VMEM((8, GROUP, 128), F32),
            pltpu.VMEM((2, 32, 8, 128), F32),
            pltpu.VMEM((32, 8, 128), F32),
            pltpu.VMEM((2, NX, 2, 8, 128), F32),
            pltpu.VMEM((2, NZ, 2, 8, 128), F32),
            pltpu.VMEM((2, NX, 40, 128), F32),
            pltpu.VMEM((2, NZ, 40, 128), F32),
            pltpu.VMEM((NX, 16, 128), F32),
            pltpu.VMEM((NZ, 16, 128), F32),
            dma((5,)),
            dma((2,)),
            dma, dma, dma, dma, dma, dma, dma, dma,
            dma((2,)), dma((2,)), dma((2,)), dma((2,)),
        ],
        name="invert",
        compiler_params=pltpu.CompilerParams(
            collective_id=0, has_side_effects=True, vmem_limit_bytes=48 * 1024 * 1024
        ),
    )(*[pltpu.with_memory_space_constraint(v, pltpu.HBM) for v in (observed, window, decays, jnp.asarray(mats), jnp.asarray(tabs))])
    return base + share[:1] * mid, mid - drop


def solution(mesh):
    return jax.shard_map(
        body,
        mesh=mesh,
        in_specs=(P(None, "chan", "beam"), P(), P("chan", "beam")),
        out_specs=(P(None, ("beam", "chan"), None), P(None, ("beam", "chan"), None)),
        check_vma=False,
    )
```

```python
import functools
import math

import jax
import jax.numpy as jnp
import numpy as np
from jax import lax
from jax.experimental import pallas as pl
from jax.experimental.pallas import tpu as pltpu
from jax.sharding import PartitionSpec as P

MESH = pl.DeviceIdType.MESH
F32 = jnp.float32
BF16 = jnp.bfloat16
GROUP = 32
NX = 4
NZ = 8
RIDGE = 0.5
FLIP = (0, 4, 2, 6, 1, 5, 3, 7)


def tables():
    lane = np.arange(128)
    k2 = 4 * (lane % 32) + lane // 32
    n2 = np.arange(128)
    angle = 2.0 * np.pi * ((k2[:, None] * n2[None, :]) % 128) / 128.0
    cos, sin = np.cos(angle) / 32.0, np.sin(angle) / 32.0
    inverse = np.block([[cos, sin], [-sin, cos]])

    mats = np.stack([inverse, inverse.T]).astype(np.float32)
    turn = 2.0 * np.pi * np.array(FLIP)[:, None] * n2[None, :] / 1024.0
    eighth = 2.0 * np.pi * np.maximum(np.arange(8) - 4, 0) / 8.0
    eighth = np.broadcast_to(eighth[:, None], (8, 128))
    tabs = np.stack([np.cos(turn), np.sin(turn), np.cos(eighth), np.sin(eighth)])
    return mats, tabs.astype(np.float32)


def kernel(
    obs_hbm, win_hbm, dec_hbm, mats_hbm, tabs_hbm, base_ref, mid_ref, drop_ref, share_ref,
    obs_v, win_v, dec_v, full_v, tabs_v, mats_v, stage_o, stage_d, got_o, got_d,
    spec, dec, carry_x, carry_z, xb, zb, cx, cz, out_halo, in_halo,
    in_sem, own_sem, o_send, o_recv, d_send, d_recv, xc_send, xc_recv,
    zc_send, zc_recv, x_send, x_recv, z_send, z_recv,
    h_send, h_recv,
):
    me = lax.axis_index("chan")
    mz = me // NX
    mx = lax.rem(me, NX)
    barrier = pltpu.get_barrier_semaphore()
    others = sorted(
        ((dz, dx) for dz in range(NZ) for dx in range(NX) if dz or dx),
        key=lambda o: -min(o[0], NZ - o[0]) - min(o[1], NX - o[1]),
    )
    others = [lax.rem(mz + dz, NZ) * NX + lax.rem(mx + dx, NX) for dz, dx in others]
    for to in others:
        pl.semaphore_signal(barrier, inc=1, device_id={"chan": to}, device_id_type=MESH)
    inputs = []
    for t, (src, dst) in enumerate(
        ((obs_hbm, obs_v), (dec_hbm, dec_v), (win_hbm, win_v), (mats_hbm, full_v), (tabs_hbm, tabs_v))
    ):
        copy = pltpu.make_async_copy(src, dst, in_sem.at[t])
        copy.start()
        inputs.append(copy)
    inputs[0].wait()
    inputs[1].wait()

    frames = 512
    lane = lax.broadcasted_iota(jnp.int32, (32, frames), 1)
    row = lax.rem(lax.broadcasted_iota(jnp.int32, (32, frames), 0), 8)

    def shift(value, steps):
        return pltpu.roll(value, steps % frames, axis=value.ndim - 1)

    a = dec_v[...]
    gain = 1.0 - a
    data = [obs_v[0], obs_v[1]]
    prod = jnp.where(lane == 0, 0.0, a)
    run = [gain * d for d in data]
    step = 1
    while step < frames:
        run = [r + prod * shift(r, step) for r in run]
        prod = prod * shift(prod, step)
        step *= 2
    first = [d + 2.0 * r for d, r in zip(data, run)]
    prod = jnp.where(lane == frames - 1, 0.0, shift(a, -1))
    run = first
    step = 1
    while step < frames:
        run = [r + prod * shift(r, -step) for r in run]
        prod = prod * shift(prod, -step)
        step *= 2
    white = [f + 2.0 * gain * r for f, r in zip(first, run)]

    up = (row == 1) | (row == 3)
    down = (row == 4) | (row == 6)

    def flipped(value):
        return jnp.where(
            up,
            pltpu.roll(value, 29, axis=0),
            jnp.where(down, pltpu.roll(value, 3, axis=0), value),
        )

    def moved(value, offset):
        moved_value = shift(value, -offset)
        inside = (lane + offset >= 0) & (lane + offset < frames)
        return jnp.where(inside, moved_value, 0.0)

    white = [flipped(w) for w in white]
    af = flipped(a)
    packed = jnp.concatenate(
        [moved(white[0], -3), moved(white[1], -3), moved(white[0], 8), moved(white[1], 8)], axis=0
    )
    stage_o[...] = packed.T.reshape(GROUP, 16, 128)
    packed = jnp.concatenate([moved(af, 6 * t - 3) for t in range(4)], axis=0)
    stage_d[...] = packed.T.reshape(GROUP, 16, 128)[:, :8]

    pl.semaphore_wait(barrier, GROUP - 1)

    for stage, got, rows, send, recv in (
        (stage_d, got_d, 6, d_send, d_recv), (stage_o, got_o, 11, o_send, o_recv)
    ):
        for to in others:
            copy = pltpu.make_async_remote_copy(
                src_ref=stage.at[to, pl.ds(0, rows)], dst_ref=got.at[pl.ds(0, rows), me, :],
                send_sem=send, recv_sem=recv,
                device_id={"chan": to}, device_id_type=MESH,
            )
            copy.start()
    own = [
        pltpu.make_async_copy(stage_d.at[me, pl.ds(0, 6)], got_d.at[pl.ds(0, 6), me, :], own_sem.at[0]),
        pltpu.make_async_copy(stage_o.at[me, pl.ds(0, 11)], got_o.at[pl.ds(0, 11), me, :], own_sem.at[1]),
    ]
    for copy in own:
        copy.start()
    for copy in inputs[2:]:
        copy.wait()

    for which in range(2):
        full = full_v[which]
        high = full.astype(BF16)
        mats_v[which, 0:256] = high
        mats_v[which, 256:512] = high
        mats_v[which, 512:768] = (full - high.astype(F32)).astype(BF16)

    win = [
        jnp.concatenate([win_v[p : p + 1, n * 128 : (n + 1) * 128] for n in range(8)], axis=0)
        for p in range(4)
    ]

    def butterfly(value, distance):
        high = (lax.broadcasted_iota(jnp.int32, (8, 128), 0) & distance) != 0
        if distance == 4:
            other = pltpu.roll(value, 4, axis=1)
        else:
            other = jnp.where(
                high, pltpu.roll(value, distance, axis=1), pltpu.roll(value, 8 - distance, axis=1)
            )
        return other + value * jnp.where(high, -1.0, 1.0)

    def quarter(re, im, sign):
        index = lax.broadcasted_iota(jnp.int32, re.shape, 1)
        turned = (index & 3) == 3
        return jnp.where(turned, -sign * im, re), jnp.where(turned, sign * re, im)

    def times(re, im, c, s):
        return re * c - im * s, re * s + im * c

    def product(re, im, which):
        count = re.shape[0]
        x = jnp.concatenate([re.reshape(count * 8, 128), im.reshape(count * 8, 128)], axis=1)
        high = x.astype(BF16)
        low = (x - high.astype(F32)).astype(BF16)
        y = jnp.dot(
            jnp.concatenate([high, low, high], axis=1), mats_v[which], preferred_element_type=F32
        )
        return y[:, :128].reshape(count, 8, 128), y[:, 128:].reshape(count, 8, 128)

    def to_wave(re, im):
        re, im = product(re, im, 0)
        re, im = times(re, im, tabs_v[0], tabs_v[1])
        re, im = butterfly(re, 1), butterfly(im, 1)
        re, im = quarter(re, im, 1.0)
        re, im = butterfly(re, 2), butterfly(im, 2)
        re, im = times(re, im, tabs_v[2], tabs_v[3])
        return butterfly(re, 4), butterfly(im, 4)

    def to_spec(re, im):
        re, im = butterfly(re, 4), butterfly(im, 4)
        re, im = times(re, im, tabs_v[2], -tabs_v[3])
        re, im = butterfly(re, 2), butterfly(im, 2)
        re, im = quarter(re, im, -1.0)
        re, im = butterfly(re, 1), butterfly(im, 1)
        re, im = times(re, im, tabs_v[0], -tabs_v[1])
        return product(re, im, 1)

    def gather_taps(u, count):
        out = win[0] * u[0:count]
        for p in range(1, 4):
            out = out + win[p] * u[p : p + count]
        return out

    def spread_taps(v, count):
        out = win[0] * v[3 : 3 + count]
        for p in range(1, 4):
            out = out + win[p] * v[3 - p : 3 - p + count]
        return out

    def part_only(value):
        index = lax.broadcasted_iota(jnp.int32, value.shape, 0)
        return jnp.where((index < 3) & (me == 0), 0.0, value)

    def wait_for(ref, sem):
        pltpu.make_async_copy(ref, ref, sem).wait()

    own[0].wait()
    wait_for(got_d.at[pl.ds(0, 6), pl.ds(0, GROUP - 1)], d_recv)

    lane8 = lax.broadcasted_iota(jnp.int32, (8, 128), 1)
    low64 = lane8 < 64
    low32 = (lane8 & 32) == 0

    def exchange(v):
        y = [None] * 4
        for i in range(2):
            y[i] = jnp.where(low64, v[i], pltpu.roll(v[i + 2], 64, axis=1))
            y[i + 2] = jnp.where(low64, pltpu.roll(v[i], 64, axis=1), v[i + 2])
        z = [None] * 4
        for i in (0, 2):
            z[i] = jnp.where(low32, y[i], pltpu.roll(y[i + 1], 32, axis=1))
            z[i + 1] = jnp.where(low32, pltpu.roll(y[i], 96, axis=1), y[i + 1])
        return z

    for q in range(2):
        turned = got_d[4 * q : 4 * q + 4].reshape(128, 128).T
        for part in range(4):
            base = part * 32
            out = exchange([turned[base + 8 * i : base + 8 * i + 8] for i in range(4)])
            for r in range(min(4, 6 - 4 * q)):
                dec[6 * part + 4 * q + r] = out[r]

    def inverse(a):
        return jnp.where(a > 0.0, 1.0 / jnp.where(a > 0.0, a, 1.0), 0.0)

    def backward(e):
        g = {18: e[18]}
        for f in range(17, 2, -1):
            g[f] = e[f] + dec[f + 1] * g[f + 1]
        return g

    def backward_left(e, g):
        for f in (2, 1, 0):
            g[f] = e[f] + dec[f + 1] * g[f + 1]

    def backward_right(e, g):
        g[19] = jnp.zeros_like(g[18])
        for f in (20, 21):
            g[f] = (g[f - 1] - e[f - 1]) * inv[f]

    inv = {f: inverse(dec[f]) for f in (1, 2, 19, 20, 21)}
    twice = {f: 2.0 * (1.0 - dec[f]) for f in range(22)}
    prods = {2: jnp.ones((8, 128), F32), 1: inv[2], 0: inv[1] * inv[2]}
    for f in range(3, 22):
        prods[f] = dec[f] * prods[f - 1]
    from_c = {f: 2.0 * prods[f] for f in range(22)}
    back_c = backward(from_c)
    backward_left(from_c, back_c)
    backward_right(from_c, back_c)
    back_d = {18: jnp.ones((8, 128), F32), 19: inv[19]}
    for f in range(17, -1, -1):
        back_d[f] = dec[f + 1] * back_d[f + 1]
    for f in (20, 21):
        back_d[f] = back_d[f - 1] * inv[f]
    left_all = jnp.stack([from_c[f] + twice[f] * back_c[f] for f in range(22)])
    right_all = jnp.stack([twice[f] * back_d[f] for f in range(22)])
    cx[mx, 0:8] = prods[18]
    cx[mx, 8:16] = dec[3] * back_c[3]

    def x_copies(part, send, recv):
        out = []
        for t in range(1, NX):
            to = mz * NX + lax.rem(mx + t, NX)
            out.append(pltpu.make_async_remote_copy(
                src_ref=part, dst_ref=part, send_sem=send, recv_sem=recv,
                device_id={"chan": to}, device_id_type=MESH,
            ))
        for copy in out:
            copy.start()

    def z_copies(part, send, recv):
        out = []
        for t in (4, 3, 5, 2, 6, 1, 7):
            to = lax.rem(mz + t, NZ) * NX + mx
            out.append(pltpu.make_async_remote_copy(
                src_ref=part, dst_ref=part, send_sem=send, recv_sem=recv,
                device_id={"chan": to}, device_id_type=MESH,
            ))
        for copy in out:
            copy.start()

    x_copies(cx.at[mx], xc_send, xc_recv)

    own[1].wait()
    wait_for(got_o.at[pl.ds(0, 11), pl.ds(0, GROUP - 1)], o_recv)

    for q in range(3):
        turned = got_o[4 * q : 4 * q + 4].reshape(128, 128).T
        for half in range(2):
            for c in range(2):
                base = half * 64 + c * 32
                out = exchange([turned[base + 8 * i : base + 8 * i + 8] for i in range(4)])
                for r in range(min(4, 11 - 4 * q)):
                    spec[c, 11 * half + 4 * q + r] = out[r]

    def halo_copy(slot, x, first, to):
        for n in range(2):
            for f in range(3):
                out_halo[slot, n, f] = x[n][first + f]
        pltpu.make_async_remote_copy(
            src_ref=out_halo.at[slot], dst_ref=in_halo.at[slot], send_sem=h_send.at[slot], recv_sem=h_recv.at[slot],
            device_id={"chan": to}, device_id_type=MESH,
        ).start()

    def halo_frames(slot, outside):
        wait_for(in_halo.at[slot], h_recv.at[slot])
        wait_for(out_halo.at[slot], h_send.at[slot])
        return [
            jnp.where(outside, 0.0, jnp.stack([in_halo[slot, 0, f], in_halo[slot, 1, f]])) for f in range(3)
        ]

    def local_whiten(x):
        s = {2: jnp.zeros((2, 8, 128), F32)}
        e = {}
        for f in range(3, 19):
            own_x = jnp.stack([x[0][f - 3], x[1][f - 3]])
            s[f] = dec[f] * s[f - 1] + (1.0 - dec[f]) * own_x
            e[f] = own_x + 2.0 * s[f]
        return s, e, backward(e)

    def left_whiten(x, s, e, g):
        for f in (2, 1, 0):
            if f < 2:
                s[f] = (s[f + 1] - (1.0 - dec[f + 1]) * x[f + 1]) * inv[f + 1]
            e[f] = x[f] + 2.0 * s[f]
        backward_left(e, g)

    def right_whiten(x, s, e, g):
        for f in (19, 20, 21):
            s[f] = dec[f] * s[f - 1] + (1.0 - dec[f]) * x[f - 19]
            e[f] = x[f - 19] + 2.0 * s[f]
        backward_right(e, g)

    def whole(e, g, start):
        return [e[f] + twice[f] * g[f] for f in range(start, 22)]

    def chain(carry, back, left, right, a, k):
        count = len(left)
        cs = [carry]
        for n in range(count):
            cs.append(a[n] * cs[n] + left[n])
        ds = [None] * count
        d = back
        for n in range(count - 1, -1, -1):
            ds[n] = d
            d = a[n] * d + (right[n] + k[n] * cs[n])
        return cs, ds, d

    def pair(ref, base):
        return jnp.stack([ref[base : base + 8], ref[base + 8 : base + 16]])

    zero = jnp.zeros((2, 8, 128), F32)

    def row_sum(value):
        return jnp.sum(value, axis=0, keepdims=True)

    def write_pair(ref, base, value):
        ref[base : base + 8] = value[0]
        ref[base + 8 : base + 16] = value[1]

    def crossed(cs, right, k):
        total = jnp.zeros((8, 128), F32)
        for c, h, q in zip(cs, right, k):
            full = (4.0 * h + (2.0 * q) * c) * c
            total = total + full[0] + full[1]
        return row_sum(total)

    def group_coefficients():
        wait_for(cx.at[pl.ds(0, NX - 1)], xc_recv)
        a, k = [[cx[n, 8 * m : 8 * m + 8] for n in range(NX)] for m in range(2)]
        ga, gk = a[0], k[0]
        for n in range(1, NX):
            gk = gk + k[n] * (ga * ga)
            ga = a[n] * ga
        cz[mz, 0:8] = ga
        cz[mz, 8:16] = gk
        z_copies(cz.at[mz], zc_send, zc_recv)

    def carries(turn, x, row):
        s, e, g = local_whiten(x)
        xv = xb.at[turn, mx]
        write_pair(xv, 0, s[18])
        write_pair(xv, 16, dec[3] * g[3])
        square = sum(e[f] * e[f] for f in range(3, 19))
        xv[32:33] = row_sum(square[0] + square[1])
        xv[33:34] = row
        x_copies(xb.at[turn, mx, pl.ds(0, 34)], x_send.at[turn], x_recv.at[turn])
        if turn == 0:
            halo_copy(0, x, 13, lax.rem(me + 1, GROUP))
            halo_copy(1, x, 0, lax.rem(me + GROUP - 1, GROUP))
            group_coefficients()
        else:
            halo_copy(2, x, 0, lax.rem(me + GROUP - 1, GROUP))
        a, k = [[cx[n, 8 * m : 8 * m + 8] for n in range(NX)] for m in range(2)]
        if turn == 0:
            wait_for(stage_d.at[pl.ds(0, GROUP - 1), pl.ds(0, 6)], d_send)
            wait_for(stage_o.at[pl.ds(0, GROUP - 1), pl.ds(0, 11)], o_send)
            wait_for(cx.at[pl.ds(0, NX - 1)], xc_send)
        else:
            wait_for(cz.at[pl.ds(0, NZ - 1)], zc_send)
            wait_for(zb.at[0, pl.ds(0, NZ - 1), pl.ds(0, 34)], z_send.at[0])
        wait_for(xb.at[turn, pl.ds(0, NX - 1), pl.ds(0, 34)], x_recv.at[turn])
        left = [pair(xb.at[turn, n], 0) for n in range(NX)]
        right = [pair(xb.at[turn, n], 16) for n in range(NX)]
        cs, _, out = chain(zero, zero, left, right, a, k)
        zv = zb.at[turn, mz]
        write_pair(zv, 0, cs[NX])
        write_pair(zv, 16, out)
        zv[32:33] = crossed(cs[:NX], right, k) + sum(xb[turn, n, 32:33] for n in range(NX))
        zv[33:34] = sum(xb[turn, n, 33:34] for n in range(NX))
        z_copies(zb.at[turn, mz, pl.ds(0, 34)], z_send.at[turn], z_recv.at[turn])
        if turn == 0:
            left_whiten(halo_frames(0, me == 0), s, e, g)
        right_whiten(halo_frames(1 + turn, me == GROUP - 1), s, e, g)
        w = whole(e, g, 3 * turn)
        if turn == 0:
            wait_for(cz.at[pl.ds(0, NZ - 1)], zc_recv)
        za, zk = [[cz[n, 8 * m : 8 * m + 8] for n in range(NZ)] for m in range(2)]
        wait_for(xb.at[turn, pl.ds(0, NX - 1), pl.ds(0, 34)], x_send.at[turn])
        wait_for(zb.at[turn, pl.ds(0, NZ - 1), pl.ds(0, 34)], z_recv.at[turn])
        zleft = [pair(zb.at[turn, n], 0) for n in range(NZ)]
        zright = [pair(zb.at[turn, n], 16) for n in range(NZ)]
        zcs, zds, _ = chain(zero, zero, zleft, zright, za, zk)
        for n in range(NZ):
            carry_z[0, n] = zcs[n]
            carry_z[1, n] = zds[n]
        cs, ds, _ = chain(carry_z[0, mz], carry_z[1, mz], left, right, a, k)
        for n in range(NX):
            carry_x[0, n] = cs[n]
            carry_x[1, n] = ds[n]

        def sums():
            squares = crossed(zcs[:NZ], zright, zk) + sum(zb[turn, n, 32:33] for n in range(NZ))
            rows = sum(zb[turn, n, 33:34] for n in range(NZ))
            return jnp.sum(squares, axis=1, keepdims=True), jnp.sum(rows, axis=1, keepdims=True)

        return w, carry_x[0, mx], carry_x[1, mx], sums

    def corrected(w, left, right, c, d):
        re = jnp.stack([v[0] for v in w]) + left * c[0] + right * d[0]
        im = jnp.stack([v[1] for v in w]) + left * c[1] + right * d[1]
        return re, im

    def padded(re, im):
        fill = jnp.zeros((1, 8, 128), F32)
        return jnp.concatenate([re, fill]), jnp.concatenate([im, fill])

    def squares(value):
        return row_sum(jnp.sum(value[0] * value[0] + value[1] * value[1], axis=0))

    u = to_wave(spec[0], spec[1])
    r0 = [part_only(gather_taps(v, 19)) for v in u]
    x0 = to_spec(*[spread_taps(v, 16) for v in r0])
    mine_r0 = [v[3:] for v in r0]
    w, c, d, sums = carries(0, x0, squares(mine_r0))
    w = corrected(w, left_all, right_all, c, d)

    u = to_wave(*w)
    q1 = [part_only(gather_taps(v, 19) + RIDGE * r) for v, r in zip(u, r0)]
    x = to_spec(*[spread_taps(v, 16) for v in q1])
    energy, rr = sums()
    alpha = rr / (energy + RIDGE * rr)
    x1 = [b - alpha * v for b, v in zip(x0, x)]
    mine_q1 = [v[3:] for v in q1]
    r1 = [r - alpha * q for r, q in zip(mine_r0, mine_q1)]
    w, c, d, sums = carries(1, x1, squares(r1))
    w = corrected(w, left_all[3:], right_all[3:], c, d)

    u = to_wave(*padded(*w))
    n1 = [gather_taps(v, 16) + RIDGE * r for v, r in zip(u, r1)]
    energy, new = sums()
    beta = new / rr
    alpha_next = new / (energy + RIDGE * new - beta * new / alpha)
    share_ref[...] = jnp.broadcast_to(alpha_next, (8, 1024))
    for n in range(2):
        image = n1[n] + beta * mine_q1[n]
        base_ref[n] = ((alpha + alpha_next * beta) * mine_r0[n]).reshape(16, 1024)
        mid_ref[n] = r1[n].reshape(16, 1024)
        drop_ref[n] = (alpha_next * image).reshape(16, 1024)
    wait_for(zb.at[1, pl.ds(0, NZ - 1), pl.ds(0, 34)], z_send.at[1])


def body(observed, window, decays):
    mats, tabs = tables()
    any_space = pl.BlockSpec(memory_space=pltpu.HBM)
    vmem = pl.BlockSpec(memory_space=pltpu.VMEM)
    dma = pltpu.SemaphoreType.DMA
    out = jax.ShapeDtypeStruct((2, 16, 1024), F32)
    base, mid, drop, share = pl.pallas_call(
        kernel,
        out_shape=(out, out, out, jax.ShapeDtypeStruct((8, 1024), F32)),
        in_specs=[any_space] * 5,
        out_specs=(vmem,) * 4,
        scratch_shapes=[
            pltpu.VMEM((2, 32, 512), F32),
            pltpu.VMEM((4, 1024), F32),
            pltpu.VMEM((32, 512), F32),
            pltpu.VMEM((2, 256, 256), F32),
            pltpu.VMEM((4, 8, 128), F32),
            pltpu.VMEM((2, 768, 256), BF16),
            pltpu.VMEM((GROUP, 16, 128), F32),
            pltpu.VMEM((GROUP, 8, 128), F32),
            pltpu.VMEM((12, GROUP, 128), F32),
            pltpu.VMEM((8, GROUP, 128), F32),
            pltpu.VMEM((2, 22, 8, 128), F32),
            pltpu.VMEM((24, 8, 128), F32),
            pltpu.VMEM((2, NX, 2, 8, 128), F32),
            pltpu.VMEM((2, NZ, 2, 8, 128), F32),
            pltpu.VMEM((2, NX, 40, 128), F32),
            pltpu.VMEM((2, NZ, 40, 128), F32),
            pltpu.VMEM((NX, 16, 128), F32),
            pltpu.VMEM((NZ, 16, 128), F32),
            pltpu.VMEM((3, 2, 3, 8, 128), F32),
            pltpu.VMEM((3, 2, 3, 8, 128), F32),
            dma((5,)),
            dma((2,)),
            dma, dma, dma, dma, dma, dma, dma, dma,
            dma((2,)), dma((2,)), dma((2,)), dma((2,)),
            dma((3,)), dma((3,)),
        ],
        name="invert",
        compiler_params=pltpu.CompilerParams(
            collective_id=0, has_side_effects=True, vmem_limit_bytes=48 * 1024 * 1024
        ),
    )(*[pltpu.with_memory_space_constraint(v, pltpu.HBM) for v in (observed, window, decays, jnp.asarray(mats), jnp.asarray(tabs))])
    return base + share[:1] * mid, mid - drop


def solution(mesh):
    return jax.shard_map(
        body,
        mesh=mesh,
        in_specs=(P(None, "chan", "beam"), P(), P("chan", "beam")),
        out_specs=(P(None, ("beam", "chan"), None), P(None, ("beam", "chan"), None)),
        check_vma=False,
    )
```

```python
import functools
import math

import jax
import jax.numpy as jnp
import numpy as np
from jax import lax
from jax.experimental import pallas as pl
from jax.experimental.pallas import tpu as pltpu
from jax.sharding import PartitionSpec as P

MESH = pl.DeviceIdType.MESH
F32 = jnp.float32
BF16 = jnp.bfloat16
GROUP = 32
NX = 4
NZ = 8
RIDGE = 0.5
FLIP = (0, 4, 2, 6, 1, 5, 3, 7)


def tables():
    lane = np.arange(128)
    k2 = 4 * (lane % 32) + lane // 32
    n2 = np.arange(128)
    angle = 2.0 * np.pi * ((k2[:, None] * n2[None, :]) % 128) / 128.0
    cos, sin = np.cos(angle) / 32.0, np.sin(angle) / 32.0
    inverse = np.block([[cos, sin], [-sin, cos]])

    mats = np.stack([inverse, inverse.T]).astype(np.float32)
    turn = 2.0 * np.pi * np.array(FLIP)[:, None] * n2[None, :] / 1024.0
    eighth = 2.0 * np.pi * np.maximum(np.arange(8) - 4, 0) / 8.0
    eighth = np.broadcast_to(eighth[:, None], (8, 128))
    tabs = np.stack([np.cos(turn), np.sin(turn), np.cos(eighth), np.sin(eighth)])
    return mats, tabs.astype(np.float32)


def kernel(
    obs_hbm, win_hbm, dec_hbm, mats_hbm, tabs_hbm, base_ref, mid_ref, drop_ref, share_ref,
    obs_v, win_v, dec_v, full_v, tabs_v, mats_v, stage_o, stage_d, got_o, got_d,
    spec, dec, carry_x, xb, zb, cx, cz, out_halo, in_halo, in_dec,
    in_sem, own_sem, o_send, o_recv, d_send, d_recv, xc_send, xc_recv,
    zc_send, zc_recv, x_send, x_recv, z_send, z_recv,
    h_send, h_recv, hd_send, hd_recv,
):
    me = lax.axis_index("chan")
    mz = me // NX
    mx = lax.rem(me, NX)
    barrier = pltpu.get_barrier_semaphore()
    others = sorted(
        ((dz, dx) for dz in range(NZ) for dx in range(NX) if dz or dx),
        key=lambda o: -min(o[0], NZ - o[0]) - min(o[1], NX - o[1]),
    )
    others = [lax.rem(mz + dz, NZ) * NX + lax.rem(mx + dx, NX) for dz, dx in others]
    for to in others:
        pl.semaphore_signal(barrier, inc=1, device_id={"chan": to}, device_id_type=MESH)
    inputs = []
    for t, (src, dst) in enumerate(
        ((obs_hbm, obs_v), (dec_hbm, dec_v), (win_hbm, win_v), (mats_hbm, full_v), (tabs_hbm, tabs_v))
    ):
        copy = pltpu.make_async_copy(src, dst, in_sem.at[t])
        copy.start()
        inputs.append(copy)
    inputs[0].wait()
    inputs[1].wait()

    frames = 512
    lane = lax.broadcasted_iota(jnp.int32, (32, frames), 1)
    row = lax.rem(lax.broadcasted_iota(jnp.int32, (32, frames), 0), 8)

    def shift(value, steps):
        return pltpu.roll(value, steps % frames, axis=value.ndim - 1)

    a = dec_v[...]
    gain = 1.0 - a
    data = [obs_v[0], obs_v[1]]
    prod = jnp.where(lane == 0, 0.0, a)
    run = [gain * d for d in data]
    step = 1
    while step < frames:
        run = [r + prod * shift(r, step) for r in run]
        prod = prod * shift(prod, step)
        step *= 2
    first = [d + 2.0 * r for d, r in zip(data, run)]
    prod = jnp.where(lane == frames - 1, 0.0, shift(a, -1))
    run = first
    step = 1
    while step < frames:
        run = [r + prod * shift(r, -step) for r in run]
        prod = prod * shift(prod, -step)
        step *= 2
    white = [f + 2.0 * gain * r for f, r in zip(first, run)]

    up = (row == 1) | (row == 3)
    down = (row == 4) | (row == 6)

    def flipped(value):
        return jnp.where(
            up,
            pltpu.roll(value, 29, axis=0),
            jnp.where(down, pltpu.roll(value, 3, axis=0), value),
        )

    def moved(value, offset):
        moved_value = shift(value, -offset)
        inside = (lane + offset >= 0) & (lane + offset < frames)
        return jnp.where(inside, moved_value, 0.0)

    white = [flipped(w) for w in white]
    af = flipped(a)
    packed = jnp.concatenate(
        [moved(white[0], -3), moved(white[1], -3), moved(white[0], 8), moved(white[1], 8)], axis=0
    )
    stage_o[...] = packed.T.reshape(GROUP, 16, 128)
    packed = jnp.concatenate([moved(af, 4 * t) for t in range(4)], axis=0)
    stage_d[...] = packed.T.reshape(GROUP, 16, 128)[:, :8]

    pl.semaphore_wait(barrier, GROUP - 1)

    for stage, got, rows, send, recv in (
        (stage_d, got_d, 4, d_send, d_recv), (stage_o, got_o, 11, o_send, o_recv)
    ):
        for to in others:
            copy = pltpu.make_async_remote_copy(
                src_ref=stage.at[to, pl.ds(0, rows)], dst_ref=got.at[pl.ds(0, rows), me, :],
                send_sem=send, recv_sem=recv,
                device_id={"chan": to}, device_id_type=MESH,
            )
            copy.start()
    own = [
        pltpu.make_async_copy(stage_d.at[me, pl.ds(0, 4)], got_d.at[:, me, :], own_sem.at[0]),
        pltpu.make_async_copy(stage_o.at[me, pl.ds(0, 11)], got_o.at[pl.ds(0, 11), me, :], own_sem.at[1]),
    ]
    for copy in own:
        copy.start()
    for copy in inputs[2:]:
        copy.wait()

    for which in range(2):
        full = full_v[which]
        high = full.astype(BF16)
        mats_v[which, 0:256] = high
        mats_v[which, 256:512] = high
        mats_v[which, 512:768] = (full - high.astype(F32)).astype(BF16)

    win = [
        jnp.concatenate([win_v[p : p + 1, n * 128 : (n + 1) * 128] for n in range(8)], axis=0)
        for p in range(4)
    ]

    def butterfly(value, distance):
        high = (lax.broadcasted_iota(jnp.int32, (8, 128), 0) & distance) != 0
        if distance == 4:
            other = pltpu.roll(value, 4, axis=1)
        else:
            other = jnp.where(
                high, pltpu.roll(value, distance, axis=1), pltpu.roll(value, 8 - distance, axis=1)
            )
        return other + value * jnp.where(high, -1.0, 1.0)

    def quarter(re, im, sign):
        index = lax.broadcasted_iota(jnp.int32, re.shape, 1)
        turned = (index & 3) == 3
        return jnp.where(turned, -sign * im, re), jnp.where(turned, sign * re, im)

    def times(re, im, c, s):
        return re * c - im * s, re * s + im * c

    def product(re, im, which):
        count = re.shape[0]
        x = jnp.concatenate([re.reshape(count * 8, 128), im.reshape(count * 8, 128)], axis=1)
        high = x.astype(BF16)
        low = (x - high.astype(F32)).astype(BF16)
        y = jnp.dot(
            jnp.concatenate([high, low, high], axis=1), mats_v[which], preferred_element_type=F32
        )
        return y[:, :128].reshape(count, 8, 128), y[:, 128:].reshape(count, 8, 128)

    def to_wave(re, im):
        re, im = product(re, im, 0)
        re, im = times(re, im, tabs_v[0], tabs_v[1])
        re, im = butterfly(re, 1), butterfly(im, 1)
        re, im = quarter(re, im, 1.0)
        re, im = butterfly(re, 2), butterfly(im, 2)
        re, im = times(re, im, tabs_v[2], tabs_v[3])
        return butterfly(re, 4), butterfly(im, 4)

    def to_spec(re, im):
        re, im = butterfly(re, 4), butterfly(im, 4)
        re, im = times(re, im, tabs_v[2], -tabs_v[3])
        re, im = butterfly(re, 2), butterfly(im, 2)
        re, im = quarter(re, im, -1.0)
        re, im = butterfly(re, 1), butterfly(im, 1)
        re, im = times(re, im, tabs_v[0], -tabs_v[1])
        return product(re, im, 1)

    def gather_taps(u, count):
        out = win[0] * u[0:count]
        for p in range(1, 4):
            out = out + win[p] * u[p : p + count]
        return out

    def spread_taps(v, count):
        out = win[0] * v[3 : 3 + count]
        for p in range(1, 4):
            out = out + win[p] * v[3 - p : 3 - p + count]
        return out

    def part_only(value):
        index = lax.broadcasted_iota(jnp.int32, value.shape, 0)
        return jnp.where((index < 3) & (me == 0), 0.0, value)

    def wait_for(ref, sem):
        pltpu.make_async_copy(ref, ref, sem).wait()

    own[0].wait()
    wait_for(got_d.at[:, pl.ds(0, GROUP - 1)], d_recv)

    lane8 = lax.broadcasted_iota(jnp.int32, (8, 128), 1)
    low64 = lane8 < 64
    low32 = (lane8 & 32) == 0

    def exchange(v):
        y = [None] * 4
        for i in range(2):
            y[i] = jnp.where(low64, v[i], pltpu.roll(v[i + 2], 64, axis=1))
            y[i + 2] = jnp.where(low64, pltpu.roll(v[i], 64, axis=1), v[i + 2])
        z = [None] * 4
        for i in (0, 2):
            z[i] = jnp.where(low32, y[i], pltpu.roll(y[i + 1], 32, axis=1))
            z[i + 1] = jnp.where(low32, pltpu.roll(y[i], 96, axis=1), y[i + 1])
        return z

    turned = got_d[...].reshape(128, 128).T
    for part in range(4):
        base = part * 32
        out = exchange([turned[base + 8 * i : base + 8 * i + 8] for i in range(4)])
        for r in range(4):
            dec[3 + 4 * part + r] = out[r]

    def send_to(src, dst, send, recv, to):
        pltpu.make_async_remote_copy(
            src_ref=src, dst_ref=dst, send_sem=send, recv_sem=recv, device_id={"chan": to}, device_id_type=MESH,
        ).start()

    after = lax.rem(me + 1, GROUP)
    before = lax.rem(me + GROUP - 1, GROUP)

    def inverse(a):
        return jnp.where(a > 0.0, 1.0 / jnp.where(a > 0.0, a, 1.0), 0.0)

    def backward(e):
        g = {18: e[18]}
        for f in range(17, 2, -1):
            g[f] = e[f] + dec[f + 1] * g[f + 1]
        return g

    def backward_left(e, g):
        for f in (2, 1, 0):
            g[f] = e[f] + dec[f + 1] * g[f + 1]

    def backward_right(e, g):
        g[19] = jnp.zeros_like(g[18])
        for f in (20, 21):
            g[f] = (g[f - 1] - e[f - 1]) * inv[f]

    twice = {f: 2.0 * (1.0 - dec[f]) for f in range(3, 19)}
    prods = {2: jnp.ones((8, 128), F32)}
    for f in range(3, 19):
        prods[f] = dec[f] * prods[f - 1]
    from_c = {f: 2.0 * prods[f] for f in range(3, 19)}
    back_c = backward(from_c)
    back_d = {18: jnp.ones((8, 128), F32)}
    for f in range(17, 2, -1):
        back_d[f] = dec[f + 1] * back_d[f + 1]
    left = {f: from_c[f] + twice[f] * back_c[f] for f in range(3, 19)}
    right = {f: twice[f] * back_d[f] for f in range(3, 19)}
    inv = {}

    def halo_coefficients():
        for side in range(2):
            wait_for(in_dec.at[side], hd_recv.at[side])
            wait_for(in_dec.at[side], hd_send.at[side])
        for f in range(3):
            dec[f] = jnp.where(me == 0, 0.0, in_dec[0, f])
            dec[19 + f] = jnp.where(me == GROUP - 1, 0.0, in_dec[1, f])
        halo = (0, 1, 2, 19, 20, 21)
        for f in (1, 2, 19, 20, 21):
            inv[f] = inverse(dec[f])
        for f in halo:
            twice[f] = 2.0 * (1.0 - dec[f])
        prods[1] = inv[2]
        prods[0] = inv[1] * inv[2]
        for f in (19, 20, 21):
            prods[f] = dec[f] * prods[f - 1]
        for f in halo:
            from_c[f] = 2.0 * prods[f]
        backward_left(from_c, back_c)
        backward_right(from_c, back_c)
        for f in (2, 1, 0):
            back_d[f] = dec[f + 1] * back_d[f + 1]
        back_d[19] = inv[19]
        for f in (20, 21):
            back_d[f] = back_d[f - 1] * inv[f]
        for f in halo:
            left[f] = from_c[f] + twice[f] * back_c[f]
            right[f] = twice[f] * back_d[f]

    cx[mx, 0:8] = prods[18]
    cx[mx, 8:16] = dec[3] * back_c[3]

    def x_copies(part, send, recv):
        out = []
        for t in (2, 1, 3):
            to = mz * NX + lax.rem(mx + t, NX)
            out.append(pltpu.make_async_remote_copy(
                src_ref=part, dst_ref=part, send_sem=send, recv_sem=recv,
                device_id={"chan": to}, device_id_type=MESH,
            ))
        for copy in out:
            copy.start()

    def z_copies(part, send, recv):
        out = []
        for t in (4, 3, 5, 2, 6, 1, 7):
            to = lax.rem(mz + t, NZ) * NX + mx
            out.append(pltpu.make_async_remote_copy(
                src_ref=part, dst_ref=part, send_sem=send, recv_sem=recv,
                device_id={"chan": to}, device_id_type=MESH,
            ))
        for copy in out:
            copy.start()

    x_copies(cx.at[mx], xc_send, xc_recv)

    own[1].wait()
    wait_for(got_o.at[pl.ds(0, 11), pl.ds(0, GROUP - 1)], o_recv)

    for q in range(3):
        turned = got_o[4 * q : 4 * q + 4].reshape(128, 128).T
        for half in range(2):
            for c in range(2):
                base = half * 64 + c * 32
                out = exchange([turned[base + 8 * i : base + 8 * i + 8] for i in range(4)])
                for r in range(min(4, 11 - 4 * q)):
                    spec[c, 11 * half + 4 * q + r] = out[r]

    def halo_copy(slot, x, first, to):
        for n in range(2):
            for f in range(3):
                out_halo[slot, n, f] = x[n][first + f]
        send_to(out_halo.at[slot], in_halo.at[slot], h_send.at[slot], h_recv.at[slot], to)

    def halo_frames(slot, outside):
        wait_for(in_halo.at[slot], h_recv.at[slot])
        wait_for(out_halo.at[slot], h_send.at[slot])
        return [
            jnp.where(outside, 0.0, jnp.stack([in_halo[slot, 0, f], in_halo[slot, 1, f]])) for f in range(3)
        ]

    def local_sums(x):
        frames_x = {f: jnp.stack([x[0][f - 3], x[1][f - 3]]) for f in range(3, 19)}
        going_right = 0.5 * sum(right[f] * frames_x[f] for f in range(3, 19))
        going_left = 0.5 * sum(left[f] * frames_x[f] for f in range(3, 19))
        s = {2: jnp.zeros((2, 8, 128), F32)}
        e = {}
        for f in range(3, 19):
            s[f] = dec[f] * s[f - 1] + (1.0 - dec[f]) * frames_x[f]
            e[f] = frames_x[f] + 2.0 * s[f]
        return going_right, going_left, s, e

    def left_whiten(x, s, e, g):
        for f in (2, 1, 0):
            if f < 2:
                s[f] = (s[f + 1] - (1.0 - dec[f + 1]) * x[f + 1]) * inv[f + 1]
            e[f] = x[f] + 2.0 * s[f]
        backward_left(e, g)

    def right_whiten(x, s, e, g):
        for f in (19, 20, 21):
            s[f] = dec[f] * s[f - 1] + (1.0 - dec[f]) * x[f - 19]
            e[f] = x[f - 19] + 2.0 * s[f]
        backward_right(e, g)

    def whole(e, g, start):
        return [e[f] + twice[f] * g[f] for f in range(start, 22)]

    def chain(carry, back, left, right, a, k):
        count = len(left)
        cs = [carry]
        for n in range(count):
            cs.append(a[n] * cs[n] + left[n])
        ds = [None] * count
        d = back
        for n in range(count - 1, -1, -1):
            ds[n] = d
            d = a[n] * d + (right[n] + k[n] * cs[n])
        return cs, ds, d

    def pair(ref, base):
        return jnp.stack([ref[base : base + 8], ref[base + 8 : base + 16]])

    zero = jnp.zeros((2, 8, 128), F32)

    def row_sum(value):
        return jnp.sum(value, axis=0, keepdims=True)

    def write_pair(ref, base, value):
        ref[base : base + 8] = value[0]
        ref[base + 8 : base + 16] = value[1]

    def crossed(cs, right, k):
        total = jnp.zeros((8, 128), F32)
        for c, h, q in zip(cs, right, k):
            full = (4.0 * h + (2.0 * q) * c) * c
            total = total + full[0] + full[1]
        return row_sum(total)

    def group_coefficients():
        wait_for(cx.at[pl.ds(0, NX - 1)], xc_recv)
        a, k = [[cx[n, 8 * m : 8 * m + 8] for n in range(NX)] for m in range(2)]
        ga, gk = a[0], k[0]
        for n in range(1, NX):
            gk = gk + k[n] * (ga * ga)
            ga = a[n] * ga
        cz[mz, 0:8] = ga
        cz[mz, 8:16] = gk
        z_copies(cz.at[mz], zc_send, zc_recv)

    def own_of(ref, values, index):
        for n, value in enumerate(values):
            ref[n] = value
        return ref[index]

    def ahead_weights(a, k):
        one = jnp.ones((8, 128), F32)
        none = jnp.zeros((8, 128), F32)
        wc, wh, wd = [none] * NZ, [none] * NZ, [none] * NZ
        run = one
        for n in range(NZ - 1, -1, -1):
            wc[n] = jnp.where(n < mz, run, none)
            run = jnp.where(n < mz, run * a[n], run)
        run = one
        for n in range(NZ):
            wh[n] = jnp.where(n > mz, run, none)
            run = jnp.where(n > mz, run * a[n], run)
        through = none
        of_c = none
        for n in range(NZ - 1, -1, -1):
            if n < NZ - 1:
                through = wh[n + 1] * k[n + 1] + a[n + 1] * through
            wd[n] = jnp.where(n < mz, none, through)
            of_c = jnp.where(n == mz, a[n] * through, of_c)
        for n in range(NZ):
            wd[n] = wd[n] + of_c * wc[n]
        return wc, wh, wd

    saved = {}

    def carries(turn, x, row):
        going_right, going_left, s, e = local_sums(x)
        xv = xb.at[turn, mx]
        write_pair(xv, 0, going_right)
        write_pair(xv, 16, going_left)
        square = sum(e[f] * e[f] for f in range(3, 19))
        xv[32:33] = row_sum(square[0] + square[1])
        xv[33:34] = row
        x_copies(xb.at[turn, mx, pl.ds(0, 34)], x_send.at[turn], x_recv.at[turn])
        if turn == 0:
            halo_copy(0, x, 13, after)
            halo_copy(1, x, 0, before)
            send_to(dec.at[pl.ds(16, 3)], in_dec.at[0], hd_send.at[0], hd_recv.at[0], after)
            send_to(dec.at[pl.ds(3, 3)], in_dec.at[1], hd_send.at[1], hd_recv.at[1], before)
            group_coefficients()
        else:
            halo_copy(2, x, 0, before)
        g = backward(e)
        a, k = [[cx[n, 8 * m : 8 * m + 8] for n in range(NX)] for m in range(2)]
        if turn == 0:
            wait_for(stage_d.at[pl.ds(0, GROUP - 1), pl.ds(0, 4)], d_send)
            wait_for(stage_o.at[pl.ds(0, GROUP - 1), pl.ds(0, 11)], o_send)
            wait_for(cx.at[pl.ds(0, NX - 1)], xc_send)
        else:
            wait_for(cz.at[pl.ds(0, NZ - 1)], zc_send)
            wait_for(zb.at[0, pl.ds(0, NZ - 1), pl.ds(0, 34)], z_send.at[0])
        wait_for(xb.at[turn, pl.ds(0, NX - 1), pl.ds(0, 34)], x_recv.at[turn])
        lefts = [pair(xb.at[turn, n], 0) for n in range(NX)]
        rights = [pair(xb.at[turn, n], 16) for n in range(NX)]
        cs, ds, out = chain(zero, zero, lefts, rights, a, k)
        zv = zb.at[turn, mz]
        write_pair(zv, 0, cs[NX])
        write_pair(zv, 16, out)
        zv[32:33] = crossed(cs[:NX], rights, k) + sum(xb[turn, n, 32:33] for n in range(NX))
        zv[33:34] = sum(xb[turn, n, 33:34] for n in range(NX))
        z_copies(zb.at[turn, mz, pl.ds(0, 34)], z_send.at[turn], z_recv.at[turn])
        c_own = own_of(carry_x.at[0], cs[:NX], mx)
        d_own = own_of(carry_x.at[1], ds, mx)
        if turn == 0:
            one = jnp.ones((2, 8, 128), F32)
            quiet = [zero] * NX
            from_left, back_left, _ = chain(one, zero, quiet, quiet, a, k)
            _, back_right, _ = chain(zero, one, quiet, quiet, a, k)
            pass_c = own_of(carry_x.at[2], from_left[:NX], mx)[0]
            turn_c = own_of(carry_x.at[3], back_left, mx)[0]
            pass_d = own_of(carry_x.at[4], back_right, mx)[0]
            halo_coefficients()
            left_whiten(halo_frames(0, me == 0), s, e, g)
            wait_for(cz.at[pl.ds(0, NZ - 1)], zc_recv)
            za, zk = [[cz[n, 8 * m : 8 * m + 8] for n in range(NZ)] for m in range(2)]
            wc, wh, wd = ahead_weights(za, zk)
            saved["z"] = za, zk
            saved["c"] = [pass_c * w for w in wc]
            saved["h"] = [pass_d * w for w in wh]
            saved["l"] = [pass_d * v + turn_c * w for v, w in zip(wd, wc)]
        za, zk = saved["z"]
        right_whiten(halo_frames(1 + turn, me == GROUP - 1), s, e, g)
        w = whole(e, g, 3 * turn)
        wait_for(xb.at[turn, pl.ds(0, NX - 1), pl.ds(0, 34)], x_send.at[turn])
        wait_for(zb.at[turn, pl.ds(0, NZ - 1), pl.ds(0, 34)], z_recv.at[turn])
        zleft = [pair(zb.at[turn, n], 0) for n in range(NZ)]
        zright = [pair(zb.at[turn, n], 16) for n in range(NZ)]
        c = c_own + sum(v * z for v, z in zip(saved["c"], zleft))
        d = d_own + sum(v * z for v, z in zip(saved["h"], zright)) + sum(v * z for v, z in zip(saved["l"], zleft))

        def sums():
            zcs = [zero]
            for n in range(NZ - 1):
                zcs.append(za[n] * zcs[n] + zleft[n])
            squares = crossed(zcs, zright, zk) + sum(zb[turn, n, 32:33] for n in range(NZ))
            rows = sum(zb[turn, n, 33:34] for n in range(NZ))
            return jnp.sum(squares, axis=1, keepdims=True), jnp.sum(rows, axis=1, keepdims=True)

        return w, c, d, sums

    def corrected(w, start, c, d):
        out = [v + left[f] * c + right[f] * d for f, v in zip(range(start, 22), w)]
        return jnp.stack([v[0] for v in out]), jnp.stack([v[1] for v in out])

    def padded(re, im):
        fill = jnp.zeros((1, 8, 128), F32)
        return jnp.concatenate([re, fill]), jnp.concatenate([im, fill])

    def squares(value):
        return row_sum(jnp.sum(value[0] * value[0] + value[1] * value[1], axis=0))

    u = to_wave(spec[0], spec[1])
    r0 = [part_only(gather_taps(v, 19)) for v in u]
    x0 = to_spec(*[spread_taps(v, 16) for v in r0])
    mine_r0 = [v[3:] for v in r0]
    w, c, d, sums = carries(0, x0, squares(mine_r0))
    w = corrected(w, 0, c, d)

    u = to_wave(*w)
    q1 = [part_only(gather_taps(v, 19) + RIDGE * r) for v, r in zip(u, r0)]
    x = to_spec(*[spread_taps(v, 16) for v in q1])
    energy, rr = sums()
    alpha = rr / (energy + RIDGE * rr)
    x1 = [b - alpha * v for b, v in zip(x0, x)]
    mine_q1 = [v[3:] for v in q1]
    r1 = [r - alpha * q for r, q in zip(mine_r0, mine_q1)]
    w, c, d, sums = carries(1, x1, squares(r1))
    w = corrected(w, 3, c, d)

    u = to_wave(*padded(*w))
    n1 = [gather_taps(v, 16) + RIDGE * r for v, r in zip(u, r1)]
    energy, new = sums()
    beta = new / rr
    alpha_next = new / (energy + RIDGE * new - beta * new / alpha)
    share_ref[...] = jnp.broadcast_to(alpha_next, (8, 1024))
    for n in range(2):
        image = n1[n] + beta * mine_q1[n]
        base_ref[n] = ((alpha + alpha_next * beta) * mine_r0[n]).reshape(16, 1024)
        mid_ref[n] = r1[n].reshape(16, 1024)
        drop_ref[n] = (alpha_next * image).reshape(16, 1024)
    wait_for(zb.at[1, pl.ds(0, NZ - 1), pl.ds(0, 34)], z_send.at[1])


def body(observed, window, decays):
    mats, tabs = tables()
    any_space = pl.BlockSpec(memory_space=pltpu.HBM)
    vmem = pl.BlockSpec(memory_space=pltpu.VMEM)
    dma = pltpu.SemaphoreType.DMA
    out = jax.ShapeDtypeStruct((2, 16, 1024), F32)
    base, mid, drop, share = pl.pallas_call(
        kernel,
        out_shape=(out, out, out, jax.ShapeDtypeStruct((8, 1024), F32)),
        in_specs=[any_space] * 5,
        out_specs=(vmem,) * 4,
        scratch_shapes=[
            pltpu.VMEM((2, 32, 512), F32),
            pltpu.VMEM((4, 1024), F32),
            pltpu.VMEM((32, 512), F32),
            pltpu.VMEM((2, 256, 256), F32),
            pltpu.VMEM((4, 8, 128), F32),
            pltpu.VMEM((2, 768, 256), BF16),
            pltpu.VMEM((GROUP, 16, 128), F32),
            pltpu.VMEM((GROUP, 8, 128), F32),
            pltpu.VMEM((12, GROUP, 128), F32),
            pltpu.VMEM((4, GROUP, 128), F32),
            pltpu.VMEM((2, 22, 8, 128), F32),
            pltpu.VMEM((24, 8, 128), F32),
            pltpu.VMEM((5, NX, 2, 8, 128), F32),
            pltpu.VMEM((2, NX, 40, 128), F32),
            pltpu.VMEM((2, NZ, 40, 128), F32),
            pltpu.VMEM((NX, 16, 128), F32),
            pltpu.VMEM((NZ, 16, 128), F32),
            pltpu.VMEM((3, 2, 3, 8, 128), F32),
            pltpu.VMEM((3, 2, 3, 8, 128), F32),
            pltpu.VMEM((2, 3, 8, 128), F32),
            dma((5,)),
            dma((2,)),
            dma, dma, dma, dma, dma, dma, dma, dma,
            dma((2,)), dma((2,)), dma((2,)), dma((2,)),
            dma((3,)), dma((3,)),
            dma((2,)), dma((2,)),
        ],
        name="invert",
        compiler_params=pltpu.CompilerParams(
            collective_id=0, has_side_effects=True, vmem_limit_bytes=48 * 1024 * 1024
        ),
    )(*[pltpu.with_memory_space_constraint(v, pltpu.HBM) for v in (observed, window, decays, jnp.asarray(mats), jnp.asarray(tabs))])
    return base + share[:1] * mid, mid - drop


def solution(mesh):
    return jax.shard_map(
        body,
        mesh=mesh,
        in_specs=(P(None, "chan", "beam"), P(), P("chan", "beam")),
        out_specs=(P(None, ("beam", "chan"), None), P(None, ("beam", "chan"), None)),
        check_vma=False,
    )
```

```python
import functools
import math

import jax
import jax.numpy as jnp
import numpy as np
from jax import lax
from jax.experimental import pallas as pl
from jax.experimental.pallas import tpu as pltpu
from jax.sharding import PartitionSpec as P

MESH = pl.DeviceIdType.MESH
F32 = jnp.float32
BF16 = jnp.bfloat16
GROUP = 32
NX = 4
NZ = 8
RIDGE = 0.5
FLIP = (0, 4, 2, 6, 1, 5, 3, 7)


def tables():
    lane = np.arange(128)
    k2 = 4 * (lane % 32) + lane // 32
    n2 = np.arange(128)
    angle = 2.0 * np.pi * ((k2[:, None] * n2[None, :]) % 128) / 128.0
    cos, sin = np.cos(angle) / 32.0, np.sin(angle) / 32.0
    inverse = np.block([[cos, sin], [-sin, cos]])

    mats = np.stack([inverse, inverse.T]).astype(np.float32)
    turn = 2.0 * np.pi * np.array(FLIP)[:, None] * n2[None, :] / 1024.0
    eighth = 2.0 * np.pi * np.maximum(np.arange(8) - 4, 0) / 8.0
    eighth = np.broadcast_to(eighth[:, None], (8, 128))
    tabs = np.stack([np.cos(turn), np.sin(turn), np.cos(eighth), np.sin(eighth)])
    return mats, tabs.astype(np.float32)


def kernel(
    obs_hbm, win_hbm, dec_hbm, mats_hbm, tabs_hbm, base_ref, mid_ref, drop_ref, share_ref,
    obs_v, win_v, dec_v, full_v, tabs_v, mats_v, stage_o, stage_d, got_o, got_d,
    spec, dec, carry_x, xb, zb, cx, cz, out_halo, in_halo,
    in_sem, own_sem, o_send, o_recv, d_send, d_recv, xc_send, xc_recv,
    zc_send, zc_recv, x_send, x_recv, z_send, z_recv,
    h_send, h_recv,
):
    me = lax.axis_index("chan")
    mz = me // NX
    mx = lax.rem(me, NX)
    barrier = pltpu.get_barrier_semaphore()
    others = sorted(
        ((dz, dx) for dz in range(NZ) for dx in range(NX) if dz or dx),
        key=lambda o: -min(o[0], NZ - o[0]) - min(o[1], NX - o[1]),
    )
    inputs = []
    for t, (src, dst) in enumerate(
        ((obs_hbm, obs_v), (dec_hbm, dec_v), (win_hbm, win_v), (mats_hbm, full_v), (tabs_hbm, tabs_v))
    ):
        copy = pltpu.make_async_copy(src, dst, in_sem.at[t])
        copy.start()
        inputs.append(copy)
    others = [lax.rem(mz + dz, NZ) * NX + lax.rem(mx + dx, NX) for dz, dx in others]
    for to in others:
        pl.semaphore_signal(barrier, inc=1, device_id={"chan": to}, device_id_type=MESH)
    inputs[0].wait()
    inputs[1].wait()

    frames = 512
    lane = lax.broadcasted_iota(jnp.int32, (32, frames), 1)
    row = lax.rem(lax.broadcasted_iota(jnp.int32, (32, frames), 0), 8)

    def shift(value, steps):
        return pltpu.roll(value, steps % frames, axis=value.ndim - 1)

    a = dec_v[...]
    gain = 1.0 - a
    data = [obs_v[0], obs_v[1]]
    prod = jnp.where(lane == 0, 0.0, a)
    run = [gain * d for d in data]
    step = 1
    while step < frames:
        run = [r + prod * shift(r, step) for r in run]
        prod = prod * shift(prod, step)
        step *= 2
    first = [d + 2.0 * r for d, r in zip(data, run)]
    prod = jnp.where(lane == frames - 1, 0.0, shift(a, -1))
    run = first
    step = 1
    while step < frames:
        run = [r + prod * shift(r, -step) for r in run]
        prod = prod * shift(prod, -step)
        step *= 2
    white = [f + 2.0 * gain * r for f, r in zip(first, run)]

    up = (row == 1) | (row == 3)
    down = (row == 4) | (row == 6)

    def flipped(value):
        return jnp.where(
            up,
            pltpu.roll(value, 29, axis=0),
            jnp.where(down, pltpu.roll(value, 3, axis=0), value),
        )

    def moved(value, offset):
        moved_value = shift(value, -offset)
        inside = (lane + offset >= 0) & (lane + offset < frames)
        return jnp.where(inside, moved_value, 0.0)

    white = [flipped(w) for w in white]
    af = flipped(a)
    packed = jnp.concatenate(
        [moved(white[0], -3), moved(white[1], -3), moved(white[0], 8), moved(white[1], 8)], axis=0
    )
    stage_o[...] = packed.T.reshape(GROUP, 16, 128)
    packed = jnp.concatenate([moved(af, 4 * t) for t in range(4)], axis=0)
    stage_d[...] = packed.T.reshape(GROUP, 16, 128)[:, :8]

    own = [
        pltpu.make_async_copy(stage_d.at[me, pl.ds(0, 4)], got_d.at[:, me, :], own_sem.at[0]),
        pltpu.make_async_copy(stage_o.at[me, pl.ds(0, 11)], got_o.at[pl.ds(0, 11), me, :], own_sem.at[1]),
    ]
    for copy in own:
        copy.start()

    pl.semaphore_wait(barrier, GROUP - 1)

    for stage, got, rows, send, recv in (
        (stage_d, got_d, 4, d_send, d_recv), (stage_o, got_o, 11, o_send, o_recv)
    ):
        for to in others:
            copy = pltpu.make_async_remote_copy(
                src_ref=stage.at[to, pl.ds(0, rows)], dst_ref=got.at[pl.ds(0, rows), me, :],
                send_sem=send, recv_sem=recv,
                device_id={"chan": to}, device_id_type=MESH,
            )
            copy.start()
    for copy in inputs[2:]:
        copy.wait()

    for which in range(2):
        full = full_v[which]
        high = full.astype(BF16)
        mats_v[which, 0:256] = high
        mats_v[which, 256:512] = high
        mats_v[which, 512:768] = (full - high.astype(F32)).astype(BF16)

    win = [
        jnp.concatenate([win_v[p : p + 1, n * 128 : (n + 1) * 128] for n in range(8)], axis=0)
        for p in range(4)
    ]

    def butterfly(value, distance):
        high = (lax.broadcasted_iota(jnp.int32, (8, 128), 0) & distance) != 0
        if distance == 4:
            other = pltpu.roll(value, 4, axis=1)
        else:
            other = jnp.where(
                high, pltpu.roll(value, distance, axis=1), pltpu.roll(value, 8 - distance, axis=1)
            )
        return other + value * jnp.where(high, -1.0, 1.0)

    def quarter(re, im, sign):
        index = lax.broadcasted_iota(jnp.int32, re.shape, 1)
        turned = (index & 3) == 3
        return jnp.where(turned, -sign * im, re), jnp.where(turned, sign * re, im)

    def times(re, im, c, s):
        return re * c - im * s, re * s + im * c

    def product(re, im, which):
        count = re.shape[0]
        x = jnp.concatenate([re.reshape(count * 8, 128), im.reshape(count * 8, 128)], axis=1)
        high = x.astype(BF16)
        low = (x - high.astype(F32)).astype(BF16)
        y = jnp.dot(
            jnp.concatenate([high, low, high], axis=1), mats_v[which], preferred_element_type=F32
        )
        return y[:, :128].reshape(count, 8, 128), y[:, 128:].reshape(count, 8, 128)

    def to_wave(re, im):
        re, im = product(re, im, 0)
        re, im = times(re, im, tabs_v[0], tabs_v[1])
        re, im = butterfly(re, 1), butterfly(im, 1)
        re, im = quarter(re, im, 1.0)
        re, im = butterfly(re, 2), butterfly(im, 2)
        re, im = times(re, im, tabs_v[2], tabs_v[3])
        return butterfly(re, 4), butterfly(im, 4)

    def to_spec(re, im):
        re, im = butterfly(re, 4), butterfly(im, 4)
        re, im = times(re, im, tabs_v[2], -tabs_v[3])
        re, im = butterfly(re, 2), butterfly(im, 2)
        re, im = quarter(re, im, -1.0)
        re, im = butterfly(re, 1), butterfly(im, 1)
        re, im = times(re, im, tabs_v[0], -tabs_v[1])
        return product(re, im, 1)

    def gather_taps(u, count):
        out = win[0] * u[0:count]
        for p in range(1, 4):
            out = out + win[p] * u[p : p + count]
        return out

    def spread_taps(v, count):
        out = win[0] * v[3 : 3 + count]
        for p in range(1, 4):
            out = out + win[p] * v[3 - p : 3 - p + count]
        return out

    def part_only(value):
        index = lax.broadcasted_iota(jnp.int32, value.shape, 0)
        return jnp.where((index < 3) & (me == 0), 0.0, value)

    def wait_for(ref, sem):
        pltpu.make_async_copy(ref, ref, sem).wait()

    own[0].wait()
    wait_for(got_d.at[:, pl.ds(0, GROUP - 1)], d_recv)

    lane8 = lax.broadcasted_iota(jnp.int32, (8, 128), 1)
    low64 = lane8 < 64
    low32 = (lane8 & 32) == 0

    def exchange(v):
        y = [None] * 4
        for i in range(2):
            y[i] = jnp.where(low64, v[i], pltpu.roll(v[i + 2], 64, axis=1))
            y[i + 2] = jnp.where(low64, pltpu.roll(v[i], 64, axis=1), v[i + 2])
        z = [None] * 4
        for i in (0, 2):
            z[i] = jnp.where(low32, y[i], pltpu.roll(y[i + 1], 32, axis=1))
            z[i + 1] = jnp.where(low32, pltpu.roll(y[i], 96, axis=1), y[i + 1])
        return z

    turned = got_d[...].reshape(128, 128).T
    for part in range(4):
        base = part * 32
        out = exchange([turned[base + 8 * i : base + 8 * i + 8] for i in range(4)])
        for r in range(4):
            dec[3 + 4 * part + r] = out[r]

    def send_to(src, dst, send, recv, to):
        pltpu.make_async_remote_copy(
            src_ref=src, dst_ref=dst, send_sem=send, recv_sem=recv, device_id={"chan": to}, device_id_type=MESH,
        ).start()

    after = lax.rem(me + 1, GROUP)
    before = lax.rem(me + GROUP - 1, GROUP)

    def inverse(a):
        return jnp.where(a > 0.0, 1.0 / jnp.where(a > 0.0, a, 1.0), 0.0)

    def backward(e):
        g = {18: e[18]}
        for f in range(17, 2, -1):
            g[f] = e[f] + dec[f + 1] * g[f + 1]
        return g

    def backward_left(e, g):
        for f in (2, 1, 0):
            g[f] = e[f] + dec[f + 1] * g[f + 1]

    def backward_right(e, g):
        g[19] = jnp.zeros_like(g[18])
        for f in (20, 21):
            g[f] = (g[f - 1] - e[f - 1]) * inv[f]

    twice = {f: 2.0 * (1.0 - dec[f]) for f in range(3, 19)}
    prods = {2: jnp.ones((8, 128), F32)}
    for f in range(3, 19):
        prods[f] = dec[f] * prods[f - 1]
    from_c = {f: 2.0 * prods[f] for f in range(3, 19)}
    back_c = backward(from_c)
    back_d, left, right, inv = {18: jnp.ones((8, 128), F32)}, {}, {}, {}

    def halo_coefficients():
        for f in range(3):
            dec[f] = jnp.where(me == 0, 0.0, in_halo[0, 2, f])
            dec[19 + f] = jnp.where(me == GROUP - 1, 0.0, in_halo[1, 2, f])
        halo = (0, 1, 2, 19, 20, 21)
        for f in (1, 2, 19, 20, 21):
            inv[f] = inverse(dec[f])
        for f in halo:
            twice[f] = 2.0 * (1.0 - dec[f])
        prods[1] = inv[2]
        prods[0] = inv[1] * inv[2]
        for f in (19, 20, 21):
            prods[f] = dec[f] * prods[f - 1]
        for f in halo:
            from_c[f] = 2.0 * prods[f]
        backward_left(from_c, back_c)
        backward_right(from_c, back_c)
        for f in (2, 1, 0):
            back_d[f] = dec[f + 1] * back_d[f + 1]
        back_d[19] = inv[19]
        for f in (20, 21):
            back_d[f] = back_d[f - 1] * inv[f]
        for f in halo:
            left[f] = from_c[f] + twice[f] * back_c[f]
            right[f] = twice[f] * back_d[f]

    cx[mx, 0:8] = prods[18]
    cx[mx, 8:16] = dec[3] * back_c[3]

    def x_copies(part, send, recv):
        out = []
        for t in (2, 1, 3):
            to = mz * NX + lax.rem(mx + t, NX)
            out.append(pltpu.make_async_remote_copy(
                src_ref=part, dst_ref=part, send_sem=send, recv_sem=recv,
                device_id={"chan": to}, device_id_type=MESH,
            ))
        for copy in out:
            copy.start()

    def z_copies(part, send, recv):
        out = []
        for t in (4, 3, 5, 2, 6, 1, 7):
            to = lax.rem(mz + t, NZ) * NX + mx
            out.append(pltpu.make_async_remote_copy(
                src_ref=part, dst_ref=part, send_sem=send, recv_sem=recv,
                device_id={"chan": to}, device_id_type=MESH,
            ))
        for copy in out:
            copy.start()

    x_copies(cx.at[mx], xc_send, xc_recv)

    own[1].wait()
    wait_for(got_o.at[pl.ds(0, 11), pl.ds(0, GROUP - 1)], o_recv)

    for f in range(17, 2, -1):
        back_d[f] = dec[f + 1] * back_d[f + 1]
    for f in range(3, 19):
        left[f] = from_c[f] + twice[f] * back_c[f]
        right[f] = twice[f] * back_d[f]

    for q in range(3):
        turned = got_o[4 * q : 4 * q + 4].reshape(128, 128).T
        for half in range(2):
            for c in range(2):
                base = half * 64 + c * 32
                out = exchange([turned[base + 8 * i : base + 8 * i + 8] for i in range(4)])
                for r in range(min(4, 11 - 4 * q)):
                    spec[c, 11 * half + 4 * q + r] = out[r]

    def halo_copy(slot, x, first, to):
        planes = 3 if slot < 2 else 2
        for f in range(3):
            out_halo[slot, 0, f] = x[0][first + f]
            out_halo[slot, 1, f] = x[1][first + f]
            if planes == 3:
                out_halo[slot, 2, f] = dec[3 + first + f]
        part = (slot, pl.ds(0, planes))
        send_to(out_halo.at[part], in_halo.at[part], h_send.at[slot], h_recv.at[slot], to)

    def halo_wait(slot):
        part = (slot, pl.ds(0, 3 if slot < 2 else 2))
        wait_for(in_halo.at[part], h_recv.at[slot])
        wait_for(out_halo.at[part], h_send.at[slot])

    def halo_frames(slot, outside):
        return [
            jnp.where(outside, 0.0, jnp.stack([in_halo[slot, 0, f], in_halo[slot, 1, f]])) for f in range(3)
        ]

    def local_sums(x):
        frames_x = {f: jnp.stack([x[0][f - 3], x[1][f - 3]]) for f in range(3, 19)}
        going_right = 0.5 * sum(right[f] * frames_x[f] for f in range(3, 19))
        going_left = 0.5 * sum(left[f] * frames_x[f] for f in range(3, 19))
        s = {2: jnp.zeros((2, 8, 128), F32)}
        e = {}
        for f in range(3, 19):
            s[f] = dec[f] * s[f - 1] + (1.0 - dec[f]) * frames_x[f]
            e[f] = frames_x[f] + 2.0 * s[f]
        return going_right, going_left, s, e

    def left_whiten(x, s, e, g):
        for f in (2, 1, 0):
            if f < 2:
                s[f] = (s[f + 1] - (1.0 - dec[f + 1]) * x[f + 1]) * inv[f + 1]
            e[f] = x[f] + 2.0 * s[f]
        backward_left(e, g)

    def right_whiten(x, s, e, g):
        for f in (19, 20, 21):
            s[f] = dec[f] * s[f - 1] + (1.0 - dec[f]) * x[f - 19]
            e[f] = x[f - 19] + 2.0 * s[f]
        backward_right(e, g)

    def whole(e, g, start):
        return [e[f] + twice[f] * g[f] for f in range(start, 22)]

    def chain(carry, back, left, right, a, k):
        count = len(left)
        cs = [carry]
        for n in range(count):
            cs.append(a[n] * cs[n] + left[n])
        ds = [None] * count
        d = back
        for n in range(count - 1, -1, -1):
            ds[n] = d
            d = a[n] * d + (right[n] + k[n] * cs[n])
        return cs, ds, d

    def pair(ref, base):
        return jnp.stack([ref[base : base + 8], ref[base + 8 : base + 16]])

    zero = jnp.zeros((2, 8, 128), F32)

    def row_sum(value):
        return jnp.sum(value, axis=0, keepdims=True)

    def write_pair(ref, base, value):
        ref[base : base + 8] = value[0]
        ref[base + 8 : base + 16] = value[1]

    def crossed(cs, right, k):
        total = jnp.zeros((8, 128), F32)
        for c, h, q in zip(cs, right, k):
            full = (4.0 * h + (2.0 * q) * c) * c
            total = total + full[0] + full[1]
        return row_sum(total)

    def group_coefficients():
        wait_for(cx.at[pl.ds(0, NX - 1)], xc_recv)
        a, k = [[cx[n, 8 * m : 8 * m + 8] for n in range(NX)] for m in range(2)]
        ga, gk = a[0], k[0]
        for n in range(1, NX):
            gk = gk + k[n] * (ga * ga)
            ga = a[n] * ga
        cz[mz, 0:8] = ga
        cz[mz, 8:16] = gk
        z_copies(cz.at[mz], zc_send, zc_recv)

    def own_of(ref, values, index):
        for n, value in enumerate(values):
            ref[n] = value
        return ref[index]

    def ahead_weights(a, k):
        one = jnp.ones((8, 128), F32)
        none = jnp.zeros((8, 128), F32)
        wc, wh, wd = [none] * NZ, [none] * NZ, [none] * NZ
        run = one
        for n in range(NZ - 1, -1, -1):
            wc[n] = jnp.where(n < mz, run, none)
            run = jnp.where(n < mz, run * a[n], run)
        run = one
        for n in range(NZ):
            wh[n] = jnp.where(n > mz, run, none)
            run = jnp.where(n > mz, run * a[n], run)
        through = none
        of_c = none
        for n in range(NZ - 1, -1, -1):
            if n < NZ - 1:
                through = wh[n + 1] * k[n + 1] + a[n + 1] * through
            wd[n] = jnp.where(n < mz, none, through)
            of_c = jnp.where(n == mz, a[n] * through, of_c)
        for n in range(NZ):
            wd[n] = wd[n] + of_c * wc[n]
        return wc, wh, wd

    def group_weights(a, k):
        one = jnp.ones((8, 128), F32)
        gl, gh = [one], [one]
        for n in range(NX - 1):
            gl.insert(0, gl[0] * a[NX - 1 - n])
            gh.append(gh[n] * a[n])
        gm = [gh[NX - 1] * k[NX - 1]]
        for n in range(NX - 2, 0, -1):
            gm.insert(0, gh[n] * k[n] + a[n] * gm[0])
        return gl, gh, gm

    saved = {}

    def carries(turn, x, row):
        going_right, going_left, s, e = local_sums(x)
        xv = xb.at[turn, mx]
        write_pair(xv, 0, going_right)
        write_pair(xv, 16, going_left)
        square = sum(e[f] * e[f] for f in range(3, 19))
        xv[32:33] = row_sum(square[0] + square[1])
        xv[33:34] = row
        x_copies(xb.at[turn, mx, pl.ds(0, 34)], x_send.at[turn], x_recv.at[turn])
        if turn == 0:
            halo_copy(0, x, 13, after)
            halo_copy(1, x, 0, before)
            group_coefficients()
        else:
            halo_copy(2, x, 0, before)
        g = backward(e)
        a, k = [[cx[n, 8 * m : 8 * m + 8] for n in range(NX)] for m in range(2)]
        if turn == 0:
            wait_for(stage_d.at[pl.ds(0, GROUP - 1), pl.ds(0, 4)], d_send)
            wait_for(stage_o.at[pl.ds(0, GROUP - 1), pl.ds(0, 11)], o_send)
            wait_for(cx.at[pl.ds(0, NX - 1)], xc_send)
        else:
            wait_for(cz.at[pl.ds(0, NZ - 1)], zc_send)
            wait_for(zb.at[0, pl.ds(0, NZ - 1), pl.ds(0, 34)], z_send.at[0])
        wait_for(xb.at[turn, pl.ds(0, NX - 1), pl.ds(0, 34)], x_recv.at[turn])
        lefts = [pair(xb.at[turn, n], 0) for n in range(NX)]
        rights = [pair(xb.at[turn, n], 16) for n in range(NX)]
        cs, ds, _ = chain(zero, zero, lefts, rights, a, k)
        gl, gh, gm = group_weights(a, k)
        zv = zb.at[turn, mz]
        write_pair(zv, 0, sum(v * z for v, z in zip(gl, lefts)))
        write_pair(zv, 16, sum(v * z for v, z in zip(gh, rights)) + sum(v * z for v, z in zip(gm, lefts[:-1])))
        zv[32:33] = crossed(cs[:NX], rights, k) + sum(xb[turn, n, 32:33] for n in range(NX))
        zv[33:34] = sum(xb[turn, n, 33:34] for n in range(NX))
        z_copies(zb.at[turn, mz, pl.ds(0, 34)], z_send.at[turn], z_recv.at[turn])
        c_own = own_of(carry_x.at[0], cs[:NX], mx)
        d_own = own_of(carry_x.at[1], ds, mx)
        if turn == 0:
            one = jnp.ones((2, 8, 128), F32)
            quiet = [zero] * NX
            from_left, back_left, _ = chain(one, zero, quiet, quiet, a, k)
            _, back_right, _ = chain(zero, one, quiet, quiet, a, k)
            pass_c = own_of(carry_x.at[2], from_left[:NX], mx)[0]
            turn_c = own_of(carry_x.at[3], back_left, mx)[0]
            pass_d = own_of(carry_x.at[4], back_right, mx)[0]
            halo_wait(0)
            halo_wait(1)
            halo_coefficients()
            left_whiten(halo_frames(0, me == 0), s, e, g)
            wait_for(cz.at[pl.ds(0, NZ - 1)], zc_recv)
            za, zk = [[cz[n, 8 * m : 8 * m + 8] for n in range(NZ)] for m in range(2)]
            wc, wh, wd = ahead_weights(za, zk)
            saved["z"] = za, zk
            saved["c"] = [pass_c * w for w in wc]
            saved["h"] = [pass_d * w for w in wh]
            saved["l"] = [pass_d * v + turn_c * w for v, w in zip(wd, wc)]
        if turn == 1:
            halo_wait(2)
        za, zk = saved["z"]
        right_whiten(halo_frames(1 + turn, me == GROUP - 1), s, e, g)
        w = whole(e, g, 3 * turn)
        wait_for(xb.at[turn, pl.ds(0, NX - 1), pl.ds(0, 34)], x_send.at[turn])
        wait_for(zb.at[turn, pl.ds(0, NZ - 1), pl.ds(0, 34)], z_recv.at[turn])
        zleft = [pair(zb.at[turn, n], 0) for n in range(NZ)]
        zright = [pair(zb.at[turn, n], 16) for n in range(NZ)]
        c = c_own + sum(v * z for v, z in zip(saved["c"], zleft))
        d = d_own + sum(v * z for v, z in zip(saved["h"], zright)) + sum(v * z for v, z in zip(saved["l"], zleft))

        def sums():
            zcs = [zero]
            for n in range(NZ - 1):
                zcs.append(za[n] * zcs[n] + zleft[n])
            squares = crossed(zcs, zright, zk) + sum(zb[turn, n, 32:33] for n in range(NZ))
            rows = sum(zb[turn, n, 33:34] for n in range(NZ))
            return jnp.sum(squares, axis=1, keepdims=True), jnp.sum(rows, axis=1, keepdims=True)

        return w, c, d, sums

    def corrected(w, start, c, d):
        out = [v + left[f] * c + right[f] * d for f, v in zip(range(start, 22), w)]
        return jnp.stack([v[0] for v in out]), jnp.stack([v[1] for v in out])

    def padded(re, im):
        fill = jnp.zeros((1, 8, 128), F32)
        return jnp.concatenate([re, fill]), jnp.concatenate([im, fill])

    def squares(value):
        return row_sum(jnp.sum(value[0] * value[0] + value[1] * value[1], axis=0))

    u = to_wave(spec[0], spec[1])
    r0 = [part_only(gather_taps(v, 19)) for v in u]
    x0 = to_spec(*[spread_taps(v, 16) for v in r0])
    mine_r0 = [v[3:] for v in r0]
    w, c, d, sums = carries(0, x0, squares(mine_r0))
    w = corrected(w, 0, c, d)

    u = to_wave(*w)
    q1 = [part_only(gather_taps(v, 19) + RIDGE * r) for v, r in zip(u, r0)]
    x = to_spec(*[spread_taps(v, 16) for v in q1])
    energy, rr = sums()
    alpha = rr / (energy + RIDGE * rr)
    x1 = [b - alpha * v for b, v in zip(x0, x)]
    mine_q1 = [v[3:] for v in q1]
    r1 = [r - alpha * q for r, q in zip(mine_r0, mine_q1)]
    w, c, d, sums = carries(1, x1, squares(r1))
    w = corrected(w, 3, c, d)

    u = to_wave(*padded(*w))
    n1 = [gather_taps(v, 16) + RIDGE * r for v, r in zip(u, r1)]
    energy, new = sums()
    beta = new / rr
    alpha_next = new / (energy + RIDGE * new - beta * new / alpha)
    share_ref[...] = jnp.broadcast_to(alpha_next, (8, 1024))
    for n in range(2):
        image = n1[n] + beta * mine_q1[n]
        base_ref[n] = ((alpha + alpha_next * beta) * mine_r0[n]).reshape(16, 1024)
        mid_ref[n] = r1[n].reshape(16, 1024)
        drop_ref[n] = (alpha_next * image).reshape(16, 1024)
    wait_for(zb.at[1, pl.ds(0, NZ - 1), pl.ds(0, 34)], z_send.at[1])


def body(observed, window, decays):
    mats, tabs = tables()
    any_space = pl.BlockSpec(memory_space=pltpu.HBM)
    vmem = pl.BlockSpec(memory_space=pltpu.VMEM)
    dma = pltpu.SemaphoreType.DMA
    out = jax.ShapeDtypeStruct((2, 16, 1024), F32)
    base, mid, drop, share = pl.pallas_call(
        kernel,
        out_shape=(out, out, out, jax.ShapeDtypeStruct((8, 1024), F32)),
        in_specs=[any_space] * 5,
        out_specs=(vmem,) * 4,
        scratch_shapes=[
            pltpu.VMEM((2, 32, 512), F32),
            pltpu.VMEM((4, 1024), F32),
            pltpu.VMEM((32, 512), F32),
            pltpu.VMEM((2, 256, 256), F32),
            pltpu.VMEM((4, 8, 128), F32),
            pltpu.VMEM((2, 768, 256), BF16),
            pltpu.VMEM((GROUP, 16, 128), F32),
            pltpu.VMEM((GROUP, 8, 128), F32),
            pltpu.VMEM((12, GROUP, 128), F32),
            pltpu.VMEM((4, GROUP, 128), F32),
            pltpu.VMEM((2, 22, 8, 128), F32),
            pltpu.VMEM((24, 8, 128), F32),
            pltpu.VMEM((5, NX, 2, 8, 128), F32),
            pltpu.VMEM((2, NX, 40, 128), F32),
            pltpu.VMEM((2, NZ, 40, 128), F32),
            pltpu.VMEM((NX, 16, 128), F32),
            pltpu.VMEM((NZ, 16, 128), F32),
            pltpu.VMEM((3, 3, 3, 8, 128), F32),
            pltpu.VMEM((3, 3, 3, 8, 128), F32),
            dma((5,)),
            dma((2,)),
            dma, dma, dma, dma, dma, dma, dma, dma,
            dma((2,)), dma((2,)), dma((2,)), dma((2,)),
            dma((3,)), dma((3,)),
        ],
        name="invert",
        compiler_params=pltpu.CompilerParams(
            collective_id=0, has_side_effects=True, vmem_limit_bytes=48 * 1024 * 1024
        ),
    )(*[pltpu.with_memory_space_constraint(v, pltpu.HBM) for v in (observed, window, decays, jnp.asarray(mats), jnp.asarray(tabs))])
    return base + share[:1] * mid, mid - drop


def solution(mesh):
    return jax.shard_map(
        body,
        mesh=mesh,
        in_specs=(P(None, "chan", "beam"), P(), P("chan", "beam")),
        out_specs=(P(None, ("beam", "chan"), None), P(None, ("beam", "chan"), None)),
        check_vma=False,
    )
```

```python
import functools
import math

import jax
import jax.numpy as jnp
import numpy as np
from jax import lax
from jax.experimental import pallas as pl
from jax.experimental.pallas import tpu as pltpu
from jax.sharding import PartitionSpec as P

MESH = pl.DeviceIdType.MESH
F32 = jnp.float32
BF16 = jnp.bfloat16
GROUP = 32
NX = 4
NZ = 8
RIDGE = 0.5
FLIP = (0, 4, 2, 6, 1, 5, 3, 7)


def tables():
    lane = np.arange(128)
    k2 = 4 * (lane % 32) + lane // 32
    n2 = np.arange(128)
    angle = 2.0 * np.pi * ((k2[:, None] * n2[None, :]) % 128) / 128.0
    cos, sin = np.cos(angle) / 32.0, np.sin(angle) / 32.0
    inverse = np.block([[cos, sin], [-sin, cos]])

    mats = np.stack([inverse, inverse.T]).astype(np.float32)
    turn = 2.0 * np.pi * np.array(FLIP)[:, None] * n2[None, :] / 1024.0
    eighth = 2.0 * np.pi * np.maximum(np.arange(8) - 4, 0) / 8.0
    eighth = np.broadcast_to(eighth[:, None], (8, 128))
    tabs = np.stack([np.cos(turn), np.sin(turn), np.cos(eighth), np.sin(eighth)])
    return mats, tabs.astype(np.float32)


def kernel(
    obs_hbm, win_hbm, dec_hbm, mats_hbm, tabs_hbm, base_ref, mid_ref, drop_ref, share_ref,
    obs_v, win_v, dec_v, full_v, tabs_v, mats_v, stage_o, stage_d, got_o, got_d,
    spec, dec, carry_x, xb, zb, cx, cz, out_halo, in_halo,
    in_sem, own_sem, o_send, o_recv, d_send, d_recv, xc_send, xc_recv,
    zc_send, zc_recv, x_send, x_recv, z_send, z_recv,
    h_send, h_recv,
):
    me = lax.axis_index("chan")
    mz = me // NX
    mx = lax.rem(me, NX)
    barrier = pltpu.get_barrier_semaphore()
    others = sorted(
        ((dz, dx) for dz in range(NZ) for dx in range(NX) if dz or dx),
        key=lambda o: -min(o[0], NZ - o[0]) - min(o[1], NX - o[1]),
    )
    inputs = []
    for t, (src, dst) in enumerate(
        ((obs_hbm, obs_v), (dec_hbm, dec_v), (win_hbm, win_v), (mats_hbm, full_v), (tabs_hbm, tabs_v))
    ):
        copy = pltpu.make_async_copy(src, dst, in_sem.at[t])
        copy.start()
        inputs.append(copy)
    others = [lax.rem(mz + dz, NZ) * NX + lax.rem(mx + dx, NX) for dz, dx in others]
    for to in others:
        pl.semaphore_signal(barrier, inc=1, device_id={"chan": to}, device_id_type=MESH)
    inputs[0].wait()
    inputs[1].wait()

    frames = 512
    lane = lax.broadcasted_iota(jnp.int32, (32, frames), 1)
    row = lax.rem(lax.broadcasted_iota(jnp.int32, (32, frames), 0), 8)

    def shift(value, steps):
        return pltpu.roll(value, steps % frames, axis=value.ndim - 1)

    a = dec_v[...]
    gain = 1.0 - a
    data = [obs_v[0], obs_v[1]]
    prod = jnp.where(lane == 0, 0.0, a)
    run = [gain * d for d in data]
    step = 1
    while step < frames:
        run = [r + prod * shift(r, step) for r in run]
        prod = prod * shift(prod, step)
        step *= 2
    first = [d + 2.0 * r for d, r in zip(data, run)]
    prod = jnp.where(lane == frames - 1, 0.0, shift(a, -1))
    run = first
    step = 1
    while step < frames:
        run = [r + prod * shift(r, -step) for r in run]
        prod = prod * shift(prod, -step)
        step *= 2
    white = [f + 2.0 * gain * r for f, r in zip(first, run)]

    up = (row == 1) | (row == 3)
    down = (row == 4) | (row == 6)

    def flipped(value):
        return jnp.where(
            up,
            pltpu.roll(value, 29, axis=0),
            jnp.where(down, pltpu.roll(value, 3, axis=0), value),
        )

    def moved(value, offset):
        moved_value = shift(value, -offset)
        inside = (lane + offset >= 0) & (lane + offset < frames)
        return jnp.where(inside, moved_value, 0.0)

    white = [flipped(w) for w in white]
    af = flipped(a)
    packed = jnp.concatenate(
        [moved(white[0], -3), moved(white[1], -3), moved(white[0], 8), moved(white[1], 8)], axis=0
    )
    stage_o[...] = packed.T.reshape(GROUP, 16, 128)
    packed = jnp.concatenate([moved(af, 4 * t) for t in range(4)], axis=0)
    stage_d[...] = packed.T.reshape(GROUP, 16, 128)[:, :8]

    own = [
        pltpu.make_async_copy(stage_d.at[me, pl.ds(0, 4)], got_d.at[:, me, :], own_sem.at[0]),
        pltpu.make_async_copy(stage_o.at[me, pl.ds(0, 11)], got_o.at[pl.ds(0, 11), me, :], own_sem.at[1]),
    ]
    for copy in own:
        copy.start()

    pl.semaphore_wait(barrier, GROUP - 1)

    for stage, got, rows, send, recv in (
        (stage_d, got_d, 4, d_send, d_recv), (stage_o, got_o, 11, o_send, o_recv)
    ):
        for to in (others[::-1] if rows < 11 else others):
            copy = pltpu.make_async_remote_copy(
                src_ref=stage.at[to, pl.ds(0, rows)], dst_ref=got.at[pl.ds(0, rows), me, :],
                send_sem=send, recv_sem=recv,
                device_id={"chan": to}, device_id_type=MESH,
            )
            copy.start()
    for copy in inputs[2:]:
        copy.wait()

    for which in range(2):
        full = full_v[which]
        high = full.astype(BF16)
        mats_v[which, 0:256] = high
        mats_v[which, 256:512] = high
        mats_v[which, 512:768] = (full - high.astype(F32)).astype(BF16)

    win = [
        jnp.concatenate([win_v[p : p + 1, n * 128 : (n + 1) * 128] for n in range(8)], axis=0)
        for p in range(4)
    ]

    def butterfly(value, distance):
        high = (lax.broadcasted_iota(jnp.int32, (8, 128), 0) & distance) != 0
        if distance == 4:
            other = pltpu.roll(value, 4, axis=1)
        else:
            other = jnp.where(
                high, pltpu.roll(value, distance, axis=1), pltpu.roll(value, 8 - distance, axis=1)
            )
        return other + value * jnp.where(high, -1.0, 1.0)

    def quarter(re, im, sign):
        index = lax.broadcasted_iota(jnp.int32, re.shape, 1)
        turned = (index & 3) == 3
        return jnp.where(turned, -sign * im, re), jnp.where(turned, sign * re, im)

    def times(re, im, c, s):
        return re * c - im * s, re * s + im * c

    def product(re, im, which):
        count = re.shape[0]
        x = jnp.concatenate([re.reshape(count * 8, 128), im.reshape(count * 8, 128)], axis=1)
        high = x.astype(BF16)
        low = (x - high.astype(F32)).astype(BF16)
        y = jnp.dot(
            jnp.concatenate([high, low, high], axis=1), mats_v[which], preferred_element_type=F32
        )
        return y[:, :128].reshape(count, 8, 128), y[:, 128:].reshape(count, 8, 128)

    def to_wave(re, im):
        re, im = product(re, im, 0)
        re, im = times(re, im, tabs_v[0], tabs_v[1])
        re, im = butterfly(re, 1), butterfly(im, 1)
        re, im = quarter(re, im, 1.0)
        re, im = butterfly(re, 2), butterfly(im, 2)
        re, im = times(re, im, tabs_v[2], tabs_v[3])
        return butterfly(re, 4), butterfly(im, 4)

    def to_spec(re, im):
        re, im = butterfly(re, 4), butterfly(im, 4)
        re, im = times(re, im, tabs_v[2], -tabs_v[3])
        re, im = butterfly(re, 2), butterfly(im, 2)
        re, im = quarter(re, im, -1.0)
        re, im = butterfly(re, 1), butterfly(im, 1)
        re, im = times(re, im, tabs_v[0], -tabs_v[1])
        return product(re, im, 1)

    def gather_taps(u, count):
        out = win[0] * u[0:count]
        for p in range(1, 4):
            out = out + win[p] * u[p : p + count]
        return out

    def spread_taps(v, count):
        out = win[0] * v[3 : 3 + count]
        for p in range(1, 4):
            out = out + win[p] * v[3 - p : 3 - p + count]
        return out

    def part_only(value):
        index = lax.broadcasted_iota(jnp.int32, value.shape, 0)
        return jnp.where((index < 3) & (me == 0), 0.0, value)

    def wait_for(ref, sem):
        pltpu.make_async_copy(ref, ref, sem).wait()

    own[0].wait()
    wait_for(got_d.at[:, pl.ds(0, GROUP - 1)], d_recv)

    lane8 = lax.broadcasted_iota(jnp.int32, (8, 128), 1)
    low64 = lane8 < 64
    low32 = (lane8 & 32) == 0

    def exchange(v):
        y = [None] * 4
        for i in range(2):
            y[i] = jnp.where(low64, v[i], pltpu.roll(v[i + 2], 64, axis=1))
            y[i + 2] = jnp.where(low64, pltpu.roll(v[i], 64, axis=1), v[i + 2])
        z = [None] * 4
        for i in (0, 2):
            z[i] = jnp.where(low32, y[i], pltpu.roll(y[i + 1], 32, axis=1))
            z[i + 1] = jnp.where(low32, pltpu.roll(y[i], 96, axis=1), y[i + 1])
        return z

    turned = got_d[...].reshape(128, 128).T
    for part in range(4):
        base = part * 32
        out = exchange([turned[base + 8 * i : base + 8 * i + 8] for i in range(4)])
        for r in range(4):
            dec[3 + 4 * part + r] = out[r]

    def send_to(src, dst, send, recv, to):
        pltpu.make_async_remote_copy(
            src_ref=src, dst_ref=dst, send_sem=send, recv_sem=recv, device_id={"chan": to}, device_id_type=MESH,
        ).start()

    after = lax.rem(me + 1, GROUP)
    before = lax.rem(me + GROUP - 1, GROUP)

    def inverse(a):
        return jnp.where(a > 0.0, 1.0 / jnp.where(a > 0.0, a, 1.0), 0.0)

    def backward(e):
        g = {18: e[18]}
        for f in range(17, 2, -1):
            g[f] = e[f] + dec[f + 1] * g[f + 1]
        return g

    def backward_left(e, g):
        for f in (2, 1, 0):
            g[f] = e[f] + dec[f + 1] * g[f + 1]

    def backward_right(e, g):
        g[19] = jnp.zeros_like(g[18])
        for f in (20, 21):
            g[f] = (g[f - 1] - e[f - 1]) * inv[f]

    twice = {f: 2.0 * (1.0 - dec[f]) for f in range(3, 19)}
    prods = {2: jnp.ones((8, 128), F32)}
    for f in range(3, 19):
        prods[f] = dec[f] * prods[f - 1]
    from_c = {f: 2.0 * prods[f] for f in range(3, 19)}
    back_c = backward(from_c)
    back_d, left, right, inv = {18: jnp.ones((8, 128), F32)}, {}, {}, {}

    def halo_coefficients():
        for f in range(3):
            dec[f] = jnp.where(me == 0, 0.0, in_halo[0, 2, f])
            dec[19 + f] = jnp.where(me == GROUP - 1, 0.0, in_halo[1, 2, f])
        halo = (0, 1, 2, 19, 20, 21)
        for f in (1, 2, 19, 20, 21):
            inv[f] = inverse(dec[f])
        for f in halo:
            twice[f] = 2.0 * (1.0 - dec[f])
        prods[1] = inv[2]
        prods[0] = inv[1] * inv[2]
        for f in (19, 20, 21):
            prods[f] = dec[f] * prods[f - 1]
        for f in halo:
            from_c[f] = 2.0 * prods[f]
        backward_left(from_c, back_c)
        backward_right(from_c, back_c)
        for f in (2, 1, 0):
            back_d[f] = dec[f + 1] * back_d[f + 1]
        back_d[19] = inv[19]
        for f in (20, 21):
            back_d[f] = back_d[f - 1] * inv[f]
        for f in halo:
            left[f] = from_c[f] + twice[f] * back_c[f]
            right[f] = twice[f] * back_d[f]

    cx[mx, 0:8] = prods[18]
    cx[mx, 8:16] = dec[3] * back_c[3]

    def x_copies(part, send, recv):
        out = []
        for t in (2, 1, 3):
            to = mz * NX + lax.rem(mx + t, NX)
            out.append(pltpu.make_async_remote_copy(
                src_ref=part, dst_ref=part, send_sem=send, recv_sem=recv,
                device_id={"chan": to}, device_id_type=MESH,
            ))
        for copy in out:
            copy.start()

    def z_copies(part, send, recv):
        out = []
        for t in (4, 3, 5, 2, 6, 1, 7):
            to = lax.rem(mz + t, NZ) * NX + mx
            out.append(pltpu.make_async_remote_copy(
                src_ref=part, dst_ref=part, send_sem=send, recv_sem=recv,
                device_id={"chan": to}, device_id_type=MESH,
            ))
        for copy in out:
            copy.start()

    x_copies(cx.at[mx], xc_send, xc_recv)

    own[1].wait()
    wait_for(got_o.at[pl.ds(0, 11), pl.ds(0, GROUP - 1)], o_recv)

    for f in range(17, 2, -1):
        back_d[f] = dec[f + 1] * back_d[f + 1]
    for f in range(3, 19):
        left[f] = from_c[f] + twice[f] * back_c[f]
        right[f] = twice[f] * back_d[f]

    for q in range(3):
        turned = got_o[4 * q : 4 * q + 4].reshape(128, 128).T
        for half in range(2):
            for c in range(2):
                base = half * 64 + c * 32
                out = exchange([turned[base + 8 * i : base + 8 * i + 8] for i in range(4)])
                for r in range(min(4, 11 - 4 * q)):
                    spec[c, 11 * half + 4 * q + r] = out[r]

    def halo_copy(slot, x, first, to):
        planes = 3 if slot < 2 else 2
        for f in range(3):
            out_halo[slot, 0, f] = x[0][first + f]
            out_halo[slot, 1, f] = x[1][first + f]
            if planes == 3:
                out_halo[slot, 2, f] = dec[3 + first + f]
        part = (slot, pl.ds(0, planes))
        send_to(out_halo.at[part], in_halo.at[part], h_send.at[slot], h_recv.at[slot], to)

    def halo_wait(slot):
        part = (slot, pl.ds(0, 3 if slot < 2 else 2))
        wait_for(in_halo.at[part], h_recv.at[slot])
        wait_for(out_halo.at[part], h_send.at[slot])

    def halo_frames(slot, outside):
        return [
            jnp.where(outside, 0.0, jnp.stack([in_halo[slot, 0, f], in_halo[slot, 1, f]])) for f in range(3)
        ]

    def local_sums(x):
        frames_x = {f: jnp.stack([x[0][f - 3], x[1][f - 3]]) for f in range(3, 19)}
        going_right = 0.5 * sum(right[f] * frames_x[f] for f in range(3, 19))
        going_left = 0.5 * sum(left[f] * frames_x[f] for f in range(3, 19))
        s = {2: jnp.zeros((2, 8, 128), F32)}
        e = {}
        for f in range(3, 19):
            s[f] = dec[f] * s[f - 1] + (1.0 - dec[f]) * frames_x[f]
            e[f] = frames_x[f] + 2.0 * s[f]
        return going_right, going_left, s, e

    def left_whiten(x, s, e, g):
        for f in (2, 1, 0):
            if f < 2:
                s[f] = (s[f + 1] - (1.0 - dec[f + 1]) * x[f + 1]) * inv[f + 1]
            e[f] = x[f] + 2.0 * s[f]
        backward_left(e, g)

    def right_whiten(x, s, e, g):
        for f in (19, 20, 21):
            s[f] = dec[f] * s[f - 1] + (1.0 - dec[f]) * x[f - 19]
            e[f] = x[f - 19] + 2.0 * s[f]
        backward_right(e, g)

    def whole(e, g, start):
        return [e[f] + twice[f] * g[f] for f in range(start, 22)]

    def chain(carry, back, left, right, a, k):
        count = len(left)
        cs = [carry]
        for n in range(count):
            cs.append(a[n] * cs[n] + left[n])
        ds = [None] * count
        d = back
        for n in range(count - 1, -1, -1):
            ds[n] = d
            d = a[n] * d + (right[n] + k[n] * cs[n])
        return cs, ds, d

    def pair(ref, base):
        return jnp.stack([ref[base : base + 8], ref[base + 8 : base + 16]])

    zero = jnp.zeros((2, 8, 128), F32)

    def row_sum(value):
        return jnp.sum(value, axis=0, keepdims=True)

    def write_pair(ref, base, value):
        ref[base : base + 8] = value[0]
        ref[base + 8 : base + 16] = value[1]

    def crossed(cs, right, k):
        total = jnp.zeros((8, 128), F32)
        for c, h, q in zip(cs, right, k):
            full = (4.0 * h + (2.0 * q) * c) * c
            total = total + full[0] + full[1]
        return row_sum(total)

    def group_coefficients():
        wait_for(cx.at[pl.ds(0, NX - 1)], xc_recv)
        a, k = [[cx[n, 8 * m : 8 * m + 8] for n in range(NX)] for m in range(2)]
        ga, gk = a[0], k[0]
        for n in range(1, NX):
            gk = gk + k[n] * (ga * ga)
            ga = a[n] * ga
        cz[mz, 0:8] = ga
        cz[mz, 8:16] = gk
        z_copies(cz.at[mz], zc_send, zc_recv)

    def own_of(ref, values, index):
        for n, value in enumerate(values):
            ref[n] = value
        return ref[index]

    def ahead_weights(a, k):
        one = jnp.ones((8, 128), F32)
        none = jnp.zeros((8, 128), F32)
        wc, wh, wd = [none] * NZ, [none] * NZ, [none] * NZ
        run = one
        for n in range(NZ - 1, -1, -1):
            wc[n] = jnp.where(n < mz, run, none)
            run = jnp.where(n < mz, run * a[n], run)
        run = one
        for n in range(NZ):
            wh[n] = jnp.where(n > mz, run, none)
            run = jnp.where(n > mz, run * a[n], run)
        through = none
        of_c = none
        for n in range(NZ - 1, -1, -1):
            if n < NZ - 1:
                through = wh[n + 1] * k[n + 1] + a[n + 1] * through
            wd[n] = jnp.where(n < mz, none, through)
            of_c = jnp.where(n == mz, a[n] * through, of_c)
        for n in range(NZ):
            wd[n] = wd[n] + of_c * wc[n]
        return wc, wh, wd

    def group_weights(a, k):
        one = jnp.ones((8, 128), F32)
        gl, gh = [one], [one]
        for n in range(NX - 1):
            gl.insert(0, gl[0] * a[NX - 1 - n])
            gh.append(gh[n] * a[n])
        gm = [gh[NX - 1] * k[NX - 1]]
        for n in range(NX - 2, 0, -1):
            gm.insert(0, gh[n] * k[n] + a[n] * gm[0])
        return gl, gh, gm

    saved = {}

    def carries(turn, x, row):
        going_right, going_left, s, e = local_sums(x)
        xv = xb.at[turn, mx]
        write_pair(xv, 0, going_right)
        write_pair(xv, 16, going_left)
        square = sum(e[f] * e[f] for f in range(3, 19))
        xv[32:33] = row_sum(square[0] + square[1])
        xv[33:34] = row
        x_copies(xb.at[turn, mx, pl.ds(0, 34)], x_send.at[turn], x_recv.at[turn])
        if turn == 0:
            halo_copy(0, x, 13, after)
            halo_copy(1, x, 0, before)
            group_coefficients()
        else:
            halo_copy(2, x, 0, before)
        g = backward(e)
        a, k = [[cx[n, 8 * m : 8 * m + 8] for n in range(NX)] for m in range(2)]
        if turn == 0:
            wait_for(stage_d.at[pl.ds(0, GROUP - 1), pl.ds(0, 4)], d_send)
            wait_for(stage_o.at[pl.ds(0, GROUP - 1), pl.ds(0, 11)], o_send)
            wait_for(cx.at[pl.ds(0, NX - 1)], xc_send)
        else:
            wait_for(cz.at[pl.ds(0, NZ - 1)], zc_send)
            wait_for(zb.at[0, pl.ds(0, NZ - 1), pl.ds(0, 34)], z_send.at[0])
        wait_for(xb.at[turn, pl.ds(0, NX - 1), pl.ds(0, 34)], x_recv.at[turn])
        lefts = [pair(xb.at[turn, n], 0) for n in range(NX)]
        rights = [pair(xb.at[turn, n], 16) for n in range(NX)]
        cs, ds, _ = chain(zero, zero, lefts, rights, a, k)
        gl, gh, gm = group_weights(a, k)
        zv = zb.at[turn, mz]
        write_pair(zv, 0, sum(v * z for v, z in zip(gl, lefts)))
        write_pair(zv, 16, sum(v * z for v, z in zip(gh, rights)) + sum(v * z for v, z in zip(gm, lefts[:-1])))
        zv[32:33] = crossed(cs[:NX], rights, k) + sum(xb[turn, n, 32:33] for n in range(NX))
        zv[33:34] = sum(xb[turn, n, 33:34] for n in range(NX))
        z_copies(zb.at[turn, mz, pl.ds(0, 34)], z_send.at[turn], z_recv.at[turn])
        c_own = own_of(carry_x.at[0], cs[:NX], mx)
        d_own = own_of(carry_x.at[1], ds, mx)
        if turn == 0:
            one = jnp.ones((2, 8, 128), F32)
            quiet = [zero] * NX
            from_left, back_left, _ = chain(one, zero, quiet, quiet, a, k)
            _, back_right, _ = chain(zero, one, quiet, quiet, a, k)
            pass_c = own_of(carry_x.at[2], from_left[:NX], mx)[0]
            turn_c = own_of(carry_x.at[3], back_left, mx)[0]
            pass_d = own_of(carry_x.at[4], back_right, mx)[0]
            halo_wait(0)
            halo_wait(1)
            halo_coefficients()
            left_whiten(halo_frames(0, me == 0), s, e, g)
            wait_for(cz.at[pl.ds(0, NZ - 1)], zc_recv)
            za, zk = [[cz[n, 8 * m : 8 * m + 8] for n in range(NZ)] for m in range(2)]
            wc, wh, wd = ahead_weights(za, zk)
            saved["z"] = za, zk
            saved["c"] = [pass_c * w for w in wc]
            saved["h"] = [pass_d * w for w in wh]
            saved["l"] = [pass_d * v + turn_c * w for v, w in zip(wd, wc)]
        if turn == 1:
            halo_wait(2)
        za, zk = saved["z"]
        right_whiten(halo_frames(1 + turn, me == GROUP - 1), s, e, g)
        w = whole(e, g, 3 * turn)
        wait_for(xb.at[turn, pl.ds(0, NX - 1), pl.ds(0, 34)], x_send.at[turn])
        wait_for(zb.at[turn, pl.ds(0, NZ - 1), pl.ds(0, 34)], z_recv.at[turn])
        zleft = [pair(zb.at[turn, n], 0) for n in range(NZ)]
        zright = [pair(zb.at[turn, n], 16) for n in range(NZ)]
        c = c_own + sum(v * z for v, z in zip(saved["c"], zleft))
        d = d_own + sum(v * z for v, z in zip(saved["h"], zright)) + sum(v * z for v, z in zip(saved["l"], zleft))

        def sums():
            zcs = [zero]
            for n in range(NZ - 1):
                zcs.append(za[n] * zcs[n] + zleft[n])
            squares = crossed(zcs, zright, zk) + sum(zb[turn, n, 32:33] for n in range(NZ))
            rows = sum(zb[turn, n, 33:34] for n in range(NZ))
            return jnp.sum(squares, axis=1, keepdims=True), jnp.sum(rows, axis=1, keepdims=True)

        return w, c, d, sums

    def corrected(w, start, c, d):
        out = [v + left[f] * c + right[f] * d for f, v in zip(range(start, 22), w)]
        return jnp.stack([v[0] for v in out]), jnp.stack([v[1] for v in out])

    def padded(re, im):
        fill = jnp.zeros((1, 8, 128), F32)
        return jnp.concatenate([re, fill]), jnp.concatenate([im, fill])

    def squares(value):
        return row_sum(jnp.sum(value[0] * value[0] + value[1] * value[1], axis=0))

    u = to_wave(spec[0], spec[1])
    r0 = [part_only(gather_taps(v, 19)) for v in u]
    x0 = to_spec(*[spread_taps(v, 16) for v in r0])
    mine_r0 = [v[3:] for v in r0]
    w, c, d, sums = carries(0, x0, squares(mine_r0))
    w = corrected(w, 0, c, d)

    u = to_wave(*w)
    q1 = [part_only(gather_taps(v, 19) + RIDGE * r) for v, r in zip(u, r0)]
    x = to_spec(*[spread_taps(v, 16) for v in q1])
    energy, rr = sums()
    alpha = rr / (energy + RIDGE * rr)
    x1 = [b - alpha * v for b, v in zip(x0, x)]
    mine_q1 = [v[3:] for v in q1]
    r1 = [r - alpha * q for r, q in zip(mine_r0, mine_q1)]
    w, c, d, sums = carries(1, x1, squares(r1))
    w = corrected(w, 3, c, d)

    u = to_wave(*padded(*w))
    n1 = [gather_taps(v, 16) + RIDGE * r for v, r in zip(u, r1)]
    energy, new = sums()
    beta = new / rr
    alpha_next = new / (energy + RIDGE * new - beta * new / alpha)
    share_ref[...] = jnp.broadcast_to(alpha_next, (8, 1024))
    for n in range(2):
        image = n1[n] + beta * mine_q1[n]
        base_ref[n] = ((alpha + alpha_next * beta) * mine_r0[n]).reshape(16, 1024)
        mid_ref[n] = r1[n].reshape(16, 1024)
        drop_ref[n] = (alpha_next * image).reshape(16, 1024)
    wait_for(zb.at[1, pl.ds(0, NZ - 1), pl.ds(0, 34)], z_send.at[1])


def body(observed, window, decays):
    mats, tabs = tables()
    any_space = pl.BlockSpec(memory_space=pltpu.HBM)
    vmem = pl.BlockSpec(memory_space=pltpu.VMEM)
    dma = pltpu.SemaphoreType.DMA
    out = jax.ShapeDtypeStruct((2, 16, 1024), F32)
    base, mid, drop, share = pl.pallas_call(
        kernel,
        out_shape=(out, out, out, jax.ShapeDtypeStruct((8, 1024), F32)),
        in_specs=[any_space] * 5,
        out_specs=(vmem,) * 4,
        scratch_shapes=[
            pltpu.VMEM((2, 32, 512), F32),
            pltpu.VMEM((4, 1024), F32),
            pltpu.VMEM((32, 512), F32),
            pltpu.VMEM((2, 256, 256), F32),
            pltpu.VMEM((4, 8, 128), F32),
            pltpu.VMEM((2, 768, 256), BF16),
            pltpu.VMEM((GROUP, 16, 128), F32),
            pltpu.VMEM((GROUP, 8, 128), F32),
            pltpu.VMEM((12, GROUP, 128), F32),
            pltpu.VMEM((4, GROUP, 128), F32),
            pltpu.VMEM((2, 22, 8, 128), F32),
            pltpu.VMEM((24, 8, 128), F32),
            pltpu.VMEM((5, NX, 2, 8, 128), F32),
            pltpu.VMEM((2, NX, 40, 128), F32),
            pltpu.VMEM((2, NZ, 40, 128), F32),
            pltpu.VMEM((NX, 16, 128), F32),
            pltpu.VMEM((NZ, 16, 128), F32),
            pltpu.VMEM((3, 3, 3, 8, 128), F32),
            pltpu.VMEM((3, 3, 3, 8, 128), F32),
            dma((5,)),
            dma((2,)),
            dma, dma, dma, dma, dma, dma, dma, dma,
            dma((2,)), dma((2,)), dma((2,)), dma((2,)),
            dma((3,)), dma((3,)),
        ],
        name="invert",
        compiler_params=pltpu.CompilerParams(
            collective_id=0, has_side_effects=True, vmem_limit_bytes=48 * 1024 * 1024
        ),
    )(*[pltpu.with_memory_space_constraint(v, pltpu.HBM) for v in (observed, window, decays, jnp.asarray(mats), jnp.asarray(tabs))])
    return base + share[:1] * mid, mid - drop


def solution(mesh):
    return jax.shard_map(
        body,
        mesh=mesh,
        in_specs=(P(None, "chan", "beam"), P(), P("chan", "beam")),
        out_specs=(P(None, ("beam", "chan"), None), P(None, ("beam", "chan"), None)),
        check_vma=False,
    )
```
